32 devices in a mesh: grp: 2 (over y), tm: 8 (over z, x), tile: 2 (over core).
Axes of the slice: x: 2, y: 2, z: 4, core: 2. Of those that a mesh axis runs over, the one named last changes fastest.
Arguments:
- vis_data: float32 [4, 128, 4, 256], P(('grp', 'tile'), 'tm'), parts along dimension 0, may hold values from -6 to 6
- vis_weight: float32 [4, 128, 256], P(('grp', 'tile'), 'tm'), parts along dimension 0, may hold values from 0.2 to 5
- kernel_taps: float32 [4, 128, 2, 8, 256], P(('grp', 'tile'), 'tm'), parts along dimension 0, may hold values from 0.2 to 1
- offsets: int32 [4, 128, 2, 256], P(('grp', 'tile'), 'tm'), parts along dimension 0, may hold values from 0 to 120
- block_patch: int32 [4, 128], P(('grp', 'tile'), 'tm'), parts along dimension 0, may hold values from 0 to 7
- block_count: int32 [4, 8], P(('grp', 'tile'), 'tm'), parts along dimension 0, may hold values from 1 to 16, 64 in all within a row
Outputs:
- image: float32 [2, 2, 8, 256, 256], P(None, None, ('grp', 'tile'), 'tm'), parts along dimension 2
The draws below stay inside these ranges and needn't reach their ends.
There are 2 independent parts, one for each index of `grp`. The reference program is written for one: setup_inputs(seed, part) draws one part's arguments, and reference() takes and returns one part's arrays. A program takes and returns all parts, laid end to end along the dimension named above; each array names one. Nothing has to cross between parts.
Inputs may be any that keep to these rules, and one draw needn't show every extreme that they name: Each row of block_count sums to 64, and its largest entry is 16 in every draw.
All inputs are finite; a program needn't handle non-finite values.
Results may differ from the reference program's by a relative error of at most 0.0037.
Values sent between devices are 32-bit elements; how exact they have to be, the bound alone decides.
No kernel may reach another device: no remote copies, remote signals or barrier semaphores. Data moves between devices by JAX's collectives and lax.ppermute only.
A program may use at most 64 MiB of HBM per device.

```python
import math
import jax
import jax.numpy as jnp
import numpy as np
from jax import lax

G = 256
P_SIZE = 128
K = 8
B = 256
POLS = 2
NT_C = 2
NBLK = 16
BLOCKS = 128
N_TM = 8
N_TILE = 2


def set_ends(result, key, low, high):
    extent = result.shape
    index_at = [jax.random.randint(jax.random.fold_in(key, axis), (), 0, extent[axis]) for axis in range(len(extent))]
    result = result.at[tuple(index_at)].set(low)
    longest = extent.index(max(extent))
    index_at[longest] = (index_at[longest] + 1) % extent[longest]
    return result.at[tuple(index_at)].set(high)


def shard_levels(stream_key, shape, split, least, high):
    factor_of, own = 1.0, jax.random.fold_in(stream_key, 6)
    for position, blocks in split:
        draws = jnp.exp(jax.random.uniform(jax.random.fold_in(own, position), (blocks,), jnp.float32, least / len(split), high / len(split)))
        factor_of = factor_of * jnp.repeat(draws, shape[position] // blocks).reshape([-1 if axis == position else 1 for axis in range(len(shape))])
    return factor_of


def split_up(count, total, limit, slope):
    portions = [(1 << 20) // math.isqrt(rank ** slope) + 1 for rank in range(2, count + 1)]
    rest, given = total - limit - (count - 1), [1] * (count - 1)
    while rest > 0:
        free = [i for i in range(count - 1) if given[i] < limit]
        mass, left = sum([portions[i] for i in free]), rest
        for i in free:
            extra = min(limit - given[i], max(1, left * portions[i] // mass), rest)
            given[i] = given[i] + extra
            rest = rest - extra
    return np.array([limit] + given)


def uneven(own_key, amount, total, reach, skew):
    if amount == 2:
        one = jax.random.randint(own_key, (), max(1, total - reach), min(reach, total - 1) + 1)
        return jnp.stack([one, total - one])
    tallies = jnp.asarray(split_up(amount, total, reach, skew), jnp.int32)
    twos = (amount - 1) // 2
    donor, sink = tallies[1:1 + 2 * twos:2], tallies[2:2 + 2 * twos:2]
    slack = jnp.minimum(donor - 1, reach - sink)
    shifted = jax.random.randint(jax.random.fold_in(own_key, 1), (twos,), 0, 1 << 20) % (slack + 1)
    tallies = tallies.at[1:1 + 2 * twos:2].set(donor - shifted).at[2:2 + 2 * twos:2].set(sink + shifted)
    return tallies[jax.random.permutation(jax.random.fold_in(own_key, 2), amount)]


def centred(rng, extent, width, most, split=(), held_as=jnp.bfloat16):
    values = width * jax.random.normal(rng, extent, jnp.float32)
    if split:
        values = values * shard_levels(rng, extent, split, -0.22, 0.18)
    return jnp.clip(values, -most, most).astype(held_as)


def setup_inputs(seed: int = 0, part: int = 0) -> dict:
    arg_keys = jax.random.split(jax.random.key(seed), 7)
    part_splits = jax.random.split(jax.random.fold_in(arg_keys[6], part), 7)
    vis_data = centred(part_splits[0], (N_TILE, BLOCKS, 4, B), 1.0, 6.0, ((0, 2), (1, 8)), jnp.float32)
    vis_weight = jnp.clip(jnp.exp(math.log(5.0) - 3.218876 * jax.random.uniform(part_splits[1], (N_TILE, BLOCKS, B), jnp.float32) ** shard_levels(part_splits[1], (N_TILE, BLOCKS, B), ((0, 2), (1, 8)), -0.2, 0.2)), 0.2, 5.0)
    kernel_taps = jnp.clip(0.2 + 0.8 * jax.random.uniform(part_splits[2], (N_TILE, BLOCKS, 2, K, B), jnp.float32) ** shard_levels(part_splits[2], (N_TILE, BLOCKS, 2, K, B), ((0, 2), (1, 8)), -0.2, 0.2), 0.2, 1.0)
    offsets = set_ends(jax.random.randint(part_splits[3], (N_TILE, BLOCKS, 2, B), 0, P_SIZE - K + 1), jax.random.fold_in(part_splits[3], 1), 0, P_SIZE - K).astype(jnp.int32)
    block_patch = set_ends(jax.random.randint(part_splits[4], (N_TILE, BLOCKS), 0, 4 * NT_C), jax.random.fold_in(part_splits[4], 1), 0, (4 * NT_C) - 1).astype(jnp.int32)
    block_count = jax.vmap(lambda own: uneven(own, N_TM, NBLK * N_TM // 2, NBLK, 2))(jax.random.split(part_splits[5], N_TILE)).reshape((N_TILE, N_TM)).astype(jnp.int32)
    return dict(vis_data=vis_data, vis_weight=vis_weight, kernel_taps=kernel_taps, offsets=offsets, block_patch=block_patch, block_count=block_count)


def block_patch_grid(vis, weight, taps, offs):
    cells = jnp.arange(P_SIZE, dtype=jnp.int32)
    a_u = jnp.zeros((B, P_SIZE), jnp.float32)
    a_v = jnp.zeros((B, P_SIZE), jnp.float32)
    for i in range(K):
        a_u = a_u + taps[0, i, :, None] * (cells[None, :] == offs[0, :, None] + i).astype(jnp.float32)
        a_v = a_v + taps[1, i, :, None] * (cells[None, :] == offs[1, :, None] + i).astype(jnp.float32)
    x = jnp.concatenate([weight[None, :], weight[None, :] * vis], axis=0)
    left = (x[:, :, None] * a_u[None, :, :]).astype(jnp.bfloat16)
    right = a_v.astype(jnp.bfloat16)
    return jnp.einsum("ekp,kr->epr", left.astype(jnp.float32), right.astype(jnp.float32))


def reference(vis_data, vis_weight, kernel_taps, offsets, block_patch, block_count):
    slots = jnp.arange(4 * NT_C, dtype=jnp.int32)
    grids = []
    for c in range(N_TILE):
        def device_step(d, grid):
            def block_step(j, inner):
                q = (d * NBLK + j).astype(jnp.int32)
                patch = block_patch_grid(vis_data[c, q], vis_weight[c, q], kernel_taps[c, q], offsets[c, q])
                onehot = (slots == block_patch[c, q]).astype(jnp.float32).reshape(NT_C, 2, 2)
                return inner + jnp.einsum("trs,epq->etrpsq", onehot, patch)
            return lax.fori_loop(0, block_count[c, d], block_step, grid)
        zero = jnp.zeros((5, NT_C, 2, P_SIZE, 2, P_SIZE), jnp.float32)
        grid = lax.fori_loop(0, N_TM, device_step, zero)
        grids.append(grid.reshape(5, NT_C * G, G))
    whole = jnp.stack(grids)
    dens = whole[:, 0]
    s1 = jnp.sum(dens)
    s2 = jnp.sum(dens * dens)
    f2 = 2.5 * s1 / s2
    weighted = whole[:, 1:] / (1.0 + f2 * dens[:, None])
    weighted = weighted.reshape(N_TILE, POLS, 2, NT_C, G, G)
    field = weighted[:, :, 0] + 1j * weighted[:, :, 1]
    spectrum = jnp.fft.fft2(field, axes=(-2, -1)) / G
    parts = jnp.stack([jnp.real(spectrum), jnp.imag(spectrum)], axis=2)
    parts = jnp.transpose(parts, (1, 2, 0, 3, 5, 4))
    return parts.reshape(POLS, 2, N_TILE * NT_C, G, G).astype(jnp.float32)
```

```python
import math

import jax
import jax.numpy as jnp
import numpy as np
from jax import lax
from jax.experimental import pallas as pl
from jax.experimental.pallas import tpu as pltpu
from jax.sharding import PartitionSpec as P

G = 256
P_SIZE = 128
K = 8
B = 256
POLS = 2
NT_C = 2
PATCHES = 4 * NT_C
GRIDS = 1 + 2 * POLS
X_ROW = 2 * K
OFF_ROW = X_ROW + GRIDS
ID_ROW = OFF_ROW + 2
ROWS = ID_ROW + 1
HIGH = lax.Precision.HIGHEST
VMEM = pl.BlockSpec(memory_space=pltpu.VMEM)
PARAMS = pltpu.CompilerParams(vmem_limit_bytes=40 * 1024 * 1024)


def pack_kernel(vis_ref, weight_ref, taps_ref, offs_ref, ids_ref, out_ref):
    for j in range(out_ref.shape[0]):
        for side in range(2):
            off = offs_ref[j, side : side + 1, :]
            taps = taps_ref[j, side]
            for bit in range(3):
                moved = pltpu.roll(taps, 1 << bit, 0)
                turn = jnp.broadcast_to((off >> bit) & 1, taps.shape) == 1
                taps = jnp.where(turn, moved, taps)
            out_ref[j, side * K : (side + 1) * K, :] = taps
        weight = weight_ref[j : j + 1, :]
        out_ref[j, X_ROW : X_ROW + 1, :] = weight
        out_ref[j, X_ROW + 1 : OFF_ROW, :] = weight * vis_ref[j]
        out_ref[j, OFF_ROW:ID_ROW, :] = offs_ref[j].astype(jnp.float32)
        out_ref[j, ID_ROW:ROWS, :] = ids_ref[...]


def pack(vis, weight, taps, offs, ids):
    slots = weight.shape[0]
    return pl.pallas_call(
        pack_kernel,
        out_shape=jax.ShapeDtypeStruct((slots, ROWS, B), jnp.float32),
        in_specs=[VMEM] * 5,
        out_specs=VMEM,
        compiler_params=PARAMS,
        name="pack",
    )(vis, weight, taps, offs, ids)


def spread(taps16, off):
    row = lax.broadcasted_iota(jnp.int32, (16, B), 0)
    gap = off.astype(jnp.int32) - row
    step = (gap + 15) >> 4
    inside = (step << 4) - gap < K
    return jnp.where(inside, step, -1).astype(jnp.float32).astype(jnp.bfloat16)


def add_block(buf_ref, ids_ref, acc_ref, j, live):
    block = buf_ref[j]
    rows_u = jnp.concatenate([block[0:K]] * 2, axis=0)
    rows_v = jnp.concatenate([block[K : 2 * K]] * 2, axis=0)
    step_u = spread(rows_u, block[OFF_ROW : OFF_ROW + 1])
    step_v = spread(rows_v, block[OFF_ROW + 1 : OFF_ROW + 2])
    if live is not None:
        rows_v = jnp.where(live, rows_v, 0.0)
    rows_v = rows_v.astype(jnp.bfloat16)
    zero = jnp.zeros((16, B), jnp.bfloat16)
    steps = P_SIZE // 16
    right = jnp.concatenate([jnp.where(step_v == s, rows_v, zero) for s in range(steps)], axis=0)
    hits = [step_u == s for s in range(steps)]
    left = []
    for e in range(GRIDS):
        product = (rows_u * block[X_ROW + e : X_ROW + e + 1]).astype(jnp.bfloat16)
        left += [jnp.where(hit, product, zero) for hit in hits]
    left = jnp.concatenate(left, axis=0)
    patch = lax.dot_general(
        left, right, (((1,), (1,)), ((), ())), preferred_element_type=jnp.float32
    )
    where_at = ids_ref[ID_ROW % 8, j].astype(jnp.int32)
    acc_ref[where_at] += patch


def grid_kernel(n_bufs, first, last, *refs):
    bufs, rest = refs[:n_bufs], refs[n_bufs:-2]
    ids, sems = refs[-2:]
    copies = []
    for i, buf_ref in enumerate(bufs):
        from_rows = buf_ref.at[0, 8 * (ID_ROW // 8) : ROWS, 0:128]
        copies.append(pltpu.make_async_copy(from_rows, ids.at[i], sems.at[i]))
        copies[-1].start()
    if first:
        acc_ref = rest[0]
        acc_ref[...] = jnp.zeros_like(acc_ref)
    else:
        acc_ref = rest[1]
        acc_ref[...] = rest[0][...]
    for i, buf_ref in enumerate(bufs):
        copies[i].wait()
        ids_ref = ids.at[i]
        slots = buf_ref.shape[0]
        count = ids_ref[ID_ROW % 8, slots].astype(jnp.int32)

        def two(pair, _, buf_ref=buf_ref, ids_ref=ids_ref, count=count):
            j = 2 * pair
            add_block(buf_ref, ids_ref, acc_ref, j, None)
            add_block(buf_ref, ids_ref, acc_ref, j + 1, j + 1 < count)
            return 0

        lax.fori_loop(0, (count + 1) // 2, two, 0)
    if last:
        sums_ref = rest[-1]
        dens = acc_ref[:, :P_SIZE, :]
        for i, value in enumerate((dens, dens * dens)):
            part = jnp.sum(value.reshape(-1, 8, P_SIZE), axis=0)
            part = jnp.sum(jnp.sum(part, axis=0, keepdims=True), axis=1, keepdims=True)
            sums_ref[8 * i : 8 * i + 8, :] = jnp.broadcast_to(part, (8, P_SIZE))


def add_blocks(acc, bufs, last=False):
    first = acc is None
    n = len(bufs)
    slots = bufs[0].shape[0]
    cells = (PATCHES, GRIDS * P_SIZE, P_SIZE)
    flops = 2 * n * slots // 2 * GRIDS * P_SIZE * P_SIZE * B
    out_shape = [jax.ShapeDtypeStruct(cells, jnp.float32)]
    if last:
        out_shape.append(jax.ShapeDtypeStruct((16, P_SIZE), jnp.float32))
    args = list(bufs) + ([] if first else [acc])
    out = pl.pallas_call(
        lambda *refs: grid_kernel(n, first, last, *refs),
        out_shape=out_shape,
        in_specs=[VMEM] * len(args),
        out_specs=[VMEM] * len(out_shape),
        scratch_shapes=[pltpu.SMEM((n, 8, 128), jnp.float32), pltpu.SemaphoreType.DMA((n,))],
        compiler_params=PARAMS,
        cost_estimate=pl.CostEstimate(flops=8 * flops, bytes_accessed=6 << 20, transcendentals=0),
        name="grid",
    )(*args)
    return tuple(out) if last else out[0]


def image_kernel(acc_ref, mine_ref, other_ref, row_ref, col_ref, out_ref):
    s1 = mine_ref[0:1, :] + other_ref[0:1, :]
    s2 = mine_ref[8:9, :] + other_ref[8:9, :]
    factor = 2.5 * s1 / s2
    width = out_ref.shape[3]
    flipped = []
    for t in range(NT_C):
        strips = [[] for _ in range(POLS)]
        for pr in range(2):
            tiles = [acc_ref[4 * t + 2 * pr + pc] for pc in range(2)]
            weight = [1.0 / (1.0 + factor * tile[:P_SIZE]) for tile in tiles]
            for pol in range(POLS):
                parts = []
                for e in (1 + 2 * pol, 2 + 2 * pol):
                    for pc in range(2):
                        parts.append(tiles[pc][e * P_SIZE : (e + 1) * P_SIZE] * weight[pc])
                strips[pol].append(jnp.concatenate(parts, axis=1))
        for pol in range(POLS):
            z = jnp.concatenate(strips[pol], axis=0)
            y = jnp.dot(z, row_ref[...], precision=HIGH, preferred_element_type=jnp.float32)
            flipped.append(y.T)
    stacked = jnp.concatenate(flipped, axis=0)
    done = jnp.dot(stacked, col_ref[...], precision=HIGH, preferred_element_type=jnp.float32)
    for t in range(NT_C):
        for pol in range(POLS):
            at = (t * POLS + pol) * 2 * width
            real, imag = done[at : at + width], done[at + width : at + 2 * width]
            out_ref[pol, 0, t] = real[:, :G] + imag[:, G:]
            out_ref[pol, 1, t] = imag[:, :G] - real[:, G:]


def make_image(acc, mine, other, row_table, col_table, width):
    return pl.pallas_call(
        image_kernel,
        out_shape=jax.ShapeDtypeStruct((POLS, 2, NT_C, width, G), jnp.float32),
        in_specs=[VMEM] * 5,
        out_specs=VMEM,
        compiler_params=PARAMS,
        name="image",
    )(acc, mine, other, row_table, col_table)


def dft_tables():
    index = np.arange(G)
    phase = (index[:, None] * index[None, :] % G) * (2.0 * math.pi / G)
    return np.cos(phase).astype(np.float32), np.sin(phase).astype(np.float32)


def by_gather(packed, n_tm):
    depth = n_tm // 2
    order = list(range(0, depth, 2)) + list(range(1, depth, 2))[::-1]
    after = {order[i]: order[(i + 1) % depth] for i in range(depth)}
    ring = [(2 * z + x, 2 * after[z] + x) for z in range(depth) for x in range(2)]
    swap = [(i, i ^ 1) for i in range(n_tm)]
    held = packed
    waiting = [packed]
    acc = None
    for step in range(depth):
        beside = lax.ppermute(held, "tm", swap)
        ahead = lax.ppermute(held, "tm", ring) if step < depth - 1 else None
        acc = add_blocks(acc, waiting)
        waiting = [beside] if ahead is None else [beside, ahead]
        held = ahead
    return add_blocks(acc, waiting, last=True)


def rest_by_rows(acc, cosine, sine):
    grid = acc.reshape(NT_C, 2, 2, GRIDS, P_SIZE, P_SIZE)
    flat = jnp.transpose(grid, (3, 0, 1, 4, 2, 5)).reshape(GRIDS, NT_C * G, G)
    owned = lax.psum_scatter(flat, "tm", scatter_dimension=1, tiled=True)
    dens = owned[0]
    totals = lax.psum((jnp.sum(dens), jnp.sum(dens * dens)), ("tm", "tile"))
    factor = 2.5 * totals[0] / totals[1]
    weighted = owned[1:] / (1.0 + factor * dens[None])
    weighted = weighted.reshape(POLS, 2, dens.shape[0], G)
    real, imag = weighted[:, 0], weighted[:, 1]

    def rows(a, b):
        return jnp.einsum("prj,jn->prn", a, b, precision=HIGH)

    done = jnp.stack([rows(real, cosine) + rows(imag, sine), rows(imag, cosine) - rows(real, sine)], axis=1)
    width = G // lax.axis_size("tm")
    every_row = lax.all_gather(done, "tm", axis=2, tiled=True)
    columns = lax.dynamic_slice_in_dim(every_row, lax.axis_index("tm") * width, width, 3)
    columns = columns.reshape(POLS, 2, NT_C, G, width)
    real, imag = columns[:, 0], columns[:, 1]

    def cols(a, b):
        return jnp.einsum("mi,ptic->ptcm", a, b, precision=HIGH)

    out = jnp.stack([cols(cosine, real) + cols(sine, imag), cols(cosine, imag) - cols(sine, real)], axis=1)
    return out / G


def body(vis_data, vis_weight, kernel_taps, offsets, block_patch, block_count):
    slots = vis_weight.shape[1]
    n_tm = lax.axis_size("tm")
    ids = jnp.concatenate([block_patch[0], block_count[0]]).astype(jnp.float32)
    ids = jnp.pad(ids, (0, B - slots - 1))[None]
    packed = pack(vis_data[0], vis_weight[0], kernel_taps[0], offsets[0], ids)
    cosine, sine = dft_tables()
    if n_tm > 8:
        return rest_by_rows(add_blocks(None, [packed]), jnp.asarray(cosine), jnp.asarray(sine))
    acc, mine = by_gather(packed, n_tm)
    n_tile = lax.axis_size("tile")
    other = lax.ppermute(mine, "tile", [(i, n_tile - 1 - i) for i in range(n_tile)])
    width = G // n_tm
    start = lax.axis_index("tm") * width
    cut_cos = lax.dynamic_slice_in_dim(jnp.asarray(cosine), start, width, 1)
    cut_sin = lax.dynamic_slice_in_dim(jnp.asarray(sine), start, width, 1)
    row_table = jnp.concatenate(
        [jnp.concatenate([cut_cos, -cut_sin], axis=1), jnp.concatenate([cut_sin, cut_cos], axis=1)], axis=0
    )
    col_table = jnp.asarray(np.concatenate([cosine, sine], axis=1) / G)
    return make_image(acc, mine, other, row_table, col_table, width)


def solution(mesh):
    return jax.shard_map(
        body,
        mesh=mesh,
        in_specs=(
            P(("grp", "tile"), "tm", None, None),
            P(("grp", "tile"), "tm", None),
            P(("grp", "tile"), "tm", None, None, None),
            P(("grp", "tile"), "tm", None, None),
            P(("grp", "tile"), "tm"),
            P(("grp", "tile"), "tm"),
        ),
        out_specs=P(None, None, ("grp", "tile"), "tm", None),
        check_vma=False,
    )
```

```python
import math

import jax
import jax.numpy as jnp
import numpy as np
from jax import lax
from jax.experimental import pallas as pl
from jax.experimental.pallas import tpu as pltpu
from jax.sharding import PartitionSpec as P

G = 256
P_SIZE = 128
K = 8
B = 256
POLS = 2
NT_C = 2
PATCHES = 4 * NT_C
GRIDS = 1 + 2 * POLS
X_ROW = 2 * K
OFF_ROW = X_ROW + GRIDS
ID_ROW = OFF_ROW + 2
ROWS = ID_ROW + 1
COUNT_LANE = 64
HIGH = lax.Precision.HIGHEST
VMEM = pl.BlockSpec(memory_space=pltpu.VMEM)
PARAMS = pltpu.CompilerParams(vmem_limit_bytes=20 * 1024 * 1024)


def pack_kernel(sizes, vis_hbm, weight_hbm, taps_hbm, offs_hbm, patch_ref, count_ref, *refs):
    outs, (vis_ref, weight_ref, taps_ref, offs_ref, sems) = refs[: len(sizes)], refs[len(sizes) :]
    pairs = ((offs_hbm, offs_ref), (taps_hbm, taps_ref), (weight_hbm, weight_ref), (vis_hbm, vis_ref))
    copies = [pltpu.make_async_copy(a, b, sems.at[i]) for i, (a, b) in enumerate(pairs)]
    for copy in copies:
        copy.start()
    lane = lax.broadcasted_iota(jnp.int32, (1, B), 1)
    places = []
    base = 0
    for out_ref, size in zip(outs, sizes):
        row = jnp.where(lane == COUNT_LANE, jnp.clip(count_ref[0, 0] - base, 0, size), 0)
        for j in range(size):
            row = jnp.where(lane == j, patch_ref[0, base + j], row)
            places.append((out_ref, j, base + j))
        out_ref[0, ID_ROW:ROWS, :] = row.astype(jnp.float32)
        base += size
    copies[0].wait()
    copies[1].wait()
    for out_ref, j, at in places:
        for side in range(2):
            off = offs_ref[at, side : side + 1, :]
            taps = taps_ref[at, side]
            for bit in range(3):
                moved = pltpu.roll(taps, 1 << bit, 0)
                turn = jnp.broadcast_to((off >> bit) & 1, taps.shape) == 1
                taps = jnp.where(turn, moved, taps)
            out_ref[j, side * K : (side + 1) * K, :] = taps
        out_ref[j, OFF_ROW:ID_ROW, :] = offs_ref[at].astype(jnp.float32)
        if j:
            out_ref[j, ID_ROW:ROWS, :] = jnp.zeros((1, B), jnp.float32)
    copies[2].wait()
    copies[3].wait()
    for out_ref, j, at in places:
        weight = weight_ref[at : at + 1, :]
        out_ref[j, X_ROW : X_ROW + 1, :] = weight
        out_ref[j, X_ROW + 1 : OFF_ROW, :] = weight * vis_ref[at]


def pack(sizes, vis, weight, taps, offs, patches, count):
    arrays = (vis, weight, taps, offs)
    smem = pl.BlockSpec(memory_space=pltpu.SMEM)
    return pl.pallas_call(
        lambda *refs: pack_kernel(sizes, *refs),
        out_shape=[jax.ShapeDtypeStruct((size, ROWS, B), jnp.float32) for size in sizes],
        in_specs=[pl.BlockSpec(memory_space=pltpu.HBM)] * 4 + [smem] * 2,
        out_specs=[VMEM] * len(sizes),
        scratch_shapes=[pltpu.VMEM(a.shape, a.dtype) for a in arrays] + [pltpu.SemaphoreType.DMA((4,))],
        compiler_params=pltpu.CompilerParams(vmem_limit_bytes=62 * 1024 * 1024),
        name="pack",
    )(*arrays, patches, count)


def spread(taps16, off):
    row = lax.broadcasted_iota(jnp.int32, (16, B), 0)
    gap = off.astype(jnp.int32) - row
    step = (gap + 15) >> 4
    inside = (step << 4) - gap < K
    return jnp.where(inside, step, -1).astype(jnp.float32).astype(jnp.bfloat16)


def add_block(buf_ref, base, ids_ref, acc_ref, j, live):
    block = buf_ref[base + j]
    rows_u = jnp.concatenate([block[0:K]] * 2, axis=0)
    rows_v = jnp.concatenate([block[K : 2 * K]] * 2, axis=0)
    step_u = spread(rows_u, block[OFF_ROW : OFF_ROW + 1])
    step_v = spread(rows_v, block[OFF_ROW + 1 : OFF_ROW + 2])
    if live is not None:
        rows_v = jnp.where(live, rows_v, 0.0)
    rows_v = rows_v.astype(jnp.bfloat16)
    zero = jnp.zeros((16, B), jnp.bfloat16)
    steps = P_SIZE // 16
    right = jnp.concatenate([jnp.where(step_v == s, rows_v, zero) for s in range(steps)], axis=0)
    hits = [step_u == s for s in range(steps)]
    left = []
    for e in range(GRIDS):
        product = (rows_u * block[X_ROW + e : X_ROW + e + 1]).astype(jnp.bfloat16)
        left += [jnp.where(hit, product, zero) for hit in hits]
    left = jnp.concatenate(left, axis=0)
    patch = lax.dot_general(
        left, right, (((1,), (1,)), ((), ())), preferred_element_type=jnp.float32
    )
    where_at = ids_ref[ID_ROW % 8, j].astype(jnp.int32)
    acc_ref[where_at] += patch


def grid_kernel(parts, first, last, *refs):
    n = len(parts)
    bufs = refs[:n]
    acc_ref = refs[n] if first else refs[n + 1]
    ids, sems = refs[-2:]
    pieces = [(buf, base, size) for buf, part in zip(bufs, parts) for base, size in part]
    copies = []
    for i, (buf_ref, base, _) in enumerate(pieces):
        from_rows = buf_ref.at[base, 8 * (ID_ROW // 8) : ROWS, 0:128]
        copies.append(pltpu.make_async_copy(from_rows, ids.at[i], sems.at[i]))
        copies[-1].start()
    if first:
        acc_ref[...] = jnp.zeros_like(acc_ref)
    for i, (buf_ref, base, size) in enumerate(pieces):
        copies[i].wait()
        ids_ref = ids.at[i]
        count = ids_ref[ID_ROW % 8, COUNT_LANE].astype(jnp.int32)

        def two(pair, _, buf_ref=buf_ref, ids_ref=ids_ref, count=count, base=base, size=size):
            j = 2 * pair
            add_block(buf_ref, base, ids_ref, acc_ref, j, None)
            add_block(buf_ref, base, ids_ref, acc_ref, jnp.minimum(j + 1, size - 1), j + 1 < count)
            return 0

        lax.fori_loop(0, (count + 1) // 2, two, 0)
    if last:
        sums_ref = refs[-3]
        dens = acc_ref[:, :P_SIZE, :]
        for i, value in enumerate((dens, dens * dens)):
            part = jnp.sum(value.reshape(-1, 8, P_SIZE), axis=0)
            part = jnp.sum(jnp.sum(part, axis=0, keepdims=True), axis=1, keepdims=True)
            sums_ref[8 * i : 8 * i + 8, :] = jnp.broadcast_to(part, (8, P_SIZE))


def add_blocks(acc, bufs, last=False):
    first = acc is None
    parts = []
    for array, sizes in bufs:
        starts = np.cumsum([0, *sizes])[:-1]
        parts.append(tuple((int(start), size) for start, size in zip(starts, sizes)))
    pieces = sum(len(part) for part in parts)
    slots = sum(sum(sizes) for _, sizes in bufs)
    out_shape = [jax.ShapeDtypeStruct((PATCHES, GRIDS * P_SIZE, P_SIZE), jnp.float32)]
    if last:
        out_shape.append(jax.ShapeDtypeStruct((16, P_SIZE), jnp.float32))
    args = [array for array, _ in bufs] + ([] if first else [acc])
    flops = 8 * slots * GRIDS * P_SIZE * P_SIZE * B
    out = pl.pallas_call(
        lambda *refs: grid_kernel(parts, first, last, *refs),
        out_shape=out_shape,
        in_specs=[VMEM] * len(args),
        out_specs=[VMEM] * len(out_shape),
        scratch_shapes=[pltpu.SMEM((pieces, 8, 128), jnp.float32), pltpu.SemaphoreType.DMA((pieces,))],
        input_output_aliases={} if first else {len(bufs): 0},
        compiler_params=PARAMS,
        cost_estimate=pl.CostEstimate(flops=flops, bytes_accessed=1 << 20, transcendentals=0),
        name="grid",
    )(*args)
    return tuple(out) if last else out[0]


def two_parts(value):
    high = value.astype(jnp.bfloat16)
    return high, (value - high.astype(jnp.float32)).astype(jnp.bfloat16)


def dot_parts(value, table_ref):
    width = table_ref.shape[1] // 2
    high, low = two_parts(value)
    both = jnp.dot(high, table_ref[...], preferred_element_type=jnp.float32)
    return both[:, :width] + both[:, width:] + jnp.dot(low, table_ref[:, :width], preferred_element_type=jnp.float32)


def image_kernel(acc_ref, mine_ref, other_ref, row_ref, col_ref, out_ref):
    s1 = mine_ref[0:1, :] + other_ref[0:1, :]
    s2 = mine_ref[8:9, :] + other_ref[8:9, :]
    factor = 2.5 * s1 / s2
    width = out_ref.shape[3]
    flipped = []
    for t in range(NT_C):
        strips = [[] for _ in range(POLS)]
        for pr in range(2):
            tiles = [acc_ref.at[4 * t + 2 * pr + pc] for pc in range(2)]
            weight = [1.0 / (1.0 + factor * tile[:P_SIZE]) for tile in tiles]
            for pol in range(POLS):
                parts = []
                for e in (1 + 2 * pol, 2 + 2 * pol):
                    for pc in range(2):
                        parts.append(tiles[pc][e * P_SIZE : (e + 1) * P_SIZE] * weight[pc])
                strips[pol].append(jnp.concatenate(parts, axis=1))
        for pol in range(POLS):
            flipped.append(dot_parts(jnp.concatenate(strips[pol], axis=0), row_ref).T)
    done = dot_parts(jnp.concatenate(flipped, axis=0), col_ref)
    for t in range(NT_C):
        for pol in range(POLS):
            at = (t * POLS + pol) * 2 * width
            real, imag = done[at : at + width], done[at + width : at + 2 * width]
            out_ref[pol, 0, t] = real[:, :G] + imag[:, G:]
            out_ref[pol, 1, t] = imag[:, :G] - real[:, G:]


def make_image(acc, mine, other, row_table, col_table, width):
    return pl.pallas_call(
        image_kernel,
        out_shape=jax.ShapeDtypeStruct((POLS, 2, NT_C, width, G), jnp.float32),
        in_specs=[VMEM] * 5,
        out_specs=VMEM,
        compiler_params=PARAMS,
        name="image",
    )(acc, mine, other, row_table, col_table)


def dft_tables():
    index = np.arange(G)
    phase = (index[:, None] * index[None, :] % G) * (2.0 * math.pi / G)
    return np.cos(phase).astype(np.float32), np.sin(phase).astype(np.float32)


def stream_sizes(slots):
    pairs = max(1, 3 * slots // 16)
    return (slots - pairs + 1) // 2, (slots - pairs) // 2, pairs


def by_gather(streams, sizes, n_tm):
    depth = n_tm // 2
    order = list(range(0, depth, 2)) + list(range(1, depth, 2))[::-1]
    after = {order[i]: order[(i + 1) % depth] for i in range(depth)}
    ring = [(2 * z + x, 2 * after[z] + x) for z in range(depth) for x in range(2)]
    swap = [(i, i ^ 1) for i in range(n_tm)]
    held = list(streams)
    kinds = [(size,) for size in sizes]
    arrived = list(zip(streams, kinds))
    acc = None
    for step in range(depth):
        ahead = []
        if step == 0:
            pair = lax.ppermute(held[-1], "tm", swap)
        if step < depth - 1:
            ahead = [lax.ppermute(a, "tm", ring) for a in held[:-1]]
        beside = [lax.ppermute(a, "tm", swap) for a in held[:-1]]
        acc = add_blocks(acc, arrived)
        arrived = list(zip(beside, kinds)) + list(zip(ahead, kinds))
        if step == 0:
            arrived.append((pair, kinds[-1]))
            held[-1] = jnp.concatenate([held[-1], pair], axis=0)
            kinds[-1] = kinds[-1] * 2
        else:
            arrived.append((held[-1], kinds[-1]))
        if step < depth - 1:
            held = ahead + [lax.ppermute(held[-1], "tm", ring)]
    acc = add_blocks(acc, arrived[:1] + arrived[2:])
    return add_blocks(acc, arrived[1:2], last=True)


def rest_by_rows(acc, cosine, sine):
    grid = acc.reshape(NT_C, 2, 2, GRIDS, P_SIZE, P_SIZE)
    flat = jnp.transpose(grid, (3, 0, 1, 4, 2, 5)).reshape(GRIDS, NT_C * G, G)
    owned = lax.psum_scatter(flat, "tm", scatter_dimension=1, tiled=True)
    dens = owned[0]
    totals = lax.psum((jnp.sum(dens), jnp.sum(dens * dens)), ("tm", "tile"))
    factor = 2.5 * totals[0] / totals[1]
    weighted = owned[1:] / (1.0 + factor * dens[None])
    weighted = weighted.reshape(POLS, 2, dens.shape[0], G)
    real, imag = weighted[:, 0], weighted[:, 1]

    def rows(a, b):
        return jnp.einsum("prj,jn->prn", a, b, precision=HIGH)

    done = jnp.stack([rows(real, cosine) + rows(imag, sine), rows(imag, cosine) - rows(real, sine)], axis=1)
    width = G // lax.axis_size("tm")
    every_row = lax.all_gather(done, "tm", axis=2, tiled=True)
    columns = lax.dynamic_slice_in_dim(every_row, lax.axis_index("tm") * width, width, 3)
    columns = columns.reshape(POLS, 2, NT_C, G, width)
    real, imag = columns[:, 0], columns[:, 1]

    def cols(a, b):
        return jnp.einsum("mi,ptic->ptcm", a, b, precision=HIGH)

    out = jnp.stack([cols(cosine, real) + cols(sine, imag), cols(cosine, imag) - cols(sine, real)], axis=1)
    return out / G


def body(vis_data, vis_weight, kernel_taps, offsets, block_patch, block_count):
    slots = vis_weight.shape[1]
    n_tm = lax.axis_size("tm")
    sizes = stream_sizes(slots) if n_tm <= 8 else (slots,)
    arrays = (vis_data[0], vis_weight[0], kernel_taps[0], offsets[0])
    streams = pack(sizes, *arrays, block_patch, block_count)
    cosine, sine = dft_tables()
    if n_tm > 8:
        return rest_by_rows(add_blocks(None, [(streams[0], sizes)]), jnp.asarray(cosine), jnp.asarray(sine))
    acc, mine = by_gather(streams, sizes, n_tm)
    n_tile = lax.axis_size("tile")
    other = lax.ppermute(mine, "tile", [(i, n_tile - 1 - i) for i in range(n_tile)])
    width = G // n_tm
    start = lax.axis_index("tm") * width
    cut_cos = lax.dynamic_slice_in_dim(jnp.asarray(cosine), start, width, 1)
    cut_sin = lax.dynamic_slice_in_dim(jnp.asarray(sine), start, width, 1)
    row_table = jnp.concatenate(
        [jnp.concatenate([cut_cos, -cut_sin], axis=1), jnp.concatenate([cut_sin, cut_cos], axis=1)], axis=0
    )
    row_table = jnp.concatenate(two_parts(row_table), axis=1)
    col_table = jnp.concatenate(two_parts(jnp.asarray(np.concatenate([cosine, sine], axis=1) / G)), axis=1)
    return make_image(acc, mine, other, row_table, col_table, width)


def solution(mesh):
    return jax.shard_map(
        body,
        mesh=mesh,
        in_specs=(
            P(("grp", "tile"), "tm", None, None),
            P(("grp", "tile"), "tm", None),
            P(("grp", "tile"), "tm", None, None, None),
            P(("grp", "tile"), "tm", None, None),
            P(("grp", "tile"), "tm"),
            P(("grp", "tile"), "tm"),
        ),
        out_specs=P(None, None, ("grp", "tile"), "tm", None),
        check_vma=False,
    )
```

```python
import math

import jax
import jax.numpy as jnp
import ml_dtypes
import numpy as np
from jax import lax
from jax.experimental import pallas as pl
from jax.experimental.pallas import tpu as pltpu
from jax.sharding import PartitionSpec as P

G = 256
P_SIZE = 128
K = 8
B = 256
POLS = 2
NT_C = 2
PATCHES = 4 * NT_C
GRIDS = 1 + 2 * POLS
X_ROW = 2 * K
OFF_ROW = X_ROW + GRIDS
ID_ROW = OFF_ROW + 2
ROWS = ID_ROW + 1
COUNT_LANE = 64
UNROLL = 4
HIGH = lax.Precision.HIGHEST
VMEM = pl.BlockSpec(memory_space=pltpu.VMEM)
PARAMS = pltpu.CompilerParams(vmem_limit_bytes=20 * 1024 * 1024)


def pack_kernel(pieces, vis_hbm, weight_hbm, taps_hbm, offs_hbm, patch_ref, count_ref, out_ref, *scratch):
    vis_ref, weight_ref, taps_ref, offs_ref, sems = scratch
    pairs = ((offs_hbm, offs_ref), (taps_hbm, taps_ref), (weight_hbm, weight_ref), (vis_hbm, vis_ref))
    copies = [pltpu.make_async_copy(a, b, sems.at[i]) for i, (a, b) in enumerate(pairs)]
    for copy in copies:
        copy.start()
    lane = lax.broadcasted_iota(jnp.int32, (1, B), 1)
    base = 0
    for size in pieces:
        row = jnp.where(lane == COUNT_LANE, jnp.clip(count_ref[0, 0] - base, 0, size), 0)
        for j in range(size):
            row = jnp.where(lane == j, patch_ref[0, base + j], row)
        row = row.astype(jnp.float32)
        for j in range(size):
            out_ref[base + j, ID_ROW:ROWS, :] = row
        base += size
    copies[0].wait()
    copies[1].wait()
    for at in range(out_ref.shape[0]):
        for side in range(2):
            off = offs_ref[at, side : side + 1, :]
            taps = taps_ref[at, side]
            for bit in range(3):
                moved = pltpu.roll(taps, 1 << bit, 0)
                turn = jnp.broadcast_to((off >> bit) & 1, taps.shape) == 1
                taps = jnp.where(turn, moved, taps)
            out_ref[at, side * K : (side + 1) * K, :] = taps
        out_ref[at, OFF_ROW:ID_ROW, :] = offs_ref[at].astype(jnp.float32)
    copies[2].wait()
    copies[3].wait()
    for at in range(out_ref.shape[0]):
        weight = weight_ref[at : at + 1, :]
        out_ref[at, X_ROW : X_ROW + 1, :] = weight
        out_ref[at, X_ROW + 1 : OFF_ROW, :] = weight * vis_ref[at]


def pack(pieces, vis, weight, taps, offs, patches, count):
    arrays = (vis, weight, taps, offs)
    smem = pl.BlockSpec(memory_space=pltpu.SMEM)
    return pl.pallas_call(
        lambda *refs: pack_kernel(pieces, *refs),
        out_shape=jax.ShapeDtypeStruct((sum(pieces), ROWS, B), jnp.float32),
        in_specs=[pl.BlockSpec(memory_space=pltpu.HBM)] * 4 + [smem] * 2,
        out_specs=VMEM,
        scratch_shapes=[pltpu.VMEM(a.shape, a.dtype) for a in arrays] + [pltpu.SemaphoreType.DMA((4,))],
        compiler_params=pltpu.CompilerParams(vmem_limit_bytes=62 * 1024 * 1024),
        name="pack",
    )(*arrays, patches, count)


def spread(off):
    row = lax.broadcasted_iota(jnp.int32, (16, B), 0)
    gap = off.astype(jnp.int32) - row
    step = (gap + 15) >> 4
    inside = (step << 4) - gap < K
    return jnp.where(inside, step, -1).astype(jnp.float32).astype(jnp.bfloat16)


def block_factors(block, live):
    rows_u = jnp.concatenate([block[0:K]] * 2, axis=0)
    rows_v = jnp.concatenate([block[K : 2 * K]] * 2, axis=0)
    step_u = spread(block[OFF_ROW : OFF_ROW + 1])
    step_v = spread(block[OFF_ROW + 1 : OFF_ROW + 2])
    if live is not None:
        rows_v = jnp.where(live, rows_v, 0.0)
    rows_v = rows_v.astype(jnp.bfloat16)
    zero = jnp.zeros((16, B), jnp.bfloat16)
    steps = P_SIZE // 16
    right = jnp.concatenate([jnp.where(step_v == s, rows_v, zero) for s in range(steps)], axis=0)
    hits = [step_u == s for s in range(steps)]
    left = []
    for e in range(GRIDS):
        product = (rows_u * block[X_ROW + e : X_ROW + e + 1]).astype(jnp.bfloat16)
        left += [jnp.where(hit, product, zero) for hit in hits]
    return jnp.concatenate(left, axis=0), right


def add_some(buf_ref, base, size, ids_ref, acc_ref, first, count):
    waiting = None
    for i in range(UNROLL):
        j = first if i == 0 else jnp.minimum(first + i, size - 1)
        left, right = block_factors(buf_ref[base + j], None if i == 0 else first + i < count)
        patch = lax.dot_general(
            left, right, (((1,), (1,)), ((), ())), preferred_element_type=jnp.float32
        )
        if waiting is not None:
            acc_ref[waiting[0]] += waiting[1]
        waiting = ids_ref[ID_ROW % 8, j].astype(jnp.int32), patch
    acc_ref[waiting[0]] += waiting[1]


def grid_kernel(parts, first, last, *refs):
    n = len(parts)
    bufs = refs[:n]
    acc_ref = refs[n] if first else refs[n + 1]
    ids, sems = refs[-2:]
    pieces = [(buf, base, size) for buf, part in zip(bufs, parts) for base, size in part]
    copies = []
    for i, (buf_ref, base, _) in enumerate(pieces):
        from_rows = buf_ref.at[base, 8 * (ID_ROW // 8) : ROWS, 0:128]
        copies.append(pltpu.make_async_copy(from_rows, ids.at[i], sems.at[i]))
        copies[-1].start()
    if first:
        acc_ref[...] = jnp.zeros_like(acc_ref)
    for i, (buf_ref, base, size) in enumerate(pieces):
        copies[i].wait()
        ids_ref = ids.at[i]
        count = ids_ref[ID_ROW % 8, COUNT_LANE].astype(jnp.int32)

        def some(step, _, buf_ref=buf_ref, ids_ref=ids_ref, count=count, base=base, size=size):
            add_some(buf_ref, base, size, ids_ref, acc_ref, UNROLL * step, count)
            return 0

        lax.fori_loop(0, (count + UNROLL - 1) // UNROLL, some, 0)
    if last:
        sums_ref = refs[-3]
        dens = acc_ref[:, :P_SIZE, :]
        for i, value in enumerate((dens, dens * dens)):
            part = jnp.sum(value.reshape(-1, 8, P_SIZE), axis=0)
            part = jnp.sum(jnp.sum(part, axis=0, keepdims=True), axis=1, keepdims=True)
            sums_ref[8 * i : 8 * i + 8, :] = jnp.broadcast_to(part, (8, P_SIZE))


def add_blocks(acc, bufs, last=False):
    first = acc is None
    parts = []
    for array, sizes in bufs:
        starts = np.cumsum([0, *sizes])[:-1]
        parts.append(tuple((int(start), size) for start, size in zip(starts, sizes)))
    pieces = sum(len(part) for part in parts)
    slots = sum(sum(sizes) for _, sizes in bufs)
    out_shape = [jax.ShapeDtypeStruct((PATCHES, GRIDS * P_SIZE, P_SIZE), jnp.float32)]
    if last:
        out_shape.append(jax.ShapeDtypeStruct((16, P_SIZE), jnp.float32))
    args = [array for array, _ in bufs] + ([] if first else [acc])
    flops = 8 * slots * GRIDS * P_SIZE * P_SIZE * B
    out = pl.pallas_call(
        lambda *refs: grid_kernel(parts, first, last, *refs),
        out_shape=out_shape,
        in_specs=[VMEM] * len(args),
        out_specs=[VMEM] * len(out_shape),
        scratch_shapes=[pltpu.SMEM((pieces, 8, 128), jnp.float32), pltpu.SemaphoreType.DMA((pieces,))],
        input_output_aliases={} if first else {len(bufs): 0},
        compiler_params=PARAMS,
        cost_estimate=pl.CostEstimate(flops=flops, bytes_accessed=1 << 20, transcendentals=0),
        name="grid",
    )(*args)
    return tuple(out) if last else out[0]


def two_parts(value):
    high = value.astype(jnp.bfloat16)
    return high, (value - high.astype(jnp.float32)).astype(jnp.bfloat16)


def dot_parts(value, table_ref):
    width = table_ref.shape[1] // 2
    high, low = two_parts(value)
    both = jnp.dot(high, table_ref[...], preferred_element_type=jnp.float32)
    return both[:, :width] + both[:, width:] + jnp.dot(low, table_ref[:, :width], preferred_element_type=jnp.float32)


def image_kernel(acc_ref, mine_ref, other_ref, row_ref, col_ref, out_ref):
    s1 = mine_ref[0:1, :] + other_ref[0:1, :]
    s2 = mine_ref[8:9, :] + other_ref[8:9, :]
    factor = 2.5 * s1 / s2
    width = out_ref.shape[3]
    flipped = []
    for t in range(NT_C):
        strips = [[] for _ in range(POLS)]
        for pr in range(2):
            tiles = [acc_ref.at[4 * t + 2 * pr + pc] for pc in range(2)]
            weight = [1.0 / (1.0 + factor * tile[:P_SIZE]) for tile in tiles]
            for pol in range(POLS):
                parts = []
                for e in (1 + 2 * pol, 2 + 2 * pol):
                    for pc in range(2):
                        parts.append(tiles[pc][e * P_SIZE : (e + 1) * P_SIZE] * weight[pc])
                strips[pol].append(jnp.concatenate(parts, axis=1))
        for pol in range(POLS):
            flipped.append(dot_parts(jnp.concatenate(strips[pol], axis=0), row_ref).T)
    done = dot_parts(jnp.concatenate(flipped, axis=0), col_ref)
    for t in range(NT_C):
        for pol in range(POLS):
            at = (t * POLS + pol) * 2 * width
            real, imag = done[at : at + width], done[at + width : at + 2 * width]
            out_ref[pol, 0, t] = real[:, :G] + imag[:, G:]
            out_ref[pol, 1, t] = imag[:, :G] - real[:, G:]


def make_image(acc, mine, other, row_table, col_table, width):
    return pl.pallas_call(
        image_kernel,
        out_shape=jax.ShapeDtypeStruct((POLS, 2, NT_C, width, G), jnp.float32),
        in_specs=[VMEM] * 5,
        out_specs=VMEM,
        compiler_params=PARAMS,
        name="image",
    )(acc, mine, other, row_table, col_table)


def dft_tables():
    index = np.arange(G)
    phase = (index[:, None] * index[None, :] % G) * (2.0 * math.pi / G)
    return np.cos(phase).astype(np.float32), np.sin(phase).astype(np.float32)


def np_parts(table):
    high = table.astype(ml_dtypes.bfloat16)
    low = (table - high.astype(np.float32)).astype(ml_dtypes.bfloat16)
    return np.concatenate([high, low], axis=-1)


def image_tables(n_tm):
    cosine, sine = dft_tables()
    rows = []
    for cos_part, sin_part in zip(np.split(cosine, n_tm, axis=1), np.split(sine, n_tm, axis=1)):
        rows.append(np_parts(np.block([[cos_part, -sin_part], [sin_part, cos_part]])))
    return np.stack(rows), np_parts(np.concatenate([cosine, sine], axis=1) / G)


def by_gather(packed, pieces, n_tm):
    order = list(range(0, n_tm, 2)) + list(range(1, n_tm, 2))[::-1]
    up = [(order[i], order[(i + 1) % n_tm]) for i in range(n_tm)]
    down = [(b, a) for a, b in up]
    half = sum(pieces[: len(pieces) // 2])
    cut = (pieces[: len(pieces) // 2], pieces[len(pieces) // 2 :])
    above, below = packed, packed
    arrived = [(packed, pieces)]
    acc = None
    for step in range(1, n_tm // 2 + 1):
        if step < n_tm // 2:
            above = lax.ppermute(above, "tm", up)
            below = lax.ppermute(below, "tm", down)
            next_ones = [(above, pieces), (below, pieces)]
        else:
            above = lax.ppermute(above[:half], "tm", up)
            below = lax.ppermute(below[half:], "tm", down)
            next_ones = [(above, cut[0]), (below, cut[1])]
        acc = add_blocks(acc, arrived)
        arrived = next_ones
    return add_blocks(acc, arrived, last=True)


def rest_by_rows(acc, cosine, sine):
    grid = acc.reshape(NT_C, 2, 2, GRIDS, P_SIZE, P_SIZE)
    flat = jnp.transpose(grid, (3, 0, 1, 4, 2, 5)).reshape(GRIDS, NT_C * G, G)
    owned = lax.psum_scatter(flat, "tm", scatter_dimension=1, tiled=True)
    dens = owned[0]
    totals = lax.psum((jnp.sum(dens), jnp.sum(dens * dens)), ("tm", "tile"))
    factor = 2.5 * totals[0] / totals[1]
    weighted = owned[1:] / (1.0 + factor * dens[None])
    weighted = weighted.reshape(POLS, 2, dens.shape[0], G)
    real, imag = weighted[:, 0], weighted[:, 1]

    def rows(a, b):
        return jnp.einsum("prj,jn->prn", a, b, precision=HIGH)

    done = jnp.stack([rows(real, cosine) + rows(imag, sine), rows(imag, cosine) - rows(real, sine)], axis=1)
    width = G // lax.axis_size("tm")
    every_row = lax.all_gather(done, "tm", axis=2, tiled=True)
    columns = lax.dynamic_slice_in_dim(every_row, lax.axis_index("tm") * width, width, 3)
    columns = columns.reshape(POLS, 2, NT_C, G, width)
    real, imag = columns[:, 0], columns[:, 1]

    def cols(a, b):
        return jnp.einsum("mi,ptic->ptcm", a, b, precision=HIGH)

    out = jnp.stack([cols(cosine, real) + cols(sine, imag), cols(cosine, imag) - cols(sine, real)], axis=1)
    return out / G


def body(vis_data, vis_weight, kernel_taps, offsets, block_patch, block_count):
    slots = vis_weight.shape[1]
    n_tm = lax.axis_size("tm")
    pieces = (slots // 2, slots - slots // 2)
    packed = pack(pieces, vis_data[0], vis_weight[0], kernel_taps[0], offsets[0], block_patch, block_count)
    if n_tm > 8:
        cosine, sine = dft_tables()
        return rest_by_rows(add_blocks(None, [(packed, pieces)]), jnp.asarray(cosine), jnp.asarray(sine))
    acc, mine = by_gather(packed, pieces, n_tm)
    n_tile = lax.axis_size("tile")
    other = lax.ppermute(mine, "tile", [(i, n_tile - 1 - i) for i in range(n_tile)])
    row_tables, col_table = image_tables(n_tm)
    row_table = lax.dynamic_index_in_dim(jnp.asarray(row_tables), lax.axis_index("tm"), 0, keepdims=False)
    return make_image(acc, mine, other, row_table, jnp.asarray(col_table), G // n_tm)


def solution(mesh):
    return jax.shard_map(
        body,
        mesh=mesh,
        in_specs=(
            P(("grp", "tile"), "tm", None, None),
            P(("grp", "tile"), "tm", None),
            P(("grp", "tile"), "tm", None, None, None),
            P(("grp", "tile"), "tm", None, None),
            P(("grp", "tile"), "tm"),
            P(("grp", "tile"), "tm"),
        ),
        out_specs=P(None, None, ("grp", "tile"), "tm", None),
        check_vma=False,
    )
```

```python
import math

import jax
import jax.numpy as jnp
import ml_dtypes
import numpy as np
from jax import lax
from jax.experimental import pallas as pl
from jax.experimental.pallas import tpu as pltpu
from jax.sharding import PartitionSpec as P

G = 256
P_SIZE = 128
K = 8
B = 256
POLS = 2
NT_C = 2
PATCHES = 4 * NT_C
GRIDS = 1 + 2 * POLS
X_ROW = 2 * K
OFF_ROW = X_ROW + GRIDS
ID_ROW = OFF_ROW + 2
ROWS = ID_ROW + 1
COUNT_LANE = 64
UNROLL = 4
HIGH = lax.Precision.HIGHEST
VMEM = pl.BlockSpec(memory_space=pltpu.VMEM)
PARAMS = pltpu.CompilerParams(vmem_limit_bytes=20 * 1024 * 1024)


def pack_kernel(pieces, vis_hbm, weight_hbm, taps_hbm, offs_hbm, patch_ref, count_ref, *refs):
    outs, (vis_ref, weight_ref, taps_ref, offs_ref, sems) = refs[: len(pieces)], refs[len(pieces) :]
    pairs = ((offs_hbm, offs_ref), (taps_hbm, taps_ref), (weight_hbm, weight_ref), (vis_hbm, vis_ref))
    copies = [pltpu.make_async_copy(a, b, sems.at[i]) for i, (a, b) in enumerate(pairs)]
    for copy in copies:
        copy.start()
    lane = lax.broadcasted_iota(jnp.int32, (1, B), 1)
    places = []
    base = 0
    for out_ref, size in zip(outs, pieces):
        row = jnp.where(lane == COUNT_LANE, jnp.clip(count_ref[0, 0] - base, 0, size), 0)
        for j in range(size):
            row = jnp.where(lane == j, patch_ref[0, base + j], row)
            places.append((out_ref, j, base + j))
        row = row.astype(jnp.float32)
        for j in range(size):
            out_ref[j, ID_ROW:ROWS, :] = row
        base += size
    copies[0].wait()
    copies[1].wait()
    for out_ref, j, at in places:
        for side in range(2):
            off = offs_ref[at, side : side + 1, :]
            taps = taps_ref[at, side]
            for bit in range(3):
                moved = pltpu.roll(taps, 1 << bit, 0)
                turn = jnp.broadcast_to((off >> bit) & 1, taps.shape) == 1
                taps = jnp.where(turn, moved, taps)
            out_ref[j, side * K : (side + 1) * K, :] = taps
        out_ref[j, OFF_ROW:ID_ROW, :] = offs_ref[at].astype(jnp.float32)
    copies[2].wait()
    copies[3].wait()
    for out_ref, j, at in places:
        weight = weight_ref[at : at + 1, :]
        out_ref[j, X_ROW : X_ROW + 1, :] = weight
        out_ref[j, X_ROW + 1 : OFF_ROW, :] = weight * vis_ref[at]


def pack(pieces, vis, weight, taps, offs, patches, count):
    arrays = [pltpu.with_memory_space_constraint(a, pltpu.HBM) for a in (vis, weight, taps, offs)]
    smem = pl.BlockSpec(memory_space=pltpu.SMEM)
    return pl.pallas_call(
        lambda *refs: pack_kernel(pieces, *refs),
        out_shape=[jax.ShapeDtypeStruct((size, ROWS, B), jnp.float32) for size in pieces],
        in_specs=[pl.BlockSpec(memory_space=pltpu.HBM)] * 4 + [smem] * 2,
        out_specs=[VMEM] * len(pieces),
        scratch_shapes=[pltpu.VMEM(a.shape, a.dtype) for a in arrays] + [pltpu.SemaphoreType.DMA((4,))],
        compiler_params=PARAMS,
        name="pack",
    )(*arrays, patches, count)


def spread(off):
    row = lax.broadcasted_iota(jnp.int32, (16, B), 0)
    gap = off.astype(jnp.int32) - row
    step = (gap + 15) >> 4
    inside = (step << 4) - gap < K
    return jnp.where(inside, step, -1).astype(jnp.float32).astype(jnp.bfloat16)


def block_factors(block, live):
    rows_u = jnp.concatenate([block[0:K]] * 2, axis=0)
    rows_v = jnp.concatenate([block[K : 2 * K]] * 2, axis=0)
    step_u = spread(block[OFF_ROW : OFF_ROW + 1])
    step_v = spread(block[OFF_ROW + 1 : OFF_ROW + 2])
    if live is not None:
        rows_v = jnp.where(live, rows_v, 0.0)
    rows_v = rows_v.astype(jnp.bfloat16)
    zero = jnp.zeros((16, B), jnp.bfloat16)
    steps = P_SIZE // 16
    right = jnp.concatenate([jnp.where(step_v == s, rows_v, zero) for s in range(steps)], axis=0)
    hits = [step_u == s for s in range(steps)]
    left = []
    for e in range(GRIDS):
        product = (rows_u * block[X_ROW + e : X_ROW + e + 1]).astype(jnp.bfloat16)
        left += [jnp.where(hit, product, zero) for hit in hits]
    return jnp.concatenate(left, axis=0), right


def add_some(buf_ref, ids_ref, acc_ref, first, count):
    waiting = None
    for i in range(UNROLL):
        j = first if i == 0 else jnp.minimum(first + i, buf_ref.shape[0] - 1)
        left, right = block_factors(buf_ref[j], None if i == 0 else first + i < count)
        patch = lax.dot_general(
            left, right, (((1,), (1,)), ((), ())), preferred_element_type=jnp.float32
        )
        if waiting is not None:
            acc_ref[waiting[0]] += waiting[1]
        waiting = ids_ref[ID_ROW % 8, j].astype(jnp.int32), patch
    acc_ref[waiting[0]] += waiting[1]


def grid_kernel(n, first, last, *refs):
    bufs = refs[:n]
    acc_ref = refs[n] if first else refs[n + 1]
    ids, sems = refs[-2:]
    copies = []
    for i, buf_ref in enumerate(bufs):
        from_rows = buf_ref.at[0, 8 * (ID_ROW // 8) : ROWS, 0:128]
        copies.append(pltpu.make_async_copy(from_rows, ids.at[i], sems.at[i]))
        copies[-1].start()
    if first:
        acc_ref[...] = jnp.zeros_like(acc_ref)
    for i, buf_ref in enumerate(bufs):
        copies[i].wait()
        ids_ref = ids.at[i]
        count = ids_ref[ID_ROW % 8, COUNT_LANE].astype(jnp.int32)

        def some(step, _, buf_ref=buf_ref, ids_ref=ids_ref, count=count):
            add_some(buf_ref, ids_ref, acc_ref, UNROLL * step, count)
            return 0

        lax.fori_loop(0, (count + UNROLL - 1) // UNROLL, some, 0)
    if last:
        sums_ref = refs[-3]
        dens = acc_ref[:, :P_SIZE, :]
        for i, value in enumerate((dens, dens * dens)):
            part = jnp.sum(value.reshape(-1, 8, P_SIZE), axis=0)
            part = jnp.sum(jnp.sum(part, axis=0, keepdims=True), axis=1, keepdims=True)
            sums_ref[8 * i : 8 * i + 8, :] = jnp.broadcast_to(part, (8, P_SIZE))


def add_blocks(acc, bufs, last=False):
    first = acc is None
    n = len(bufs)
    slots = sum(buf.shape[0] for buf in bufs)
    out_shape = [jax.ShapeDtypeStruct((PATCHES, GRIDS * P_SIZE, P_SIZE), jnp.float32)]
    if last:
        out_shape.append(jax.ShapeDtypeStruct((16, P_SIZE), jnp.float32))
    args = list(bufs) + ([] if first else [acc])
    flops = 8 * slots * GRIDS * P_SIZE * P_SIZE * B
    out = pl.pallas_call(
        lambda *refs: grid_kernel(n, first, last, *refs),
        out_shape=out_shape,
        in_specs=[VMEM] * len(args),
        out_specs=[VMEM] * len(out_shape),
        scratch_shapes=[pltpu.SMEM((n, 8, 128), jnp.float32), pltpu.SemaphoreType.DMA((n,))],
        input_output_aliases={} if first else {n: 0},
        compiler_params=PARAMS,
        cost_estimate=pl.CostEstimate(flops=flops, bytes_accessed=1 << 20, transcendentals=0),
        name="grid",
    )(*args)
    return tuple(out) if last else out[0]


def two_parts(value):
    high = value.astype(jnp.bfloat16)
    return high, (value - high.astype(jnp.float32)).astype(jnp.bfloat16)


def dot_parts(value, table_ref):
    width = table_ref.shape[1] // 2
    high, low = two_parts(value)
    both = jnp.dot(high, table_ref[...], preferred_element_type=jnp.float32)
    return both[:, :width] + both[:, width:] + jnp.dot(low, table_ref[:, :width], preferred_element_type=jnp.float32)


def image_kernel(acc_ref, mine_ref, other_ref, row_ref, col_ref, out_ref):
    s1 = mine_ref[0:1, :] + other_ref[0:1, :]
    s2 = mine_ref[8:9, :] + other_ref[8:9, :]
    factor = 2.5 * s1 / s2
    width = out_ref.shape[3]
    flipped = []
    for t in range(NT_C):
        strips = [[] for _ in range(POLS)]
        for pr in range(2):
            tiles = [acc_ref.at[4 * t + 2 * pr + pc] for pc in range(2)]
            weight = [1.0 / (1.0 + factor * tile[:P_SIZE]) for tile in tiles]
            for pol in range(POLS):
                parts = []
                for e in (1 + 2 * pol, 2 + 2 * pol):
                    for pc in range(2):
                        parts.append(tiles[pc][e * P_SIZE : (e + 1) * P_SIZE] * weight[pc])
                strips[pol].append(jnp.concatenate(parts, axis=1))
        for pol in range(POLS):
            flipped.append(dot_parts(jnp.concatenate(strips[pol], axis=0), row_ref).T)
    done = dot_parts(jnp.concatenate(flipped, axis=0), col_ref)
    for t in range(NT_C):
        for pol in range(POLS):
            at = (t * POLS + pol) * 2 * width
            real, imag = done[at : at + width], done[at + width : at + 2 * width]
            out_ref[pol, 0, t] = real[:, :G] + imag[:, G:]
            out_ref[pol, 1, t] = imag[:, :G] - real[:, G:]


def make_image(acc, mine, other, row_table, col_table, width):
    return pl.pallas_call(
        image_kernel,
        out_shape=jax.ShapeDtypeStruct((POLS, 2, NT_C, width, G), jnp.float32),
        in_specs=[VMEM] * 5,
        out_specs=VMEM,
        compiler_params=PARAMS,
        name="image",
    )(acc, mine, other, row_table, col_table)


def dft_tables():
    index = np.arange(G)
    phase = (index[:, None] * index[None, :] % G) * (2.0 * math.pi / G)
    return np.cos(phase).astype(np.float32), np.sin(phase).astype(np.float32)


def np_parts(table):
    high = table.astype(ml_dtypes.bfloat16)
    low = (table - high.astype(np.float32)).astype(ml_dtypes.bfloat16)
    return np.concatenate([high, low], axis=-1)


def image_tables(n_tm):
    cosine, sine = dft_tables()
    rows = []
    for cos_part, sin_part in zip(np.split(cosine, n_tm, axis=1), np.split(sine, n_tm, axis=1)):
        rows.append(np_parts(np.block([[cos_part, -sin_part], [sin_part, cos_part]])))
    return np.stack(rows), np_parts(np.concatenate([cosine, sine], axis=1) / G)


def by_gather(packed, n_tm):
    order = list(range(0, n_tm, 2)) + list(range(1, n_tm, 2))[::-1]
    up = [(order[i], order[(i + 1) % n_tm]) for i in range(n_tm)]
    down = [(b, a) for a, b in up]
    arrived = [list(packed)]
    held = [[a, a] for a in packed]
    acc = None
    for step in range(1, n_tm // 2 + 1):
        far = step == n_tm // 2
        for i, pair in enumerate(held):
            if not (far and i == 1):
                pair[0] = lax.ppermute(pair[0], "tm", up)
            if not (far and i == 0):
                pair[1] = lax.ppermute(pair[1], "tm", down)
        for group in arrived:
            acc = add_blocks(acc, group)
        arrived = [[held[0][0], held[1][1]]] if far else [list(pair) for pair in held]
    return add_blocks(acc, arrived[0], last=True)


def rest_by_rows(acc, cosine, sine):
    grid = acc.reshape(NT_C, 2, 2, GRIDS, P_SIZE, P_SIZE)
    flat = jnp.transpose(grid, (3, 0, 1, 4, 2, 5)).reshape(GRIDS, NT_C * G, G)
    owned = lax.psum_scatter(flat, "tm", scatter_dimension=1, tiled=True)
    dens = owned[0]
    totals = lax.psum((jnp.sum(dens), jnp.sum(dens * dens)), ("tm", "tile"))
    factor = 2.5 * totals[0] / totals[1]
    weighted = owned[1:] / (1.0 + factor * dens[None])
    weighted = weighted.reshape(POLS, 2, dens.shape[0], G)
    real, imag = weighted[:, 0], weighted[:, 1]

    def rows(a, b):
        return jnp.einsum("prj,jn->prn", a, b, precision=HIGH)

    done = jnp.stack([rows(real, cosine) + rows(imag, sine), rows(imag, cosine) - rows(real, sine)], axis=1)
    width = G // lax.axis_size("tm")
    every_row = lax.all_gather(done, "tm", axis=2, tiled=True)
    columns = lax.dynamic_slice_in_dim(every_row, lax.axis_index("tm") * width, width, 3)
    columns = columns.reshape(POLS, 2, NT_C, G, width)
    real, imag = columns[:, 0], columns[:, 1]

    def cols(a, b):
        return jnp.einsum("mi,ptic->ptcm", a, b, precision=HIGH)

    out = jnp.stack([cols(cosine, real) + cols(sine, imag), cols(cosine, imag) - cols(sine, real)], axis=1)
    return out / G


def body(vis_data, vis_weight, kernel_taps, offsets, block_patch, block_count):
    slots = vis_weight.shape[1]
    n_tm = lax.axis_size("tm")
    pieces = (slots // 2, slots - slots // 2)
    packed = pack(pieces, vis_data[0], vis_weight[0], kernel_taps[0], offsets[0], block_patch, block_count)
    if n_tm > 8:
        cosine, sine = dft_tables()
        return rest_by_rows(add_blocks(None, packed), jnp.asarray(cosine), jnp.asarray(sine))
    acc, mine = by_gather(packed, n_tm)
    n_tile = lax.axis_size("tile")
    other = lax.ppermute(mine, "tile", [(i, n_tile - 1 - i) for i in range(n_tile)])
    row_tables, col_table = image_tables(n_tm)
    row_table = lax.dynamic_index_in_dim(jnp.asarray(row_tables), lax.axis_index("tm"), 0, keepdims=False)
    return make_image(acc, mine, other, row_table, jnp.asarray(col_table), G // n_tm)


def solution(mesh):
    return jax.shard_map(
        body,
        mesh=mesh,
        in_specs=(
            P(("grp", "tile"), "tm", None, None),
            P(("grp", "tile"), "tm", None),
            P(("grp", "tile"), "tm", None, None, None),
            P(("grp", "tile"), "tm", None, None),
            P(("grp", "tile"), "tm"),
            P(("grp", "tile"), "tm"),
        ),
        out_specs=P(None, None, ("grp", "tile"), "tm", None),
        check_vma=False,
    )
```

```python
import math

import jax
import jax.numpy as jnp
import ml_dtypes
import numpy as np
from jax import lax
from jax.experimental import pallas as pl
from jax.experimental.pallas import tpu as pltpu
from jax.sharding import PartitionSpec as P

G = 256
P_SIZE = 128
K = 8
B = 256
POLS = 2
NT_C = 2
PATCHES = 4 * NT_C
GRIDS = 1 + 2 * POLS
X_ROW = 2 * K
OFF_ROW = X_ROW + GRIDS
ID_ROW = OFF_ROW + 2
ROWS = ID_ROW + 1
COUNT_LANE = 128
UNROLL = 4
HIGH = lax.Precision.HIGHEST
VMEM = pl.BlockSpec(memory_space=pltpu.VMEM)
PARAMS = pltpu.CompilerParams(vmem_limit_bytes=20 * 1024 * 1024)


def pack_kernel(pieces, vis_hbm, weight_hbm, taps_hbm, offs_hbm, patch_hbm, count_ref, *refs):
    outs, scratch = refs[: len(pieces)], refs[len(pieces) :]
    vis_ref, weight_ref, taps_ref, offs_ref, patch_ref, sems = scratch
    pairs = (
        (offs_hbm, offs_ref),
        (taps_hbm, taps_ref),
        (weight_hbm, weight_ref),
        (vis_hbm, vis_ref),
        (patch_hbm, patch_ref),
    )
    copies = [pltpu.make_async_copy(a, b, sems.at[i]) for i, (a, b) in enumerate(pairs)]
    for copy in copies:
        copy.start()
    places = []
    base = 0
    for out_ref, size in zip(outs, pieces):
        places += [(out_ref, j, base + j) for j in range(size)]
        base += size
    copies[0].wait()
    copies[1].wait()
    for out_ref, j, at in places:
        for side in range(2):
            off = offs_ref[at, side : side + 1, :]
            taps = taps_ref[at, side]
            for bit in range(3):
                moved = pltpu.roll(taps, 1 << bit, 0)
                turn = jnp.broadcast_to((off >> bit) & 1, taps.shape) == 1
                taps = jnp.where(turn, moved, taps)
            out_ref[j, side * K : (side + 1) * K, :] = taps
        out_ref[j, OFF_ROW:ID_ROW, :] = offs_ref[at].astype(jnp.float32)
    copies[2].wait()
    copies[3].wait()
    for out_ref, j, at in places:
        weight = weight_ref[at : at + 1, :]
        out_ref[j, X_ROW : X_ROW + 1, :] = weight
        out_ref[j, X_ROW + 1 : OFF_ROW, :] = weight * vis_ref[at]
    copies[4].wait()
    lane = lax.broadcasted_iota(jnp.int32, (1, B), 1)
    for out_ref, j, at in places:
        live = jnp.clip(count_ref[0, 0] - (at - j), 0, out_ref.shape[0])
        row = jnp.where(lane < COUNT_LANE, patch_ref[0, at], live)
        out_ref[j, ID_ROW:ROWS, :] = row.astype(jnp.float32)


def pack(pieces, vis, weight, taps, offs, patches, count):
    arrays = (vis, weight, taps, offs, patches)
    spaces = [pltpu.VMEM] * 4 + [pltpu.SMEM]
    hbm, smem = pl.BlockSpec(memory_space=pltpu.HBM), pl.BlockSpec(memory_space=pltpu.SMEM)
    return pl.pallas_call(
        lambda *refs: pack_kernel(pieces, *refs),
        out_shape=[jax.ShapeDtypeStruct((size, ROWS, B), jnp.float32) for size in pieces],
        in_specs=[hbm] * 5 + [smem],
        out_specs=[VMEM] * len(pieces),
        scratch_shapes=[space(a.shape, a.dtype) for space, a in zip(spaces, arrays)] + [pltpu.SemaphoreType.DMA((5,))],
        compiler_params=PARAMS,
        name="pack",
    )(*[pltpu.with_memory_space_constraint(a, pltpu.HBM) for a in arrays], count)


def spread(off):
    row = lax.broadcasted_iota(jnp.int32, (16, B), 0)
    gap = off.astype(jnp.int32) - row
    step = (gap + 15) >> 4
    inside = (step << 4) - gap < K
    return jnp.where(inside, step, -1).astype(jnp.float32).astype(jnp.bfloat16)


def block_factors(block, live):
    rows_u = jnp.concatenate([block[0:K]] * 2, axis=0)
    rows_v = jnp.concatenate([block[K : 2 * K]] * 2, axis=0)
    step_u = spread(block[OFF_ROW : OFF_ROW + 1])
    step_v = spread(block[OFF_ROW + 1 : OFF_ROW + 2])
    if live is not None:
        rows_v = jnp.where(live, rows_v, 0.0)
    rows_v = rows_v.astype(jnp.bfloat16)
    zero = jnp.zeros((16, B), jnp.bfloat16)
    steps = P_SIZE // 16
    right = jnp.concatenate([jnp.where(step_v == s, rows_v, zero) for s in range(steps)], axis=0)
    hits = [step_u == s for s in range(steps)]
    left = []
    for e in range(GRIDS):
        product = (rows_u * block[X_ROW + e : X_ROW + e + 1]).astype(jnp.bfloat16)
        left += [jnp.where(hit, product, zero) for hit in hits]
    return jnp.concatenate(left, axis=0), right


def add_some(buf_ref, acc_ref, first, count):
    waiting = None
    for i in range(UNROLL):
        j = first if i == 0 else jnp.minimum(first + i, buf_ref.shape[0] - 1)
        block = buf_ref[j]
        left, right = block_factors(block, None if i == 0 else first + i < count)
        patch = lax.dot_general(
            left, right, (((1,), (1,)), ((), ())), preferred_element_type=jnp.float32
        )
        if waiting is not None:
            acc_ref[waiting[0]] += waiting[1]
        waiting = block[ID_ROW:ROWS, 0:1][0, 0].astype(jnp.int32), patch
    acc_ref[waiting[0]] += waiting[1]


def grid_kernel(n, first, last, *refs):
    bufs = refs[:n]
    acc_ref = refs[n] if first else refs[n + 1]
    if first:
        acc_ref[...] = jnp.zeros_like(acc_ref)
    for buf_ref in bufs:
        count = buf_ref[0, ID_ROW:ROWS, COUNT_LANE : COUNT_LANE + 1][0, 0].astype(jnp.int32)

        def some(step, _, buf_ref=buf_ref, count=count):
            add_some(buf_ref, acc_ref, UNROLL * step, count)
            return 0

        lax.fori_loop(0, (count + UNROLL - 1) // UNROLL, some, 0)
    if last:
        sums_ref = refs[-1]
        dens = acc_ref[:, :P_SIZE, :]
        for i, value in enumerate((dens, dens * dens)):
            part = jnp.sum(value.reshape(-1, 8, P_SIZE), axis=0)
            part = jnp.sum(jnp.sum(part, axis=0, keepdims=True), axis=1, keepdims=True)
            sums_ref[8 * i : 8 * i + 8, :] = jnp.broadcast_to(part, (8, P_SIZE))


def add_blocks(acc, bufs, last=False):
    first = acc is None
    n = len(bufs)
    slots = sum(buf.shape[0] for buf in bufs)
    out_shape = [jax.ShapeDtypeStruct((PATCHES, GRIDS * P_SIZE, P_SIZE), jnp.float32)]
    if last:
        out_shape.append(jax.ShapeDtypeStruct((16, P_SIZE), jnp.float32))
    args = list(bufs) + ([] if first else [acc])
    flops = 2 * slots * GRIDS * P_SIZE * P_SIZE * B
    out = pl.pallas_call(
        lambda *refs: grid_kernel(n, first, last, *refs),
        out_shape=out_shape,
        in_specs=[VMEM] * len(args),
        out_specs=[VMEM] * len(out_shape),
        input_output_aliases={} if first else {n: 0},
        compiler_params=PARAMS,
        cost_estimate=pl.CostEstimate(flops=flops, bytes_accessed=slots * ROWS * B, transcendentals=0),
        name="grid",
    )(*args)
    return tuple(out) if last else out[0]


def two_parts(value):
    high = value.astype(jnp.bfloat16)
    return high, (value - high.astype(jnp.float32)).astype(jnp.bfloat16)


def dot_parts(value, table_ref):
    width = table_ref.shape[1] // 2
    high, low = two_parts(value)
    both = jnp.dot(high, table_ref[...], preferred_element_type=jnp.float32)
    return both[:, :width] + both[:, width:] + jnp.dot(low, table_ref[:, :width], preferred_element_type=jnp.float32)


def image_kernel(acc_ref, mine_ref, other_ref, row_ref, col_ref, out_ref):
    s1 = mine_ref[0:1, :] + other_ref[0:1, :]
    s2 = mine_ref[8:9, :] + other_ref[8:9, :]
    factor = 2.5 * s1 / s2
    width = out_ref.shape[3]
    flipped = []
    for t in range(NT_C):
        strips = [[] for _ in range(POLS)]
        for pr in range(2):
            tiles = [acc_ref.at[4 * t + 2 * pr + pc] for pc in range(2)]
            weight = [1.0 / (1.0 + factor * tile[:P_SIZE]) for tile in tiles]
            for pol in range(POLS):
                parts = []
                for e in (1 + 2 * pol, 2 + 2 * pol):
                    for pc in range(2):
                        parts.append(tiles[pc][e * P_SIZE : (e + 1) * P_SIZE] * weight[pc])
                strips[pol].append(jnp.concatenate(parts, axis=1))
        for pol in range(POLS):
            flipped.append(dot_parts(jnp.concatenate(strips[pol], axis=0), row_ref).T)
    done = dot_parts(jnp.concatenate(flipped, axis=0), col_ref)
    for t in range(NT_C):
        for pol in range(POLS):
            at = (t * POLS + pol) * 2 * width
            real, imag = done[at : at + width], done[at + width : at + 2 * width]
            out_ref[pol, 0, t] = real[:, :G] + imag[:, G:]
            out_ref[pol, 1, t] = imag[:, :G] - real[:, G:]


def make_image(acc, mine, other, row_table, col_table, width):
    return pl.pallas_call(
        image_kernel,
        out_shape=jax.ShapeDtypeStruct((POLS, 2, NT_C, width, G), jnp.float32),
        in_specs=[VMEM] * 5,
        out_specs=VMEM,
        compiler_params=PARAMS,
        name="image",
    )(acc, mine, other, row_table, col_table)


def dft_tables():
    index = np.arange(G)
    phase = (index[:, None] * index[None, :] % G) * (2.0 * math.pi / G)
    return np.cos(phase).astype(np.float32), np.sin(phase).astype(np.float32)


def np_parts(table):
    high = table.astype(ml_dtypes.bfloat16)
    low = (table - high.astype(np.float32)).astype(ml_dtypes.bfloat16)
    return np.concatenate([high, low], axis=-1)


def image_tables(n_tm):
    cosine, sine = dft_tables()
    rows = []
    for cos_part, sin_part in zip(np.split(cosine, n_tm, axis=1), np.split(sine, n_tm, axis=1)):
        rows.append(np_parts(np.block([[cos_part, -sin_part], [sin_part, cos_part]])))
    return np.stack(rows), np_parts(np.concatenate([cosine, sine], axis=1) / G)


def by_gather(packed, n_tm):
    order = list(range(0, n_tm, 2)) + list(range(1, n_tm, 2))[::-1]
    up = [(order[i], order[(i + 1) % n_tm]) for i in range(n_tm)]
    down = [(b, a) for a, b in up]
    acc = None
    held = [[a, a] for a in packed]
    arrived = list(held)
    for step in range(1, n_tm // 2 + 1):
        far = step == n_tm // 2
        for i, pair in enumerate(arrived):
            if step > 1 and i > 0:
                acc, *pair = lax.optimization_barrier((acc, *pair))
            sent = list(pair)
            if not (far and i == 1):
                sent[0] = lax.ppermute(pair[0], "tm", up)
            if not (far and i == 0):
                sent[1] = lax.ppermute(pair[1], "tm", down)
            if step > 1:
                acc = add_blocks(acc, pair)
            held[i] = sent
        if step == 1:
            acc = add_blocks(None, packed)
        arrived = list(held)
    acc = add_blocks(acc, [held[0][0]])
    return add_blocks(acc, [held[1][1]], last=True)


def rest_by_rows(acc, cosine, sine):
    grid = acc.reshape(NT_C, 2, 2, GRIDS, P_SIZE, P_SIZE)
    flat = jnp.transpose(grid, (3, 0, 1, 4, 2, 5)).reshape(GRIDS, NT_C * G, G)
    owned = lax.psum_scatter(flat, "tm", scatter_dimension=1, tiled=True)
    dens = owned[0]
    totals = lax.psum((jnp.sum(dens), jnp.sum(dens * dens)), ("tm", "tile"))
    factor = 2.5 * totals[0] / totals[1]
    weighted = owned[1:] / (1.0 + factor * dens[None])
    weighted = weighted.reshape(POLS, 2, dens.shape[0], G)
    real, imag = weighted[:, 0], weighted[:, 1]

    def rows(a, b):
        return jnp.einsum("prj,jn->prn", a, b, precision=HIGH)

    done = jnp.stack([rows(real, cosine) + rows(imag, sine), rows(imag, cosine) - rows(real, sine)], axis=1)
    width = G // lax.axis_size("tm")
    every_row = lax.all_gather(done, "tm", axis=2, tiled=True)
    columns = lax.dynamic_slice_in_dim(every_row, lax.axis_index("tm") * width, width, 3)
    columns = columns.reshape(POLS, 2, NT_C, G, width)
    real, imag = columns[:, 0], columns[:, 1]

    def cols(a, b):
        return jnp.einsum("mi,ptic->ptcm", a, b, precision=HIGH)

    out = jnp.stack([cols(cosine, real) + cols(sine, imag), cols(cosine, imag) - cols(sine, real)], axis=1)
    return out / G


def body(vis_data, vis_weight, kernel_taps, offsets, block_patch, block_count):
    slots = vis_weight.shape[1]
    n_tm = lax.axis_size("tm")
    pieces = (slots // 2, slots - slots // 2)
    packed = pack(pieces, vis_data[0], vis_weight[0], kernel_taps[0], offsets[0], block_patch, block_count)
    if n_tm > 8:
        cosine, sine = dft_tables()
        return rest_by_rows(add_blocks(None, packed), jnp.asarray(cosine), jnp.asarray(sine))
    acc, mine = by_gather(packed, n_tm)
    n_tile = lax.axis_size("tile")
    other = lax.ppermute(mine, "tile", [(i, n_tile - 1 - i) for i in range(n_tile)])
    row_tables, col_table = image_tables(n_tm)
    row_table = lax.dynamic_index_in_dim(jnp.asarray(row_tables), lax.axis_index("tm"), 0, keepdims=False)
    return make_image(acc, mine, other, row_table, jnp.asarray(col_table), G // n_tm)


def solution(mesh):
    return jax.shard_map(
        body,
        mesh=mesh,
        in_specs=(
            P(("grp", "tile"), "tm", None, None),
            P(("grp", "tile"), "tm", None),
            P(("grp", "tile"), "tm", None, None, None),
            P(("grp", "tile"), "tm", None, None),
            P(("grp", "tile"), "tm"),
            P(("grp", "tile"), "tm"),
        ),
        out_specs=P(None, None, ("grp", "tile"), "tm", None),
        check_vma=False,
    )
```

```python
import math

import jax
import jax.numpy as jnp
import ml_dtypes
import numpy as np
from jax import lax
from jax.experimental import pallas as pl
from jax.experimental.pallas import tpu as pltpu
from jax.sharding import PartitionSpec as P

G = 256
P_SIZE = 128
K = 8
B = 256
POLS = 2
NT_C = 2
PATCHES = 4 * NT_C
GRIDS = 1 + 2 * POLS
X_ROW = 2 * K
OFF_ROW = X_ROW + GRIDS
ID_ROW = OFF_ROW + 2
ROWS = ID_ROW + 1
COUNT_LANE = 128
UNROLL = 4
HIGH = lax.Precision.HIGHEST
VMEM = pl.BlockSpec(memory_space=pltpu.VMEM)
PARAMS = pltpu.CompilerParams(vmem_limit_bytes=20 * 1024 * 1024)


def pack_kernel(pieces, vis_hbm, weight_hbm, taps_hbm, offs_hbm, patch_hbm, count_ref, *refs):
    outs, scratch = refs[: len(pieces)], refs[len(pieces) :]
    vis_ref, weight_ref, taps_ref, offs_ref, patch_ref, sems = scratch
    pairs = (
        (offs_hbm, offs_ref),
        (taps_hbm, taps_ref),
        (weight_hbm, weight_ref),
        (vis_hbm, vis_ref),
        (patch_hbm, patch_ref),
    )
    copies = [pltpu.make_async_copy(a, b, sems.at[i]) for i, (a, b) in enumerate(pairs)]
    for copy in copies:
        copy.start()
    places = []
    base = 0
    for out_ref, size in zip(outs, pieces):
        places += [(out_ref, j, base + j) for j in range(size)]
        base += size
    copies[0].wait()
    copies[1].wait()
    for out_ref, j, at in places:
        for side in range(2):
            off = offs_ref[at, side : side + 1, :]
            taps = taps_ref[at, side]
            for bit in range(3):
                moved = pltpu.roll(taps, 1 << bit, 0)
                turn = jnp.broadcast_to((off >> bit) & 1, taps.shape) == 1
                taps = jnp.where(turn, moved, taps)
            out_ref[j, side * K : (side + 1) * K, :] = taps
        out_ref[j, OFF_ROW:ID_ROW, :] = offs_ref[at].astype(jnp.float32)
    copies[2].wait()
    copies[3].wait()
    for out_ref, j, at in places:
        weight = weight_ref[at : at + 1, :]
        out_ref[j, X_ROW : X_ROW + 1, :] = weight
        out_ref[j, X_ROW + 1 : OFF_ROW, :] = weight * vis_ref[at]
    copies[4].wait()
    lane = lax.broadcasted_iota(jnp.int32, (1, B), 1)
    for out_ref, j, at in places:
        live = jnp.clip(count_ref[0, 0] - (at - j), 0, out_ref.shape[0])
        row = jnp.where(lane < COUNT_LANE, patch_ref[0, at], live)
        out_ref[j, ID_ROW:ROWS, :] = row.astype(jnp.float32)


def pack(pieces, vis, weight, taps, offs, patches, count):
    arrays = (vis, weight, taps, offs, patches)
    spaces = [pltpu.VMEM] * 4 + [pltpu.SMEM]
    hbm, smem = pl.BlockSpec(memory_space=pltpu.HBM), pl.BlockSpec(memory_space=pltpu.SMEM)
    return pl.pallas_call(
        lambda *refs: pack_kernel(pieces, *refs),
        out_shape=[jax.ShapeDtypeStruct((size, ROWS, B), jnp.float32) for size in pieces],
        in_specs=[hbm] * 5 + [smem],
        out_specs=[VMEM] * len(pieces),
        scratch_shapes=[space(a.shape, a.dtype) for space, a in zip(spaces, arrays)] + [pltpu.SemaphoreType.DMA((5,))],
        compiler_params=PARAMS,
        name="pack",
    )(*[pltpu.with_memory_space_constraint(a, pltpu.HBM) for a in arrays], count)


def spread(off):
    row = lax.broadcasted_iota(jnp.int32, (16, B), 0)
    gap = off.astype(jnp.int32) - row
    step = (gap + 15) >> 4
    inside = (step << 4) - gap < K
    return jnp.where(inside, step, -1).astype(jnp.float32).astype(jnp.bfloat16)


def block_factors(block, live):
    rows_u = jnp.concatenate([block[0:K]] * 2, axis=0)
    rows_v = jnp.concatenate([block[K : 2 * K]] * 2, axis=0)
    step_u = spread(block[OFF_ROW : OFF_ROW + 1])
    step_v = spread(block[OFF_ROW + 1 : OFF_ROW + 2])
    if live is not None:
        rows_v = jnp.where(live, rows_v, 0.0)
    rows_v = rows_v.astype(jnp.bfloat16)
    zero = jnp.zeros((16, B), jnp.bfloat16)
    steps = P_SIZE // 16
    right = jnp.concatenate([jnp.where(step_v == s, rows_v, zero) for s in range(steps)], axis=0)
    hits = [step_u == s for s in range(steps)]
    left = []
    for e in range(GRIDS):
        product = (rows_u * block[X_ROW + e : X_ROW + e + 1]).astype(jnp.bfloat16)
        left += [jnp.where(hit, product, zero) for hit in hits]
    return jnp.concatenate(left, axis=0), right


def add_some(buf_ref, acc_ref, first, count):
    waiting = None
    for i in range(UNROLL):
        j = first if i == 0 else jnp.minimum(first + i, buf_ref.shape[0] - 1)
        block = buf_ref[j]
        left, right = block_factors(block, None if i == 0 else first + i < count)
        patch = lax.dot_general(
            left, right, (((1,), (1,)), ((), ())), preferred_element_type=jnp.float32
        )
        if waiting is not None:
            acc_ref[waiting[0]] += waiting[1]
        waiting = block[ID_ROW:ROWS, 0:1][0, 0].astype(jnp.int32), patch
    acc_ref[waiting[0]] += waiting[1]


def grid_kernel(bases, first, last, *refs):
    n = len(bases)
    bufs = refs[:n]
    acc_ref = refs[n] if first else refs[n + 1]
    if first:
        acc_ref[...] = jnp.zeros_like(acc_ref)
    for buf_ref, base in zip(bufs, bases):
        count = buf_ref[0, ID_ROW:ROWS, COUNT_LANE : COUNT_LANE + 1][0, 0].astype(jnp.int32)
        count = jnp.clip(count - base, 0, buf_ref.shape[0])

        def some(step, _, buf_ref=buf_ref, count=count):
            add_some(buf_ref, acc_ref, UNROLL * step, count)
            return 0

        lax.fori_loop(0, (count + UNROLL - 1) // UNROLL, some, 0)
    if last:
        sums_ref = refs[-1]
        dens = acc_ref[:, :P_SIZE, :]
        for i, value in enumerate((dens, dens * dens)):
            part = jnp.sum(value.reshape(-1, 8, P_SIZE), axis=0)
            part = jnp.sum(jnp.sum(part, axis=0, keepdims=True), axis=1, keepdims=True)
            sums_ref[8 * i : 8 * i + 8, :] = jnp.broadcast_to(part, (8, P_SIZE))


def add_blocks(acc, bufs, bases=None, last=False):
    first = acc is None
    n = len(bufs)
    bases = bases or (0,) * n
    slots = sum(buf.shape[0] for buf in bufs)
    out_shape = [jax.ShapeDtypeStruct((PATCHES, GRIDS * P_SIZE, P_SIZE), jnp.float32)]
    if last:
        out_shape.append(jax.ShapeDtypeStruct((16, P_SIZE), jnp.float32))
    args = list(bufs) + ([] if first else [acc])
    flops = 2 * slots * GRIDS * P_SIZE * P_SIZE * B
    out = pl.pallas_call(
        lambda *refs: grid_kernel(bases, first, last, *refs),
        out_shape=out_shape,
        in_specs=[VMEM] * len(args),
        out_specs=[VMEM] * len(out_shape),
        input_output_aliases={} if first else {n: 0},
        compiler_params=PARAMS,
        cost_estimate=pl.CostEstimate(flops=flops, bytes_accessed=slots * ROWS * B, transcendentals=0),
        name="grid",
    )(*args)
    return tuple(out) if last else out[0]


def two_parts(value):
    high = value.astype(jnp.bfloat16)
    return high, (value - high.astype(jnp.float32)).astype(jnp.bfloat16)


def dot_parts(value, table_ref):
    width = table_ref.shape[1] // 2
    high, low = two_parts(value)
    both = jnp.dot(high, table_ref[...], preferred_element_type=jnp.float32)
    return both[:, :width] + both[:, width:] + jnp.dot(low, table_ref[:, :width], preferred_element_type=jnp.float32)


def image_kernel(acc_ref, mine_ref, other_ref, row_ref, col_ref, out_ref):
    s1 = mine_ref[0:1, :] + other_ref[0:1, :]
    s2 = mine_ref[8:9, :] + other_ref[8:9, :]
    factor = 2.5 * s1 / s2
    width = out_ref.shape[3]
    flipped = []
    for t in range(NT_C):
        strips = [[] for _ in range(POLS)]
        for pr in range(2):
            tiles = [acc_ref.at[4 * t + 2 * pr + pc] for pc in range(2)]
            weight = [1.0 / (1.0 + factor * tile[:P_SIZE]) for tile in tiles]
            for pol in range(POLS):
                parts = []
                for e in (1 + 2 * pol, 2 + 2 * pol):
                    for pc in range(2):
                        parts.append(tiles[pc][e * P_SIZE : (e + 1) * P_SIZE] * weight[pc])
                strips[pol].append(jnp.concatenate(parts, axis=1))
        for pol in range(POLS):
            flipped.append(dot_parts(jnp.concatenate(strips[pol], axis=0), row_ref).T)
    done = dot_parts(jnp.concatenate(flipped, axis=0), col_ref)
    for t in range(NT_C):
        for pol in range(POLS):
            at = (t * POLS + pol) * 2 * width
            real, imag = done[at : at + width], done[at + width : at + 2 * width]
            out_ref[pol, 0, t] = real[:, :G] + imag[:, G:]
            out_ref[pol, 1, t] = imag[:, :G] - real[:, G:]


def make_image(acc, mine, other, row_table, col_table, width):
    return pl.pallas_call(
        image_kernel,
        out_shape=jax.ShapeDtypeStruct((POLS, 2, NT_C, width, G), jnp.float32),
        in_specs=[VMEM] * 5,
        out_specs=VMEM,
        compiler_params=PARAMS,
        name="image",
    )(acc, mine, other, row_table, col_table)


def dft_tables():
    index = np.arange(G)
    phase = (index[:, None] * index[None, :] % G) * (2.0 * math.pi / G)
    return np.cos(phase).astype(np.float32), np.sin(phase).astype(np.float32)


def np_parts(table):
    high = table.astype(ml_dtypes.bfloat16)
    low = (table - high.astype(np.float32)).astype(ml_dtypes.bfloat16)
    return np.concatenate([high, low], axis=-1)


def image_tables(n_tm):
    cosine, sine = dft_tables()
    rows = []
    for cos_part, sin_part in zip(np.split(cosine, n_tm, axis=1), np.split(sine, n_tm, axis=1)):
        rows.append(np_parts(np.block([[cos_part, -sin_part], [sin_part, cos_part]])))
    return np.stack(rows), np_parts(np.concatenate([cosine, sine], axis=1) / G)


def by_gather(packed, n_tm):
    order = list(range(0, n_tm, 2)) + list(range(1, n_tm, 2))[::-1]
    up = [(order[i], order[(i + 1) % n_tm]) for i in range(n_tm)]
    down = [(b, a) for a, b in up]
    held = [[a, a] for a in packed]
    acc = None
    for step in range(1, n_tm // 2):
        for i, pair in enumerate(held):
            if step > 1 and i > 0:
                acc, *pair = lax.optimization_barrier((acc, *pair))
            held[i] = [lax.ppermute(pair[0], "tm", up), lax.ppermute(pair[1], "tm", down)]
            if step > 1:
                acc = add_blocks(acc, pair)
        if step == 1:
            acc = add_blocks(None, packed)
    far = []
    for i, pair in enumerate(held):
        if i > 0:
            acc, *pair = lax.optimization_barrier((acc, *pair))
        cut = pair[0].shape[0] // 2
        far.append([lax.ppermute(pair[0][:cut], "tm", up), lax.ppermute(pair[1][cut:], "tm", down)])
        acc = add_blocks(acc, pair)
    acc = add_blocks(acc, far[0], (0, cut))
    return add_blocks(acc, far[1], (0, cut), last=True)


def rest_by_rows(acc, cosine, sine):
    grid = acc.reshape(NT_C, 2, 2, GRIDS, P_SIZE, P_SIZE)
    flat = jnp.transpose(grid, (3, 0, 1, 4, 2, 5)).reshape(GRIDS, NT_C * G, G)
    owned = lax.psum_scatter(flat, "tm", scatter_dimension=1, tiled=True)
    dens = owned[0]
    totals = lax.psum((jnp.sum(dens), jnp.sum(dens * dens)), ("tm", "tile"))
    factor = 2.5 * totals[0] / totals[1]
    weighted = owned[1:] / (1.0 + factor * dens[None])
    weighted = weighted.reshape(POLS, 2, dens.shape[0], G)
    real, imag = weighted[:, 0], weighted[:, 1]

    def rows(a, b):
        return jnp.einsum("prj,jn->prn", a, b, precision=HIGH)

    done = jnp.stack([rows(real, cosine) + rows(imag, sine), rows(imag, cosine) - rows(real, sine)], axis=1)
    width = G // lax.axis_size("tm")
    every_row = lax.all_gather(done, "tm", axis=2, tiled=True)
    columns = lax.dynamic_slice_in_dim(every_row, lax.axis_index("tm") * width, width, 3)
    columns = columns.reshape(POLS, 2, NT_C, G, width)
    real, imag = columns[:, 0], columns[:, 1]

    def cols(a, b):
        return jnp.einsum("mi,ptic->ptcm", a, b, precision=HIGH)

    out = jnp.stack([cols(cosine, real) + cols(sine, imag), cols(cosine, imag) - cols(sine, real)], axis=1)
    return out / G


def body(vis_data, vis_weight, kernel_taps, offsets, block_patch, block_count):
    slots = vis_weight.shape[1]
    n_tm = lax.axis_size("tm")
    pieces = (slots // 2, slots - slots // 2)
    packed = pack(pieces, vis_data[0], vis_weight[0], kernel_taps[0], offsets[0], block_patch, block_count)
    if n_tm > 8:
        cosine, sine = dft_tables()
        return rest_by_rows(add_blocks(None, packed), jnp.asarray(cosine), jnp.asarray(sine))
    acc, mine = by_gather(packed, n_tm)
    n_tile = lax.axis_size("tile")
    other = lax.ppermute(mine, "tile", [(i, n_tile - 1 - i) for i in range(n_tile)])
    row_tables, col_table = image_tables(n_tm)
    row_table = lax.dynamic_index_in_dim(jnp.asarray(row_tables), lax.axis_index("tm"), 0, keepdims=False)
    return make_image(acc, mine, other, row_table, jnp.asarray(col_table), G // n_tm)


def solution(mesh):
    return jax.shard_map(
        body,
        mesh=mesh,
        in_specs=(
            P(("grp", "tile"), "tm", None, None),
            P(("grp", "tile"), "tm", None),
            P(("grp", "tile"), "tm", None, None, None),
            P(("grp", "tile"), "tm", None, None),
            P(("grp", "tile"), "tm"),
            P(("grp", "tile"), "tm"),
        ),
        out_specs=P(None, None, ("grp", "tile"), "tm", None),
        check_vma=False,
    )
```

```python
import math

import jax
import jax.numpy as jnp
import ml_dtypes
import numpy as np
from jax import lax
from jax.experimental import pallas as pl
from jax.experimental.pallas import tpu as pltpu
from jax.sharding import PartitionSpec as P

G = 256
P_SIZE = 128
K = 8
B = 256
POLS = 2
NT_C = 2
PATCHES = 4 * NT_C
GRIDS = 1 + 2 * POLS
X_ROW = 2 * K
OFF_ROW = X_ROW + GRIDS
ID_ROW = OFF_ROW + 2
ROWS = ID_ROW + 1
COUNT_LANE = 128
HIGH = lax.Precision.HIGHEST
VMEM = pl.BlockSpec(memory_space=pltpu.VMEM)
PARAMS = pltpu.CompilerParams(vmem_limit_bytes=20 * 1024 * 1024)


def pack_kernel(pieces, vis_hbm, weight_hbm, taps_hbm, offs_hbm, patch_hbm, count_ref, *refs):
    outs, scratch = refs[: len(pieces)], refs[len(pieces) :]
    vis_ref, weight_ref, taps_ref, offs_ref, patch_ref, sems = scratch
    pairs = (
        (offs_hbm, offs_ref),
        (taps_hbm, taps_ref),
        (weight_hbm, weight_ref),
        (vis_hbm, vis_ref),
        (patch_hbm, patch_ref),
    )
    copies = [pltpu.make_async_copy(a, b, sems.at[i]) for i, (a, b) in enumerate(pairs)]
    for copy in copies:
        copy.start()
    places = []
    base = 0
    for out_ref, size in zip(outs, pieces):
        places += [(out_ref, j, base + j) for j in range(size)]
        base += size
    copies[0].wait()
    copies[1].wait()
    for out_ref, j, at in places:
        for side in range(2):
            off = offs_ref[at, side : side + 1, :]
            taps = taps_ref[at, side]
            for bit in range(3):
                moved = pltpu.roll(taps, 1 << bit, 0)
                turn = jnp.broadcast_to((off >> bit) & 1, taps.shape) == 1
                taps = jnp.where(turn, moved, taps)
            out_ref[j, side * K : (side + 1) * K, :] = taps
        out_ref[j, OFF_ROW:ID_ROW, :] = offs_ref[at].astype(jnp.float32)
    copies[2].wait()
    copies[3].wait()
    for out_ref, j, at in places:
        weight = weight_ref[at : at + 1, :]
        out_ref[j, X_ROW : X_ROW + 1, :] = weight
        out_ref[j, X_ROW + 1 : OFF_ROW, :] = weight * vis_ref[at]
    copies[4].wait()
    lane = lax.broadcasted_iota(jnp.int32, (1, B), 1)
    for out_ref, j, at in places:
        live = jnp.clip(count_ref[0, 0] - (at - j), 0, out_ref.shape[0])
        row = jnp.where(lane < COUNT_LANE, patch_ref[0, at], live)
        out_ref[j, ID_ROW:ROWS, :] = row.astype(jnp.float32)


def pack(pieces, vis, weight, taps, offs, patches, count):
    arrays = (vis, weight, taps, offs, patches)
    spaces = [pltpu.VMEM] * 4 + [pltpu.SMEM]
    hbm, smem = pl.BlockSpec(memory_space=pltpu.HBM), pl.BlockSpec(memory_space=pltpu.SMEM)
    return pl.pallas_call(
        lambda *refs: pack_kernel(pieces, *refs),
        out_shape=[jax.ShapeDtypeStruct((size, ROWS, B), jnp.float32) for size in pieces],
        in_specs=[hbm] * 5 + [smem],
        out_specs=[VMEM] * len(pieces),
        scratch_shapes=[space(a.shape, a.dtype) for space, a in zip(spaces, arrays)] + [pltpu.SemaphoreType.DMA((5,))],
        compiler_params=PARAMS,
        name="pack",
    )(*[pltpu.with_memory_space_constraint(a, pltpu.HBM) for a in arrays], count)


def spread(off):
    row = lax.broadcasted_iota(jnp.int32, (16, B), 0)
    gap = off.astype(jnp.int32) - row
    step = (gap + 15) >> 4
    inside = (step << 4) - gap < K
    return jnp.where(inside, step, -1).astype(jnp.float32).astype(jnp.bfloat16)


def block_factors(block, live):
    rows_u = jnp.concatenate([block[0:K]] * 2, axis=0)
    rows_v = jnp.concatenate([block[K : 2 * K]] * 2, axis=0)
    step_u = spread(block[OFF_ROW : OFF_ROW + 1])
    step_v = spread(block[OFF_ROW + 1 : OFF_ROW + 2])
    if live is not None:
        rows_v = jnp.where(live, rows_v, 0.0)
    rows_v = rows_v.astype(jnp.bfloat16)
    zero = jnp.zeros((16, B), jnp.bfloat16)
    steps = P_SIZE // 16
    right = jnp.concatenate([jnp.where(step_v == s, rows_v, zero) for s in range(steps)], axis=0)
    hits = [step_u == s for s in range(steps)]
    left = []
    for e in range(GRIDS):
        product = (rows_u * block[X_ROW + e : X_ROW + e + 1]).astype(jnp.bfloat16)
        left += [jnp.where(hit, product, zero) for hit in hits]
    return jnp.concatenate(left, axis=0), right


def add_some(buf_ref, acc_ref, first, count, unroll):
    waiting = None
    for i in range(unroll):
        j = first if i == 0 else jnp.minimum(first + i, buf_ref.shape[0] - 1)
        block = buf_ref[j]
        left, right = block_factors(block, None if i == 0 else first + i < count)
        patch = lax.dot_general(
            left, right, (((1,), (1,)), ((), ())), preferred_element_type=jnp.float32
        )
        if waiting is not None:
            acc_ref[waiting[0]] += waiting[1]
        waiting = block[ID_ROW:ROWS, 0:1][0, 0].astype(jnp.int32), patch
    acc_ref[waiting[0]] += waiting[1]


def grid_kernel(n, first, last, *refs):
    bufs = refs[:n]
    acc_ref = refs[n] if first else refs[n + 1]
    if first:
        acc_ref[...] = jnp.zeros_like(acc_ref)
    for buf_ref in bufs:
        count = buf_ref[0, ID_ROW:ROWS, COUNT_LANE : COUNT_LANE + 1][0, 0].astype(jnp.int32)

        unroll = max(d for d in range(1, 6) if buf_ref.shape[0] % d == 0)

        def some(step, _, buf_ref=buf_ref, count=count, unroll=unroll):
            add_some(buf_ref, acc_ref, unroll * step, count, unroll)
            return 0

        lax.fori_loop(0, (count + unroll - 1) // unroll, some, 0)
    if last:
        sums_ref = refs[-1]
        dens = acc_ref[:, :P_SIZE, :]
        for i, value in enumerate((dens, dens * dens)):
            part = jnp.sum(value.reshape(-1, 8, P_SIZE), axis=0)
            part = jnp.sum(jnp.sum(part, axis=0, keepdims=True), axis=1, keepdims=True)
            sums_ref[8 * i : 8 * i + 8, :] = jnp.broadcast_to(part, (8, P_SIZE))


def add_blocks(acc, bufs, last=False):
    first = acc is None
    n = len(bufs)
    slots = sum(buf.shape[0] for buf in bufs)
    out_shape = [jax.ShapeDtypeStruct((PATCHES, GRIDS * P_SIZE, P_SIZE), jnp.float32)]
    if last:
        out_shape.append(jax.ShapeDtypeStruct((16, P_SIZE), jnp.float32))
    args = list(bufs) + ([] if first else [acc])
    flops = 4 * slots * GRIDS * P_SIZE * P_SIZE * B
    out = pl.pallas_call(
        lambda *refs: grid_kernel(n, first, last, *refs),
        out_shape=out_shape,
        in_specs=[VMEM] * len(args),
        out_specs=[VMEM] * len(out_shape),
        input_output_aliases={} if first else {n: 0},
        compiler_params=PARAMS,
        cost_estimate=pl.CostEstimate(flops=flops, bytes_accessed=slots * ROWS * B, transcendentals=0),
        name="grid",
    )(*args)
    return tuple(out) if last else out[0]


def two_parts(value):
    high = value.astype(jnp.bfloat16)
    return high, (value - high.astype(jnp.float32)).astype(jnp.bfloat16)


def dot_parts(value, table_ref):
    width = table_ref.shape[1] // 2
    high, low = two_parts(value)
    both = jnp.dot(high, table_ref[...], preferred_element_type=jnp.float32)
    return both[:, :width] + both[:, width:] + jnp.dot(low, table_ref[:, :width], preferred_element_type=jnp.float32)


def image_kernel(acc_ref, mine_ref, other_ref, row_ref, col_ref, out_ref):
    s1 = mine_ref[0:1, :] + other_ref[0:1, :]
    s2 = mine_ref[8:9, :] + other_ref[8:9, :]
    factor = 2.5 * s1 / s2
    width = out_ref.shape[3]
    flipped = []
    for t in range(NT_C):
        strips = [[] for _ in range(POLS)]
        for pr in range(2):
            tiles = [acc_ref.at[4 * t + 2 * pr + pc] for pc in range(2)]
            weight = [1.0 / (1.0 + factor * tile[:P_SIZE]) for tile in tiles]
            for pol in range(POLS):
                parts = []
                for e in (1 + 2 * pol, 2 + 2 * pol):
                    for pc in range(2):
                        parts.append(tiles[pc][e * P_SIZE : (e + 1) * P_SIZE] * weight[pc])
                strips[pol].append(jnp.concatenate(parts, axis=1))
        for pol in range(POLS):
            flipped.append(dot_parts(jnp.concatenate(strips[pol], axis=0), row_ref).T)
    done = dot_parts(jnp.concatenate(flipped, axis=0), col_ref)
    for t in range(NT_C):
        for pol in range(POLS):
            at = (t * POLS + pol) * 2 * width
            real, imag = done[at : at + width], done[at + width : at + 2 * width]
            out_ref[pol, 0, t] = real[:, :G] + imag[:, G:]
            out_ref[pol, 1, t] = imag[:, :G] - real[:, G:]


def make_image(acc, mine, other, row_table, col_table, width):
    return pl.pallas_call(
        image_kernel,
        out_shape=jax.ShapeDtypeStruct((POLS, 2, NT_C, width, G), jnp.float32),
        in_specs=[VMEM] * 5,
        out_specs=VMEM,
        compiler_params=PARAMS,
        name="image",
    )(acc, mine, other, row_table, col_table)


def dft_tables():
    index = np.arange(G)
    phase = (index[:, None] * index[None, :] % G) * (2.0 * math.pi / G)
    return np.cos(phase).astype(np.float32), np.sin(phase).astype(np.float32)


def np_parts(table):
    high = table.astype(ml_dtypes.bfloat16)
    low = (table - high.astype(np.float32)).astype(ml_dtypes.bfloat16)
    return np.concatenate([high, low], axis=-1)


def image_tables(n_tm):
    cosine, sine = dft_tables()
    rows = []
    for cos_part, sin_part in zip(np.split(cosine, n_tm, axis=1), np.split(sine, n_tm, axis=1)):
        rows.append(np_parts(np.block([[cos_part, -sin_part], [sin_part, cos_part]])))
    return np.stack(rows), np_parts(np.concatenate([cosine, sine], axis=1) / G)


def by_gather(packed, n_tm):
    order = list(range(0, n_tm, 2)) + list(range(1, n_tm, 2))[::-1]
    up = [(order[i], order[(i + 1) % n_tm]) for i in range(n_tm)]
    down = [(b, a) for a, b in up]
    held = [[lax.ppermute(a, "tm", up), lax.ppermute(a, "tm", down)] for a in packed]
    acc = add_blocks(None, packed)
    for step in range(2, n_tm // 2 + 1):
        far = step == n_tm // 2
        for i, pair in enumerate(held):
            if i > 0:
                acc, *pair = lax.optimization_barrier((acc, *pair))
            sent = []
            if not (far and i == 1):
                sent.append(lax.ppermute(pair[0], "tm", up))
            if not (far and i == 0):
                sent.append(lax.ppermute(pair[1], "tm", down))
            acc = add_blocks(acc, pair)
            held[i] = sent
    acc = add_blocks(acc, held[0])
    return add_blocks(acc, held[1], last=True)


def rest_by_rows(acc, cosine, sine):
    grid = acc.reshape(NT_C, 2, 2, GRIDS, P_SIZE, P_SIZE)
    flat = jnp.transpose(grid, (3, 0, 1, 4, 2, 5)).reshape(GRIDS, NT_C * G, G)
    owned = lax.psum_scatter(flat, "tm", scatter_dimension=1, tiled=True)
    dens = owned[0]
    totals = lax.psum((jnp.sum(dens), jnp.sum(dens * dens)), ("tm", "tile"))
    factor = 2.5 * totals[0] / totals[1]
    weighted = owned[1:] / (1.0 + factor * dens[None])
    weighted = weighted.reshape(POLS, 2, dens.shape[0], G)
    real, imag = weighted[:, 0], weighted[:, 1]

    def rows(a, b):
        return jnp.einsum("prj,jn->prn", a, b, precision=HIGH)

    done = jnp.stack([rows(real, cosine) + rows(imag, sine), rows(imag, cosine) - rows(real, sine)], axis=1)
    width = G // lax.axis_size("tm")
    every_row = lax.all_gather(done, "tm", axis=2, tiled=True)
    columns = lax.dynamic_slice_in_dim(every_row, lax.axis_index("tm") * width, width, 3)
    columns = columns.reshape(POLS, 2, NT_C, G, width)
    real, imag = columns[:, 0], columns[:, 1]

    def cols(a, b):
        return jnp.einsum("mi,ptic->ptcm", a, b, precision=HIGH)

    out = jnp.stack([cols(cosine, real) + cols(sine, imag), cols(cosine, imag) - cols(sine, real)], axis=1)
    return out / G


def body(vis_data, vis_weight, kernel_taps, offsets, block_patch, block_count):
    slots = vis_weight.shape[1]
    n_tm = lax.axis_size("tm")
    pieces = (10 * slots // 16, slots - 10 * slots // 16)
    packed = pack(pieces, vis_data[0], vis_weight[0], kernel_taps[0], offsets[0], block_patch, block_count)
    if n_tm > 8:
        cosine, sine = dft_tables()
        return rest_by_rows(add_blocks(None, packed), jnp.asarray(cosine), jnp.asarray(sine))
    acc, mine = by_gather(packed, n_tm)
    n_tile = lax.axis_size("tile")
    other = lax.ppermute(mine, "tile", [(i, n_tile - 1 - i) for i in range(n_tile)])
    row_tables, col_table = image_tables(n_tm)
    row_table = lax.dynamic_index_in_dim(jnp.asarray(row_tables), lax.axis_index("tm"), 0, keepdims=False)
    return make_image(acc, mine, other, row_table, jnp.asarray(col_table), G // n_tm)


def solution(mesh):
    return jax.shard_map(
        body,
        mesh=mesh,
        in_specs=(
            P(("grp", "tile"), "tm", None, None),
            P(("grp", "tile"), "tm", None),
            P(("grp", "tile"), "tm", None, None, None),
            P(("grp", "tile"), "tm", None, None),
            P(("grp", "tile"), "tm"),
            P(("grp", "tile"), "tm"),
        ),
        out_specs=P(None, None, ("grp", "tile"), "tm", None),
        check_vma=False,
    )
```

```python
import math

import jax
import jax.numpy as jnp
import ml_dtypes
import numpy as np
from jax import lax
from jax.experimental import pallas as pl
from jax.experimental.pallas import tpu as pltpu
from jax.sharding import PartitionSpec as P

G = 256
P_SIZE = 128
K = 8
B = 256
POLS = 2
NT_C = 2
PATCHES = 4 * NT_C
GRIDS = 1 + 2 * POLS
X_ROW = 2 * K
OFF_ROW = X_ROW + GRIDS
ID_ROW = OFF_ROW + 2
ROWS = ID_ROW + 1
COUNT_LANE = 128
HIGH = lax.Precision.HIGHEST
VMEM = pl.BlockSpec(memory_space=pltpu.VMEM)
PARAMS = pltpu.CompilerParams(vmem_limit_bytes=20 * 1024 * 1024)


def pack_kernel(pieces, vis_hbm, weight_hbm, taps_hbm, offs_hbm, patch_hbm, count_ref, *refs):
    outs, scratch = refs[: len(pieces)], refs[len(pieces) :]
    vis_ref, weight_ref, taps_ref, offs_ref, patch_ref, sems = scratch
    pairs = (
        (offs_hbm, offs_ref),
        (taps_hbm, taps_ref),
        (weight_hbm, weight_ref),
        (vis_hbm, vis_ref),
        (patch_hbm, patch_ref),
    )
    copies = [pltpu.make_async_copy(a, b, sems.at[i]) for i, (a, b) in enumerate(pairs)]
    for copy in copies:
        copy.start()
    places = []
    base = 0
    for out_ref, size in zip(outs, pieces):
        places += [(out_ref, j, base + j) for j in range(size)]
        base += size
    copies[0].wait()
    copies[1].wait()
    for out_ref, j, at in places:
        for side in range(2):
            off = offs_ref[at, side : side + 1, :]
            taps = taps_ref[at, side]
            for bit in range(3):
                moved = pltpu.roll(taps, 1 << bit, 0)
                turn = jnp.broadcast_to((off >> bit) & 1, taps.shape) == 1
                taps = jnp.where(turn, moved, taps)
            out_ref[j, side * K : (side + 1) * K, :] = taps
        out_ref[j, OFF_ROW:ID_ROW, :] = offs_ref[at].astype(jnp.float32)
    copies[2].wait()
    copies[3].wait()
    for out_ref, j, at in places:
        weight = weight_ref[at : at + 1, :]
        out_ref[j, X_ROW : X_ROW + 1, :] = weight
        out_ref[j, X_ROW + 1 : OFF_ROW, :] = weight * vis_ref[at]
    copies[4].wait()
    lane = lax.broadcasted_iota(jnp.int32, (1, B), 1)
    for out_ref, j, at in places:
        live = jnp.clip(count_ref[0, 0] - (at - j), 0, out_ref.shape[0])
        row = jnp.where(lane < COUNT_LANE, patch_ref[0, at], live)
        out_ref[j, ID_ROW:ROWS, :] = row.astype(jnp.float32)


def pack(pieces, vis, weight, taps, offs, patches, count):
    arrays = (vis, weight, taps, offs, patches)
    spaces = [pltpu.VMEM] * 4 + [pltpu.SMEM]
    hbm, smem = pl.BlockSpec(memory_space=pltpu.HBM), pl.BlockSpec(memory_space=pltpu.SMEM)
    return pl.pallas_call(
        lambda *refs: pack_kernel(pieces, *refs),
        out_shape=[jax.ShapeDtypeStruct((size, ROWS, B), jnp.float32) for size in pieces],
        in_specs=[hbm] * 5 + [smem],
        out_specs=[VMEM] * len(pieces),
        scratch_shapes=[space(a.shape, a.dtype) for space, a in zip(spaces, arrays)] + [pltpu.SemaphoreType.DMA((5,))],
        compiler_params=PARAMS,
        name="pack",
    )(*[pltpu.with_memory_space_constraint(a, pltpu.HBM) for a in arrays], count)


def spread(off):
    row = lax.broadcasted_iota(jnp.int32, (16, B), 0)
    gap = off.astype(jnp.int32) - row
    step = (gap + 15) >> 4
    inside = (step << 4) - gap < K
    return jnp.where(inside, step, -1).astype(jnp.float32).astype(jnp.bfloat16)


def block_factors(block, live):
    rows_u = jnp.concatenate([block[0:K]] * 2, axis=0)
    rows_v = jnp.concatenate([block[K : 2 * K]] * 2, axis=0)
    step_u = spread(block[OFF_ROW : OFF_ROW + 1])
    step_v = spread(block[OFF_ROW + 1 : OFF_ROW + 2])
    if live is not None:
        rows_v = jnp.where(live, rows_v, 0.0)
    rows_v = rows_v.astype(jnp.bfloat16)
    zero = jnp.zeros((16, B), jnp.bfloat16)
    steps = P_SIZE // 16
    right = jnp.concatenate([jnp.where(step_v == s, rows_v, zero) for s in range(steps)], axis=0)
    hits = [step_u == s for s in range(steps)]
    left = []
    for e in range(GRIDS):
        product = (rows_u * block[X_ROW + e : X_ROW + e + 1]).astype(jnp.bfloat16)
        left += [jnp.where(hit, product, zero) for hit in hits]
    return jnp.concatenate(left, axis=0), right


def add_some(buf_ref, acc_ref, first, count, unroll):
    waiting = None
    for i in range(unroll):
        j = first if i == 0 else jnp.minimum(first + i, buf_ref.shape[0] - 1)
        block = buf_ref[j]
        left, right = block_factors(block, None if i == 0 else first + i < count)
        patch = lax.dot_general(
            left, right, (((1,), (1,)), ((), ())), preferred_element_type=jnp.float32
        )
        if waiting is not None:
            acc_ref[waiting[0]] += waiting[1]
        waiting = block[ID_ROW:ROWS, 0:1][0, 0].astype(jnp.int32), patch
    acc_ref[waiting[0]] += waiting[1]


def grid_kernel(n, first, last, *refs):
    bufs = refs[:n]
    acc_ref = refs[n] if first else refs[n + 1]
    if first:
        acc_ref[...] = jnp.zeros_like(acc_ref)
    for buf_ref in bufs:
        count = buf_ref[0, ID_ROW:ROWS, COUNT_LANE : COUNT_LANE + 1][0, 0].astype(jnp.int32)

        unroll = min(5, (buf_ref.shape[0] + 1) // 2)

        def some(step, _, buf_ref=buf_ref, count=count, unroll=unroll):
            add_some(buf_ref, acc_ref, unroll * step, count, unroll)
            return 0

        lax.fori_loop(0, (count + unroll - 1) // unroll, some, 0)
    if last:
        sums_ref = refs[-1]
        dens = acc_ref[:, :P_SIZE, :]
        for i, value in enumerate((dens, dens * dens)):
            part = jnp.sum(value.reshape(-1, 8, P_SIZE), axis=0)
            part = jnp.sum(jnp.sum(part, axis=0, keepdims=True), axis=1, keepdims=True)
            sums_ref[8 * i : 8 * i + 8, :] = jnp.broadcast_to(part, (8, P_SIZE))


def add_blocks(acc, bufs, last=False):
    first = acc is None
    n = len(bufs)
    slots = sum(buf.shape[0] for buf in bufs)
    out_shape = [jax.ShapeDtypeStruct((PATCHES, GRIDS * P_SIZE, P_SIZE), jnp.float32)]
    if last:
        out_shape.append(jax.ShapeDtypeStruct((16, P_SIZE), jnp.float32))
    args = list(bufs) + ([] if first else [acc])
    flops = 4 * slots * GRIDS * P_SIZE * P_SIZE * B
    out = pl.pallas_call(
        lambda *refs: grid_kernel(n, first, last, *refs),
        out_shape=out_shape,
        in_specs=[VMEM] * len(args),
        out_specs=[VMEM] * len(out_shape),
        input_output_aliases={} if first else {n: 0},
        compiler_params=PARAMS,
        cost_estimate=pl.CostEstimate(flops=flops, bytes_accessed=slots * ROWS * B, transcendentals=0),
        name="grid",
    )(*args)
    return tuple(out) if last else out[0]


def two_parts(value):
    high = value.astype(jnp.bfloat16)
    return high, (value - high.astype(jnp.float32)).astype(jnp.bfloat16)


def dot_parts(value, table_ref):
    width = table_ref.shape[1] // 2
    high, low = two_parts(value)
    both = jnp.dot(high, table_ref[...], preferred_element_type=jnp.float32)
    return both[:, :width] + both[:, width:] + jnp.dot(low, table_ref[:, :width], preferred_element_type=jnp.float32)


def image_kernel(acc_ref, mine_ref, other_ref, row_ref, col_ref, out_ref):
    s1 = mine_ref[0:1, :] + other_ref[0:1, :]
    s2 = mine_ref[8:9, :] + other_ref[8:9, :]
    factor = 2.5 * s1 / s2
    width = out_ref.shape[3]
    flipped = []
    for t in range(NT_C):
        strips = [[] for _ in range(POLS)]
        for pr in range(2):
            tiles = [acc_ref.at[4 * t + 2 * pr + pc] for pc in range(2)]
            weight = [1.0 / (1.0 + factor * tile[:P_SIZE]) for tile in tiles]
            for pol in range(POLS):
                parts = []
                for e in (1 + 2 * pol, 2 + 2 * pol):
                    for pc in range(2):
                        parts.append(tiles[pc][e * P_SIZE : (e + 1) * P_SIZE] * weight[pc])
                strips[pol].append(jnp.concatenate(parts, axis=1))
        for pol in range(POLS):
            flipped.append(dot_parts(jnp.concatenate(strips[pol], axis=0), row_ref).T)
    done = dot_parts(jnp.concatenate(flipped, axis=0), col_ref)
    for t in range(NT_C):
        for pol in range(POLS):
            at = (t * POLS + pol) * 2 * width
            real, imag = done[at : at + width], done[at + width : at + 2 * width]
            out_ref[pol, 0, t] = real[:, :G] + imag[:, G:]
            out_ref[pol, 1, t] = imag[:, :G] - real[:, G:]


def make_image(acc, mine, other, row_table, col_table, width):
    return pl.pallas_call(
        image_kernel,
        out_shape=jax.ShapeDtypeStruct((POLS, 2, NT_C, width, G), jnp.float32),
        in_specs=[VMEM] * 5,
        out_specs=VMEM,
        compiler_params=PARAMS,
        name="image",
    )(acc, mine, other, row_table, col_table)


def dft_tables():
    index = np.arange(G)
    phase = (index[:, None] * index[None, :] % G) * (2.0 * math.pi / G)
    return np.cos(phase).astype(np.float32), np.sin(phase).astype(np.float32)


def np_parts(table):
    high = table.astype(ml_dtypes.bfloat16)
    low = (table - high.astype(np.float32)).astype(ml_dtypes.bfloat16)
    return np.concatenate([high, low], axis=-1)


def image_tables(n_tm):
    cosine, sine = dft_tables()
    rows = []
    for cos_part, sin_part in zip(np.split(cosine, n_tm, axis=1), np.split(sine, n_tm, axis=1)):
        rows.append(np_parts(np.block([[cos_part, -sin_part], [sin_part, cos_part]])))
    return np.stack(rows), np_parts(np.concatenate([cosine, sine], axis=1) / G)


def by_gather(packed, n_tm):
    order = list(range(0, n_tm, 2)) + list(range(1, n_tm, 2))[::-1]
    up = [(order[i], order[(i + 1) % n_tm]) for i in range(n_tm)]
    down = [(b, a) for a, b in up]

    def both_ways(pair):
        return [lax.ppermute(pair[0], "tm", up), lax.ppermute(pair[1], "tm", down)]

    leading = both_ways(packed)
    acc = add_blocks(None, packed)
    acc, *packed = lax.optimization_barrier((acc, *packed))
    trailing = both_ways(packed[::-1])
    for step in range(2, n_tm // 2 + 1):
        following = both_ways(leading)
        acc = add_blocks(acc, leading)
        acc, *trailing = lax.optimization_barrier((acc, *trailing))
        leading = following
        following = both_ways(trailing) if step < n_tm // 2 else None
        acc = add_blocks(acc, trailing)
        trailing = following
    acc = add_blocks(acc, leading[:1])
    return add_blocks(acc, leading[1:], last=True)


def rest_by_rows(acc, cosine, sine):
    grid = acc.reshape(NT_C, 2, 2, GRIDS, P_SIZE, P_SIZE)
    flat = jnp.transpose(grid, (3, 0, 1, 4, 2, 5)).reshape(GRIDS, NT_C * G, G)
    owned = lax.psum_scatter(flat, "tm", scatter_dimension=1, tiled=True)
    dens = owned[0]
    totals = lax.psum((jnp.sum(dens), jnp.sum(dens * dens)), ("tm", "tile"))
    factor = 2.5 * totals[0] / totals[1]
    weighted = owned[1:] / (1.0 + factor * dens[None])
    weighted = weighted.reshape(POLS, 2, dens.shape[0], G)
    real, imag = weighted[:, 0], weighted[:, 1]

    def rows(a, b):
        return jnp.einsum("prj,jn->prn", a, b, precision=HIGH)

    done = jnp.stack([rows(real, cosine) + rows(imag, sine), rows(imag, cosine) - rows(real, sine)], axis=1)
    width = G // lax.axis_size("tm")
    every_row = lax.all_gather(done, "tm", axis=2, tiled=True)
    columns = lax.dynamic_slice_in_dim(every_row, lax.axis_index("tm") * width, width, 3)
    columns = columns.reshape(POLS, 2, NT_C, G, width)
    real, imag = columns[:, 0], columns[:, 1]

    def cols(a, b):
        return jnp.einsum("mi,ptic->ptcm", a, b, precision=HIGH)

    out = jnp.stack([cols(cosine, real) + cols(sine, imag), cols(cosine, imag) - cols(sine, real)], axis=1)
    return out / G


def body(vis_data, vis_weight, kernel_taps, offsets, block_patch, block_count):
    slots = vis_weight.shape[1]
    n_tm = lax.axis_size("tm")
    pieces = (7 * slots // 16, slots - 7 * slots // 16)
    packed = pack(pieces, vis_data[0], vis_weight[0], kernel_taps[0], offsets[0], block_patch, block_count)
    if n_tm > 8:
        cosine, sine = dft_tables()
        return rest_by_rows(add_blocks(None, packed), jnp.asarray(cosine), jnp.asarray(sine))
    acc, mine = by_gather(packed, n_tm)
    n_tile = lax.axis_size("tile")
    other = lax.ppermute(mine, "tile", [(i, n_tile - 1 - i) for i in range(n_tile)])
    row_tables, col_table = image_tables(n_tm)
    row_table = lax.dynamic_index_in_dim(jnp.asarray(row_tables), lax.axis_index("tm"), 0, keepdims=False)
    return make_image(acc, mine, other, row_table, jnp.asarray(col_table), G // n_tm)


def solution(mesh):
    return jax.shard_map(
        body,
        mesh=mesh,
        in_specs=(
            P(("grp", "tile"), "tm", None, None),
            P(("grp", "tile"), "tm", None),
            P(("grp", "tile"), "tm", None, None, None),
            P(("grp", "tile"), "tm", None, None),
            P(("grp", "tile"), "tm"),
            P(("grp", "tile"), "tm"),
        ),
        out_specs=P(None, None, ("grp", "tile"), "tm", None),
        check_vma=False,
    )
```

```python
import math

import jax
import jax.numpy as jnp
import ml_dtypes
import numpy as np
from jax import lax
from jax.experimental import pallas as pl
from jax.experimental.pallas import tpu as pltpu
from jax.sharding import PartitionSpec as P

G = 256
P_SIZE = 128
K = 8
B = 256
POLS = 2
NT_C = 2
PATCHES = 4 * NT_C
GRIDS = 1 + 2 * POLS
X_ROW = 2 * K
OFF_ROW = X_ROW + GRIDS
ID_ROW = OFF_ROW + 2
ROWS = ID_ROW + 1
COUNT_LANE = 128
HIGH = lax.Precision.HIGHEST
VMEM = pl.BlockSpec(memory_space=pltpu.VMEM)
PARAMS = pltpu.CompilerParams(vmem_limit_bytes=20 * 1024 * 1024)


def pack_kernel(pieces, vis_hbm, weight_hbm, taps_hbm, offs_hbm, patch_hbm, count_ref, *refs):
    outs, scratch = refs[: len(pieces)], refs[len(pieces) :]
    vis_ref, weight_ref, taps_ref, offs_ref, patch_ref, sems = scratch
    pairs = (
        (offs_hbm, offs_ref),
        (taps_hbm, taps_ref),
        (weight_hbm, weight_ref),
        (vis_hbm, vis_ref),
        (patch_hbm, patch_ref),
    )
    copies = [pltpu.make_async_copy(a, b, sems.at[i]) for i, (a, b) in enumerate(pairs)]
    for copy in copies:
        copy.start()
    places = []
    base = 0
    for out_ref, size in zip(outs, pieces):
        places += [(out_ref, j, base + j) for j in range(size)]
        base += size
    copies[0].wait()
    copies[1].wait()
    for out_ref, j, at in places:
        for side in range(2):
            off = offs_ref[at, side : side + 1, :]
            taps = taps_ref[at, side]
            for bit in range(3):
                moved = pltpu.roll(taps, 1 << bit, 0)
                turn = jnp.broadcast_to((off >> bit) & 1, taps.shape) == 1
                taps = jnp.where(turn, moved, taps)
            out_ref[j, side * K : (side + 1) * K, :] = taps
        out_ref[j, OFF_ROW:ID_ROW, :] = offs_ref[at].astype(jnp.float32)
    copies[2].wait()
    copies[3].wait()
    for out_ref, j, at in places:
        weight = weight_ref[at : at + 1, :]
        out_ref[j, X_ROW : X_ROW + 1, :] = weight
        out_ref[j, X_ROW + 1 : OFF_ROW, :] = weight * vis_ref[at]
    copies[4].wait()
    lane = lax.broadcasted_iota(jnp.int32, (1, B), 1)
    for out_ref, j, at in places:
        live = jnp.clip(count_ref[0, 0] - (at - j), 0, out_ref.shape[0])
        row = jnp.where(lane < COUNT_LANE, patch_ref[0, at], live)
        out_ref[j, ID_ROW:ROWS, :] = row.astype(jnp.float32)


def pack(pieces, vis, weight, taps, offs, patches, count):
    arrays = (vis, weight, taps, offs, patches)
    spaces = [pltpu.VMEM] * 4 + [pltpu.SMEM]
    hbm, smem = pl.BlockSpec(memory_space=pltpu.HBM), pl.BlockSpec(memory_space=pltpu.SMEM)
    return pl.pallas_call(
        lambda *refs: pack_kernel(pieces, *refs),
        out_shape=[jax.ShapeDtypeStruct((size, ROWS, B), jnp.float32) for size in pieces],
        in_specs=[hbm] * 5 + [smem],
        out_specs=[VMEM] * len(pieces),
        scratch_shapes=[space(a.shape, a.dtype) for space, a in zip(spaces, arrays)] + [pltpu.SemaphoreType.DMA((5,))],
        compiler_params=PARAMS,
        name="pack",
    )(*[pltpu.with_memory_space_constraint(a, pltpu.HBM) for a in arrays], count)


def spread(off):
    row = lax.broadcasted_iota(jnp.int32, (16, B), 0)
    gap = off.astype(jnp.int32) - row
    step = (gap + 15) >> 4
    inside = (step << 4) - gap < K
    return jnp.where(inside, step, -1).astype(jnp.float32).astype(jnp.bfloat16)


def block_factors(block, live):
    rows_u = jnp.concatenate([block[0:K]] * 2, axis=0)
    rows_v = jnp.concatenate([block[K : 2 * K]] * 2, axis=0)
    step_u = spread(block[OFF_ROW : OFF_ROW + 1])
    step_v = spread(block[OFF_ROW + 1 : OFF_ROW + 2])
    if live is not None:
        rows_v = jnp.where(live, rows_v, 0.0)
    rows_v = rows_v.astype(jnp.bfloat16)
    zero = jnp.zeros((16, B), jnp.bfloat16)
    steps = P_SIZE // 16
    right = jnp.concatenate([jnp.where(step_v == s, rows_v, zero) for s in range(steps)], axis=0)
    hits = [step_u == s for s in range(steps)]
    left = []
    for e in range(GRIDS):
        product = (rows_u * block[X_ROW + e : X_ROW + e + 1]).astype(jnp.bfloat16)
        left += [jnp.where(hit, product, zero) for hit in hits]
    return jnp.concatenate(left, axis=0), right


def add_some(buf_ref, acc_ref, first, count, unroll):
    waiting = None
    for i in range(unroll):
        j = first if i == 0 else jnp.minimum(first + i, buf_ref.shape[0] - 1)
        block = buf_ref[j]
        left, right = block_factors(block, None if i == 0 else first + i < count)
        patch = lax.dot_general(
            left, right, (((1,), (1,)), ((), ())), preferred_element_type=jnp.float32
        )
        if waiting is not None:
            acc_ref[waiting[0]] += waiting[1]
        waiting = block[ID_ROW:ROWS, 0:1][0, 0].astype(jnp.int32), patch
    acc_ref[waiting[0]] += waiting[1]


def grid_kernel(n, first, last, *refs):
    bufs = refs[:n]
    acc_ref = refs[n] if first else refs[n + 1]
    if first:
        acc_ref[...] = jnp.zeros_like(acc_ref)
    for buf_ref in bufs:
        count = buf_ref[0, ID_ROW:ROWS, COUNT_LANE : COUNT_LANE + 1][0, 0].astype(jnp.int32)

        unroll = min(5, (buf_ref.shape[0] + 1) // 2)

        def some(step, _, buf_ref=buf_ref, count=count, unroll=unroll):
            add_some(buf_ref, acc_ref, unroll * step, count, unroll)
            return 0

        lax.fori_loop(0, (count + unroll - 1) // unroll, some, 0)
    if last:
        sums_ref = refs[-1]
        dens = acc_ref[:, :P_SIZE, :]
        for i, value in enumerate((dens, dens * dens)):
            part = jnp.sum(value.reshape(-1, 8, P_SIZE), axis=0)
            part = jnp.sum(jnp.sum(part, axis=0, keepdims=True), axis=1, keepdims=True)
            sums_ref[8 * i : 8 * i + 8, :] = jnp.broadcast_to(part, (8, P_SIZE))


def add_blocks(acc, bufs, last=False):
    first = acc is None
    n = len(bufs)
    slots = sum(buf.shape[0] for buf in bufs)
    out_shape = [jax.ShapeDtypeStruct((PATCHES, GRIDS * P_SIZE, P_SIZE), jnp.float32)]
    if last:
        out_shape.append(jax.ShapeDtypeStruct((16, P_SIZE), jnp.float32))
    args = list(bufs) + ([] if first else [acc])
    flops = 4 * slots * GRIDS * P_SIZE * P_SIZE * B
    out = pl.pallas_call(
        lambda *refs: grid_kernel(n, first, last, *refs),
        out_shape=out_shape,
        in_specs=[VMEM] * len(args),
        out_specs=[VMEM] * len(out_shape),
        input_output_aliases={} if first else {n: 0},
        compiler_params=PARAMS,
        cost_estimate=pl.CostEstimate(flops=flops, bytes_accessed=slots * ROWS * B, transcendentals=0),
        name="grid",
    )(*args)
    return tuple(out) if last else out[0]


def two_parts(value):
    high = value.astype(jnp.bfloat16)
    return high, (value - high.astype(jnp.float32)).astype(jnp.bfloat16)


def dot_parts(value, table_ref):
    width = table_ref.shape[1] // 2
    high, low = two_parts(value)
    both = jnp.dot(high, table_ref[...], preferred_element_type=jnp.float32)
    return both[:, :width] + both[:, width:] + jnp.dot(low, table_ref[:, :width], preferred_element_type=jnp.float32)


def image_kernel(acc_ref, mine_ref, other_ref, row_ref, col_ref, out_ref):
    s1 = mine_ref[0:1, :] + other_ref[0:1, :]
    s2 = mine_ref[8:9, :] + other_ref[8:9, :]
    factor = 2.5 * s1 / s2
    width = out_ref.shape[3]
    flipped = []
    for t in range(NT_C):
        strips = [[] for _ in range(POLS)]
        for pr in range(2):
            tiles = [acc_ref.at[4 * t + 2 * pr + pc] for pc in range(2)]
            weight = [1.0 / (1.0 + factor * tile[:P_SIZE]) for tile in tiles]
            for pol in range(POLS):
                parts = []
                for e in (1 + 2 * pol, 2 + 2 * pol):
                    for pc in range(2):
                        parts.append(tiles[pc][e * P_SIZE : (e + 1) * P_SIZE] * weight[pc])
                strips[pol].append(jnp.concatenate(parts, axis=1))
        for pol in range(POLS):
            flipped.append(dot_parts(jnp.concatenate(strips[pol], axis=0), row_ref).T)
    done = dot_parts(jnp.concatenate(flipped, axis=0), col_ref)
    for t in range(NT_C):
        for pol in range(POLS):
            at = (t * POLS + pol) * 2 * width
            real, imag = done[at : at + width], done[at + width : at + 2 * width]
            out_ref[pol, 0, t] = real[:, :G] + imag[:, G:]
            out_ref[pol, 1, t] = imag[:, :G] - real[:, G:]


def make_image(acc, mine, other, row_table, col_table, width):
    return pl.pallas_call(
        image_kernel,
        out_shape=jax.ShapeDtypeStruct((POLS, 2, NT_C, width, G), jnp.float32),
        in_specs=[VMEM] * 5,
        out_specs=VMEM,
        compiler_params=PARAMS,
        name="image",
    )(acc, mine, other, row_table, col_table)


def dft_tables():
    index = np.arange(G)
    phase = (index[:, None] * index[None, :] % G) * (2.0 * math.pi / G)
    return np.cos(phase).astype(np.float32), np.sin(phase).astype(np.float32)


def np_parts(table):
    high = table.astype(ml_dtypes.bfloat16)
    low = (table - high.astype(np.float32)).astype(ml_dtypes.bfloat16)
    return np.concatenate([high, low], axis=-1)


def image_tables(n_tm):
    cosine, sine = dft_tables()
    rows = []
    for cos_part, sin_part in zip(np.split(cosine, n_tm, axis=1), np.split(sine, n_tm, axis=1)):
        rows.append(np_parts(np.block([[cos_part, -sin_part], [sin_part, cos_part]])))
    return np.stack(rows), np_parts(np.concatenate([cosine, sine], axis=1) / G)


def by_gather(packed, n_tm):
    order = list(range(0, n_tm, 2)) + list(range(1, n_tm, 2))[::-1]
    up = [(order[i], order[(i + 1) % n_tm]) for i in range(n_tm)]
    down = [(b, a) for a, b in up]

    def both_ways(pair):
        return [lax.ppermute(pair[0], "tm", up), lax.ppermute(pair[1], "tm", down)]

    leading = both_ways(packed)
    trailing = both_ways(packed[::-1])
    acc = add_blocks(None, packed)
    for step in range(2, n_tm // 2 + 1):
        following = both_ways(leading)
        acc = add_blocks(acc, leading)
        acc, *trailing = lax.optimization_barrier((acc, *trailing))
        leading = following
        following = both_ways(trailing) if step < n_tm // 2 else None
        acc = add_blocks(acc, trailing)
        trailing = following
    acc = add_blocks(acc, leading[:1])
    return add_blocks(acc, leading[1:], last=True)


def rest_by_rows(acc, cosine, sine):
    grid = acc.reshape(NT_C, 2, 2, GRIDS, P_SIZE, P_SIZE)
    flat = jnp.transpose(grid, (3, 0, 1, 4, 2, 5)).reshape(GRIDS, NT_C * G, G)
    owned = lax.psum_scatter(flat, "tm", scatter_dimension=1, tiled=True)
    dens = owned[0]
    totals = lax.psum((jnp.sum(dens), jnp.sum(dens * dens)), ("tm", "tile"))
    factor = 2.5 * totals[0] / totals[1]
    weighted = owned[1:] / (1.0 + factor * dens[None])
    weighted = weighted.reshape(POLS, 2, dens.shape[0], G)
    real, imag = weighted[:, 0], weighted[:, 1]

    def rows(a, b):
        return jnp.einsum("prj,jn->prn", a, b, precision=HIGH)

    done = jnp.stack([rows(real, cosine) + rows(imag, sine), rows(imag, cosine) - rows(real, sine)], axis=1)
    width = G // lax.axis_size("tm")
    every_row = lax.all_gather(done, "tm", axis=2, tiled=True)
    columns = lax.dynamic_slice_in_dim(every_row, lax.axis_index("tm") * width, width, 3)
    columns = columns.reshape(POLS, 2, NT_C, G, width)
    real, imag = columns[:, 0], columns[:, 1]

    def cols(a, b):
        return jnp.einsum("mi,ptic->ptcm", a, b, precision=HIGH)

    out = jnp.stack([cols(cosine, real) + cols(sine, imag), cols(cosine, imag) - cols(sine, real)], axis=1)
    return out / G


def body(vis_data, vis_weight, kernel_taps, offsets, block_patch, block_count):
    slots = vis_weight.shape[1]
    n_tm = lax.axis_size("tm")
    pieces = (slots // 2, slots - slots // 2)
    packed = pack(pieces, vis_data[0], vis_weight[0], kernel_taps[0], offsets[0], block_patch, block_count)
    if n_tm > 8:
        cosine, sine = dft_tables()
        return rest_by_rows(add_blocks(None, packed), jnp.asarray(cosine), jnp.asarray(sine))
    acc, mine = by_gather(packed, n_tm)
    n_tile = lax.axis_size("tile")
    other = lax.ppermute(mine, "tile", [(i, n_tile - 1 - i) for i in range(n_tile)])
    row_tables, col_table = image_tables(n_tm)
    row_table = lax.dynamic_index_in_dim(jnp.asarray(row_tables), lax.axis_index("tm"), 0, keepdims=False)
    return make_image(acc, mine, other, row_table, jnp.asarray(col_table), G // n_tm)


def solution(mesh):
    return jax.shard_map(
        body,
        mesh=mesh,
        in_specs=(
            P(("grp", "tile"), "tm", None, None),
            P(("grp", "tile"), "tm", None),
            P(("grp", "tile"), "tm", None, None, None),
            P(("grp", "tile"), "tm", None, None),
            P(("grp", "tile"), "tm"),
            P(("grp", "tile"), "tm"),
        ),
        out_specs=P(None, None, ("grp", "tile"), "tm", None),
        check_vma=False,
    )
```

```python
import math

import jax
import jax.numpy as jnp
import ml_dtypes
import numpy as np
from jax import lax
from jax.experimental import pallas as pl
from jax.experimental.pallas import tpu as pltpu
from jax.sharding import PartitionSpec as P

G = 256
P_SIZE = 128
K = 8
B = 256
POLS = 2
NT_C = 2
PATCHES = 4 * NT_C
GRIDS = 1 + 2 * POLS
X_ROW = 2 * K
OFF_ROW = X_ROW + GRIDS
ID_ROW = OFF_ROW + 2
ROWS = ID_ROW + 1
COUNT_LANE = 128
HIGH = lax.Precision.HIGHEST
VMEM = pl.BlockSpec(memory_space=pltpu.VMEM)
PARAMS = pltpu.CompilerParams(vmem_limit_bytes=20 * 1024 * 1024)


def pack_kernel(pieces, vis_hbm, weight_hbm, taps_hbm, offs_hbm, patch_hbm, count_ref, *refs):
    outs, scratch = refs[: len(pieces)], refs[len(pieces) :]
    vis_ref, weight_ref, taps_ref, offs_ref, patch_ref, sems = scratch
    pairs = (
        (offs_hbm, offs_ref),
        (taps_hbm, taps_ref),
        (weight_hbm, weight_ref),
        (vis_hbm, vis_ref),
        (patch_hbm, patch_ref),
    )
    copies = [pltpu.make_async_copy(a, b, sems.at[i]) for i, (a, b) in enumerate(pairs)]
    for copy in copies:
        copy.start()
    places = []
    base = 0
    for out_ref, size in zip(outs, pieces):
        places += [(out_ref, j, base + j) for j in range(size)]
        base += size
    copies[0].wait()
    copies[1].wait()
    for out_ref, j, at in places:
        for side in range(2):
            off = offs_ref[at, side : side + 1, :]
            taps = taps_ref[at, side]
            for bit in range(3):
                moved = pltpu.roll(taps, 1 << bit, 0)
                turn = jnp.broadcast_to((off >> bit) & 1, taps.shape) == 1
                taps = jnp.where(turn, moved, taps)
            out_ref[j, side * K : (side + 1) * K, :] = taps
        out_ref[j, OFF_ROW:ID_ROW, :] = offs_ref[at].astype(jnp.float32)
    copies[2].wait()
    copies[3].wait()
    for out_ref, j, at in places:
        weight = weight_ref[at : at + 1, :]
        out_ref[j, X_ROW : X_ROW + 1, :] = weight
        out_ref[j, X_ROW + 1 : OFF_ROW, :] = weight * vis_ref[at]
    copies[4].wait()
    lane = lax.broadcasted_iota(jnp.int32, (1, B), 1)
    for out_ref, j, at in places:
        live = jnp.clip(count_ref[0, 0] - (at - j), 0, out_ref.shape[0])
        row = jnp.where(lane < COUNT_LANE, patch_ref[0, at], live)
        out_ref[j, ID_ROW:ROWS, :] = row.astype(jnp.float32)


def pack(pieces, vis, weight, taps, offs, patches, count):
    arrays = (vis, weight, taps, offs, patches)
    spaces = [pltpu.VMEM] * 4 + [pltpu.SMEM]
    hbm, smem = pl.BlockSpec(memory_space=pltpu.HBM), pl.BlockSpec(memory_space=pltpu.SMEM)
    return pl.pallas_call(
        lambda *refs: pack_kernel(pieces, *refs),
        out_shape=[jax.ShapeDtypeStruct((size, ROWS, B), jnp.float32) for size in pieces],
        in_specs=[hbm] * 5 + [smem],
        out_specs=[VMEM] * len(pieces),
        scratch_shapes=[space(a.shape, a.dtype) for space, a in zip(spaces, arrays)] + [pltpu.SemaphoreType.DMA((5,))],
        compiler_params=PARAMS,
        name="pack",
    )(*[pltpu.with_memory_space_constraint(a, pltpu.HBM) for a in arrays], count)


def spread(off):
    row = lax.broadcasted_iota(jnp.int32, (16, B), 0)
    gap = off.astype(jnp.int32) - row
    step = (gap + 15) >> 4
    inside = (step << 4) - gap < K
    return jnp.where(inside, step, -1).astype(jnp.float32).astype(jnp.bfloat16)


def block_factors(block, live):
    rows_u = jnp.concatenate([block[0:K]] * 2, axis=0)
    rows_v = jnp.concatenate([block[K : 2 * K]] * 2, axis=0)
    step_u = spread(block[OFF_ROW : OFF_ROW + 1])
    step_v = spread(block[OFF_ROW + 1 : OFF_ROW + 2])
    if live is not None:
        rows_v = jnp.where(live, rows_v, 0.0)
    rows_v = rows_v.astype(jnp.bfloat16)
    zero = jnp.zeros((16, B), jnp.bfloat16)
    steps = P_SIZE // 16
    right = jnp.concatenate([jnp.where(step_v == s, rows_v, zero) for s in range(steps)], axis=0)
    hits = [step_u == s for s in range(steps)]
    left = []
    for e in range(GRIDS):
        product = (rows_u * block[X_ROW + e : X_ROW + e + 1]).astype(jnp.bfloat16)
        left += [jnp.where(hit, product, zero) for hit in hits]
    return jnp.concatenate(left, axis=0), right


def add_some(buf_ref, acc_ref, first, count, unroll):
    waiting = None
    for i in range(unroll):
        j = first if i == 0 else jnp.minimum(first + i, buf_ref.shape[0] - 1)
        block = buf_ref[j]
        left, right = block_factors(block, None if i == 0 else first + i < count)
        patch = lax.dot_general(
            right, left, (((1,), (1,)), ((), ())), preferred_element_type=jnp.float32
        )
        if waiting is not None:
            acc_ref[waiting[0]] += waiting[1]
        waiting = block[ID_ROW:ROWS, 0:1][0, 0].astype(jnp.int32), patch
    acc_ref[waiting[0]] += waiting[1]


def grid_kernel(n, first, last, *refs):
    bufs = refs[:n]
    acc_ref = refs[n] if first else refs[n + 1]
    if first:
        acc_ref[...] = jnp.zeros_like(acc_ref)
    for buf_ref in bufs:
        count = buf_ref[0, ID_ROW:ROWS, COUNT_LANE : COUNT_LANE + 1][0, 0].astype(jnp.int32)

        unroll = min(5, (buf_ref.shape[0] + 1) // 2)

        def some(step, _, buf_ref=buf_ref, count=count, unroll=unroll):
            add_some(buf_ref, acc_ref, unroll * step, count, unroll)
            return 0

        lax.fori_loop(0, (count + unroll - 1) // unroll, some, 0)
    if last:
        sums_ref = refs[-1]
        dens = acc_ref[:, :, :P_SIZE]
        for i, value in enumerate((dens, dens * dens)):
            part = jnp.sum(value.reshape(-1, 8, P_SIZE), axis=0)
            part = jnp.sum(jnp.sum(part, axis=0, keepdims=True), axis=1, keepdims=True)
            sums_ref[8 * i : 8 * i + 8, :] = jnp.broadcast_to(part, (8, P_SIZE))


def add_blocks(acc, bufs, last=False):
    first = acc is None
    n = len(bufs)
    slots = sum(buf.shape[0] for buf in bufs)
    out_shape = [jax.ShapeDtypeStruct((PATCHES, P_SIZE, GRIDS * P_SIZE), jnp.float32)]
    if last:
        out_shape.append(jax.ShapeDtypeStruct((16, P_SIZE), jnp.float32))
    args = list(bufs) + ([] if first else [acc])
    flops = 4 * slots * GRIDS * P_SIZE * P_SIZE * B
    out = pl.pallas_call(
        lambda *refs: grid_kernel(n, first, last, *refs),
        out_shape=out_shape,
        in_specs=[VMEM] * len(args),
        out_specs=[VMEM] * len(out_shape),
        input_output_aliases={} if first else {n: 0},
        compiler_params=PARAMS,
        cost_estimate=pl.CostEstimate(flops=flops, bytes_accessed=slots * ROWS * B, transcendentals=0),
        name="grid",
    )(*args)
    return tuple(out) if last else out[0]


def two_parts(value):
    high = value.astype(jnp.bfloat16)
    return high, (value - high.astype(jnp.float32)).astype(jnp.bfloat16)


def image_kernel(acc_ref, mine_ref, other_ref, row_ref, col_ref, out_ref):
    s1 = mine_ref[0:1, :] + other_ref[0:1, :]
    s2 = mine_ref[8:9, :] + other_ref[8:9, :]
    factor = 2.5 * s1 / s2
    width = out_ref.shape[3]
    half = 2 * width
    done = []
    for t in range(NT_C):
        tiles = [[acc_ref.at[4 * t + 2 * pr + pc] for pr in range(2)] for pc in range(2)]
        weights = [[1.0 / (1.0 + factor * tile[:, :P_SIZE]) for tile in pair] for pair in tiles]
        for pol in range(POLS):
            cells = []
            for e in (1 + 2 * pol, 2 + 2 * pol):
                for pc in range(2):
                    strip = [
                        tiles[pc][pr][:, e * P_SIZE : (e + 1) * P_SIZE] * weights[pc][pr] for pr in range(2)
                    ]
                    cells.append(jnp.concatenate(strip, axis=1))
            high, low = two_parts(jnp.concatenate(cells, axis=0))
            both = jnp.dot(row_ref[...], high, preferred_element_type=jnp.float32)
            rest = jnp.dot(row_ref[:half], low, preferred_element_type=jnp.float32)
            done.append(both[:half] + both[half:] + rest)
    high, low = two_parts(jnp.concatenate(done, axis=0))
    both = jnp.dot(high, col_ref[...], preferred_element_type=jnp.float32)
    rest = jnp.dot(low, col_ref[:, : 2 * G], preferred_element_type=jnp.float32)
    done = both[:, : 2 * G] + both[:, 2 * G :] + rest
    for t in range(NT_C):
        for pol in range(POLS):
            at = (t * POLS + pol) * half
            real, imag = done[at : at + width], done[at + width : at + half]
            out_ref[pol, 0, t] = real[:, :G] + imag[:, G:]
            out_ref[pol, 1, t] = imag[:, :G] - real[:, G:]


def make_image(acc, mine, other, row_table, col_table, width):
    return pl.pallas_call(
        image_kernel,
        out_shape=jax.ShapeDtypeStruct((POLS, 2, NT_C, width, G), jnp.float32),
        in_specs=[VMEM] * 5,
        out_specs=VMEM,
        compiler_params=PARAMS,
        name="image",
    )(acc, mine, other, row_table, col_table)


def dft_tables():
    index = np.arange(G)
    phase = (index[:, None] * index[None, :] % G) * (2.0 * math.pi / G)
    return np.cos(phase).astype(np.float32), np.sin(phase).astype(np.float32)


def np_parts(table, axis):
    high = table.astype(ml_dtypes.bfloat16)
    low = (table - high.astype(np.float32)).astype(ml_dtypes.bfloat16)
    return np.concatenate([high, low], axis=axis)


def image_tables(n_tm):
    cosine, sine = dft_tables()
    rows = []
    for cos_part, sin_part in zip(np.split(cosine, n_tm, axis=1), np.split(sine, n_tm, axis=1)):
        rows.append(np_parts(np.block([[cos_part, -sin_part], [sin_part, cos_part]]).T, 0))
    return np.stack(rows), np_parts(np.concatenate([cosine, sine], axis=1) / G, 1)


def by_gather(packed, n_tm):
    order = list(range(0, n_tm, 2)) + list(range(1, n_tm, 2))[::-1]
    up = [(order[i], order[(i + 1) % n_tm]) for i in range(n_tm)]
    down = [(b, a) for a, b in up]

    def both_ways(pair):
        return [lax.ppermute(pair[0], "tm", up), lax.ppermute(pair[1], "tm", down)]

    leading = both_ways(packed)
    trailing = both_ways(packed[::-1])
    acc = add_blocks(None, packed)
    for step in range(2, n_tm // 2 + 1):
        following = both_ways(leading)
        acc = add_blocks(acc, leading)
        acc, *trailing = lax.optimization_barrier((acc, *trailing))
        leading = following
        following = both_ways(trailing) if step < n_tm // 2 else None
        acc = add_blocks(acc, trailing)
        trailing = following
    acc = add_blocks(acc, leading[:1])
    return add_blocks(acc, leading[1:], last=True)


def rest_by_rows(acc, cosine, sine):
    grid = acc.reshape(NT_C, 2, 2, P_SIZE, GRIDS, P_SIZE)
    flat = jnp.transpose(grid, (4, 0, 1, 5, 2, 3)).reshape(GRIDS, NT_C * G, G)
    owned = lax.psum_scatter(flat, "tm", scatter_dimension=1, tiled=True)
    dens = owned[0]
    totals = lax.psum((jnp.sum(dens), jnp.sum(dens * dens)), ("tm", "tile"))
    factor = 2.5 * totals[0] / totals[1]
    weighted = owned[1:] / (1.0 + factor * dens[None])
    weighted = weighted.reshape(POLS, 2, dens.shape[0], G)
    real, imag = weighted[:, 0], weighted[:, 1]

    def rows(a, b):
        return jnp.einsum("prj,jn->prn", a, b, precision=HIGH)

    done = jnp.stack([rows(real, cosine) + rows(imag, sine), rows(imag, cosine) - rows(real, sine)], axis=1)
    width = G // lax.axis_size("tm")
    every_row = lax.all_gather(done, "tm", axis=2, tiled=True)
    columns = lax.dynamic_slice_in_dim(every_row, lax.axis_index("tm") * width, width, 3)
    columns = columns.reshape(POLS, 2, NT_C, G, width)
    real, imag = columns[:, 0], columns[:, 1]

    def cols(a, b):
        return jnp.einsum("mi,ptic->ptcm", a, b, precision=HIGH)

    out = jnp.stack([cols(cosine, real) + cols(sine, imag), cols(cosine, imag) - cols(sine, real)], axis=1)
    return out / G


def body(vis_data, vis_weight, kernel_taps, offsets, block_patch, block_count):
    slots = vis_weight.shape[1]
    n_tm = lax.axis_size("tm")
    pieces = (slots // 2, slots - slots // 2)
    packed = pack(pieces, vis_data[0], vis_weight[0], kernel_taps[0], offsets[0], block_patch, block_count)
    if n_tm > 8:
        cosine, sine = dft_tables()
        return rest_by_rows(add_blocks(None, packed), jnp.asarray(cosine), jnp.asarray(sine))
    acc, mine = by_gather(packed, n_tm)
    n_tile = lax.axis_size("tile")
    other = lax.ppermute(mine, "tile", [(i, n_tile - 1 - i) for i in range(n_tile)])
    row_tables, col_table = image_tables(n_tm)
    row_table = lax.dynamic_index_in_dim(jnp.asarray(row_tables), lax.axis_index("tm"), 0, keepdims=False)
    return make_image(acc, mine, other, row_table, jnp.asarray(col_table), G // n_tm)


def solution(mesh):
    return jax.shard_map(
        body,
        mesh=mesh,
        in_specs=(
            P(("grp", "tile"), "tm", None, None),
            P(("grp", "tile"), "tm", None),
            P(("grp", "tile"), "tm", None, None, None),
            P(("grp", "tile"), "tm", None, None),
            P(("grp", "tile"), "tm"),
            P(("grp", "tile"), "tm"),
        ),
        out_specs=P(None, None, ("grp", "tile"), "tm", None),
        check_vma=False,
    )
```

```python
import math

import jax
import jax.numpy as jnp
import ml_dtypes
import numpy as np
from jax import lax
from jax.experimental import pallas as pl
from jax.experimental.pallas import tpu as pltpu
from jax.sharding import PartitionSpec as P

G = 256
P_SIZE = 128
K = 8
B = 256
POLS = 2
NT_C = 2
PATCHES = 4 * NT_C
GRIDS = 1 + 2 * POLS
X_ROW = 2 * K
OFF_ROW = X_ROW + GRIDS
ID_ROW = OFF_ROW + 2
ROWS = ID_ROW + 1
COUNT_LANE = 128
HIGH = lax.Precision.HIGHEST
VMEM = pl.BlockSpec(memory_space=pltpu.VMEM)
PARAMS = pltpu.CompilerParams(vmem_limit_bytes=20 * 1024 * 1024)


def pack_kernel(pieces, vis_hbm, weight_hbm, taps_hbm, offs_hbm, patch_hbm, count_ref, *refs):
    outs, scratch = refs[: len(pieces)], refs[len(pieces) :]
    vis_ref, weight_ref, taps_ref, offs_ref, patch_ref, sems = scratch
    pairs = (
        (offs_hbm, offs_ref),
        (taps_hbm, taps_ref),
        (weight_hbm, weight_ref),
        (vis_hbm, vis_ref),
        (patch_hbm, patch_ref),
    )
    copies = [pltpu.make_async_copy(a, b, sems.at[i]) for i, (a, b) in enumerate(pairs)]
    for copy in copies:
        copy.start()
    places = []
    base = 0
    for out_ref, size in zip(outs, pieces):
        places += [(out_ref, j, base + j) for j in range(size)]
        base += size
    copies[0].wait()
    copies[1].wait()
    for out_ref, j, at in places:
        for side in range(2):
            off = offs_ref[at, side : side + 1, :]
            taps = taps_ref[at, side]
            for bit in range(3):
                moved = pltpu.roll(taps, 1 << bit, 0)
                turn = jnp.broadcast_to((off >> bit) & 1, taps.shape) == 1
                taps = jnp.where(turn, moved, taps)
            out_ref[j, side * K : (side + 1) * K, :] = taps
        out_ref[j, OFF_ROW:ID_ROW, :] = offs_ref[at].astype(jnp.float32)
    copies[2].wait()
    copies[3].wait()
    for out_ref, j, at in places:
        weight = weight_ref[at : at + 1, :]
        out_ref[j, X_ROW : X_ROW + 1, :] = weight
        out_ref[j, X_ROW + 1 : OFF_ROW, :] = weight * vis_ref[at]
    copies[4].wait()
    lane = lax.broadcasted_iota(jnp.int32, (1, B), 1)
    for out_ref, j, at in places:
        live = jnp.clip(count_ref[0, 0] - (at - j), 0, out_ref.shape[0])
        row = jnp.where(lane < COUNT_LANE, patch_ref[0, at], live)
        out_ref[j, ID_ROW:ROWS, :] = row.astype(jnp.float32)


def pack(pieces, vis, weight, taps, offs, patches, count):
    arrays = (vis, weight, taps, offs, patches)
    spaces = [pltpu.VMEM] * 4 + [pltpu.SMEM]
    hbm, smem = pl.BlockSpec(memory_space=pltpu.HBM), pl.BlockSpec(memory_space=pltpu.SMEM)
    return pl.pallas_call(
        lambda *refs: pack_kernel(pieces, *refs),
        out_shape=[jax.ShapeDtypeStruct((size, ROWS, B), jnp.float32) for size in pieces],
        in_specs=[hbm] * 5 + [smem],
        out_specs=[VMEM] * len(pieces),
        scratch_shapes=[space(a.shape, a.dtype) for space, a in zip(spaces, arrays)] + [pltpu.SemaphoreType.DMA((5,))],
        compiler_params=PARAMS,
        name="pack",
    )(*[pltpu.with_memory_space_constraint(a, pltpu.HBM) for a in arrays], count)


def spread(off):
    row = lax.broadcasted_iota(jnp.int32, (16, B), 0)
    gap = off.astype(jnp.int32) - row
    step = (gap + 15) >> 4
    inside = (step << 4) - gap < K
    return jnp.where(inside, step, -1).astype(jnp.float32).astype(jnp.bfloat16)


def block_factors(block, live):
    rows_u = jnp.concatenate([block[0:K]] * 2, axis=0)
    rows_v = jnp.concatenate([block[K : 2 * K]] * 2, axis=0)
    step_u = spread(block[OFF_ROW : OFF_ROW + 1])
    step_v = spread(block[OFF_ROW + 1 : OFF_ROW + 2])
    if live is not None:
        rows_v = jnp.where(live, rows_v, 0.0)
    rows_v = rows_v.astype(jnp.bfloat16)
    zero = jnp.zeros((16, B), jnp.bfloat16)
    steps = P_SIZE // 16
    right = jnp.concatenate([jnp.where(step_v == s, rows_v, zero) for s in range(steps)], axis=0)
    hits = [step_u == s for s in range(steps)]
    left = []
    for e in range(GRIDS):
        product = (rows_u * block[X_ROW + e : X_ROW + e + 1]).astype(jnp.bfloat16)
        left += [jnp.where(hit, product, zero) for hit in hits]
    return jnp.concatenate(left, axis=0), right


def add_some(buf_ref, acc_ref, first, count, unroll):
    waiting = None
    for i in range(unroll):
        j = first if i == 0 else jnp.minimum(first + i, buf_ref.shape[0] - 1)
        block = buf_ref[j]
        left, right = block_factors(block, None if i == 0 else first + i < count)
        patch = lax.dot_general(
            right, left, (((1,), (1,)), ((), ())), preferred_element_type=jnp.float32
        )
        if waiting is not None:
            acc_ref[waiting[0]] += waiting[1]
        waiting = block[ID_ROW:ROWS, 0:1][0, 0].astype(jnp.int32), patch
    acc_ref[waiting[0]] += waiting[1]


def grid_kernel(n, first, last, *refs):
    bufs = refs[:n]
    acc_ref = refs[n] if first else refs[n + 1]
    if first:
        acc_ref[...] = jnp.zeros_like(acc_ref)
    for buf_ref in bufs:
        count = buf_ref[0, ID_ROW:ROWS, COUNT_LANE : COUNT_LANE + 1][0, 0].astype(jnp.int32)

        tall = (count + 3) // 8

        def eight(step, _, buf_ref=buf_ref, count=count):
            add_some(buf_ref, acc_ref, 8 * step, count, 8)
            return 0

        lax.fori_loop(0, tall, eight, 0)

        @pl.when(count > 8 * tall)
        def _(buf_ref=buf_ref, count=count, tall=tall):
            add_some(buf_ref, acc_ref, 8 * tall, count, 4)

    if last:
        sums_ref = refs[-1]
        dens = acc_ref[:, :, :P_SIZE]
        for i, value in enumerate((dens, dens * dens)):
            part = jnp.sum(value.reshape(-1, 8, P_SIZE), axis=0)
            part = jnp.sum(jnp.sum(part, axis=0, keepdims=True), axis=1, keepdims=True)
            sums_ref[8 * i : 8 * i + 8, :] = jnp.broadcast_to(part, (8, P_SIZE))


def add_blocks(acc, bufs, last=False):
    first = acc is None
    n = len(bufs)
    slots = sum(buf.shape[0] for buf in bufs)
    out_shape = [jax.ShapeDtypeStruct((PATCHES, P_SIZE, GRIDS * P_SIZE), jnp.float32)]
    if last:
        out_shape.append(jax.ShapeDtypeStruct((16, P_SIZE), jnp.float32))
    args = list(bufs) + ([] if first else [acc])
    flops = 4 * slots * GRIDS * P_SIZE * P_SIZE * B
    out = pl.pallas_call(
        lambda *refs: grid_kernel(n, first, last, *refs),
        out_shape=out_shape,
        in_specs=[VMEM] * len(args),
        out_specs=[VMEM] * len(out_shape),
        input_output_aliases={} if first else {n: 0},
        compiler_params=PARAMS,
        cost_estimate=pl.CostEstimate(flops=flops, bytes_accessed=slots * ROWS * B, transcendentals=0),
        name="grid",
    )(*args)
    return tuple(out) if last else out[0]


def two_parts(value):
    high = value.astype(jnp.bfloat16)
    return high, (value - high.astype(jnp.float32)).astype(jnp.bfloat16)


def image_kernel(acc_ref, mine_ref, other_ref, row_ref, col_ref, out_ref):
    s1 = mine_ref[0:1, :] + other_ref[0:1, :]
    s2 = mine_ref[8:9, :] + other_ref[8:9, :]
    factor = 2.5 * s1 / s2
    width = out_ref.shape[3]
    half = 2 * width
    done = []
    for t in range(NT_C):
        tiles = [[acc_ref.at[4 * t + 2 * pr + pc] for pr in range(2)] for pc in range(2)]
        weights = [[1.0 / (1.0 + factor * tile[:, :P_SIZE]) for tile in pair] for pair in tiles]
        for pol in range(POLS):
            cells = []
            for e in (1 + 2 * pol, 2 + 2 * pol):
                for pc in range(2):
                    strip = [
                        tiles[pc][pr][:, e * P_SIZE : (e + 1) * P_SIZE] * weights[pc][pr] for pr in range(2)
                    ]
                    cells.append(jnp.concatenate(strip, axis=1))
            high, low = two_parts(jnp.concatenate(cells, axis=0))
            both = jnp.dot(row_ref[...], high, preferred_element_type=jnp.float32)
            rest = jnp.dot(row_ref[:half], low, preferred_element_type=jnp.float32)
            done.append(both[:half] + both[half:] + rest)
    high, low = two_parts(jnp.concatenate(done, axis=0))
    both = jnp.dot(high, col_ref[...], preferred_element_type=jnp.float32)
    rest = jnp.dot(low, col_ref[:, : 2 * G], preferred_element_type=jnp.float32)
    done = both[:, : 2 * G] + both[:, 2 * G :] + rest
    for t in range(NT_C):
        for pol in range(POLS):
            at = (t * POLS + pol) * half
            real, imag = done[at : at + width], done[at + width : at + half]
            out_ref[pol, 0, t] = real[:, :G] + imag[:, G:]
            out_ref[pol, 1, t] = imag[:, :G] - real[:, G:]


def make_image(acc, mine, other, row_table, col_table, width):
    return pl.pallas_call(
        image_kernel,
        out_shape=jax.ShapeDtypeStruct((POLS, 2, NT_C, width, G), jnp.float32),
        in_specs=[VMEM] * 5,
        out_specs=VMEM,
        compiler_params=PARAMS,
        name="image",
    )(acc, mine, other, row_table, col_table)


def dft_tables():
    index = np.arange(G)
    phase = (index[:, None] * index[None, :] % G) * (2.0 * math.pi / G)
    return np.cos(phase).astype(np.float32), np.sin(phase).astype(np.float32)


def np_parts(table, axis):
    high = table.astype(ml_dtypes.bfloat16)
    low = (table - high.astype(np.float32)).astype(ml_dtypes.bfloat16)
    return np.concatenate([high, low], axis=axis)


def image_tables(n_tm):
    cosine, sine = dft_tables()
    rows = []
    for cos_part, sin_part in zip(np.split(cosine, n_tm, axis=1), np.split(sine, n_tm, axis=1)):
        rows.append(np_parts(np.block([[cos_part, -sin_part], [sin_part, cos_part]]).T, 0))
    return np.stack(rows), np_parts(np.concatenate([cosine, sine], axis=1) / G, 1)


def by_gather(packed, n_tm):
    order = list(range(0, n_tm, 2)) + list(range(1, n_tm, 2))[::-1]
    up = [(order[i], order[(i + 1) % n_tm]) for i in range(n_tm)]
    down = [(b, a) for a, b in up]

    def both_ways(pair):
        return [lax.ppermute(pair[0], "tm", up), lax.ppermute(pair[1], "tm", down)]

    leading = both_ways(packed)
    trailing = both_ways(packed[::-1])
    acc = add_blocks(None, packed)
    for step in range(2, n_tm // 2 + 1):
        following = both_ways(leading)
        acc = add_blocks(acc, leading)
        acc, *trailing = lax.optimization_barrier((acc, *trailing))
        leading = following
        following = both_ways(trailing) if step < n_tm // 2 else None
        acc = add_blocks(acc, trailing)
        trailing = following
    acc = add_blocks(acc, leading[:1])
    return add_blocks(acc, leading[1:], last=True)


def rest_by_rows(acc, cosine, sine):
    grid = acc.reshape(NT_C, 2, 2, P_SIZE, GRIDS, P_SIZE)
    flat = jnp.transpose(grid, (4, 0, 1, 5, 2, 3)).reshape(GRIDS, NT_C * G, G)
    owned = lax.psum_scatter(flat, "tm", scatter_dimension=1, tiled=True)
    dens = owned[0]
    totals = lax.psum((jnp.sum(dens), jnp.sum(dens * dens)), ("tm", "tile"))
    factor = 2.5 * totals[0] / totals[1]
    weighted = owned[1:] / (1.0 + factor * dens[None])
    weighted = weighted.reshape(POLS, 2, dens.shape[0], G)
    real, imag = weighted[:, 0], weighted[:, 1]

    def rows(a, b):
        return jnp.einsum("prj,jn->prn", a, b, precision=HIGH)

    done = jnp.stack([rows(real, cosine) + rows(imag, sine), rows(imag, cosine) - rows(real, sine)], axis=1)
    width = G // lax.axis_size("tm")
    every_row = lax.all_gather(done, "tm", axis=2, tiled=True)
    columns = lax.dynamic_slice_in_dim(every_row, lax.axis_index("tm") * width, width, 3)
    columns = columns.reshape(POLS, 2, NT_C, G, width)
    real, imag = columns[:, 0], columns[:, 1]

    def cols(a, b):
        return jnp.einsum("mi,ptic->ptcm", a, b, precision=HIGH)

    out = jnp.stack([cols(cosine, real) + cols(sine, imag), cols(cosine, imag) - cols(sine, real)], axis=1)
    return out / G


def body(vis_data, vis_weight, kernel_taps, offsets, block_patch, block_count):
    slots = vis_weight.shape[1]
    n_tm = lax.axis_size("tm")
    pieces = (slots // 2, slots - slots // 2)
    packed = pack(pieces, vis_data[0], vis_weight[0], kernel_taps[0], offsets[0], block_patch, block_count)
    if n_tm > 8:
        cosine, sine = dft_tables()
        return rest_by_rows(add_blocks(None, packed), jnp.asarray(cosine), jnp.asarray(sine))
    acc, mine = by_gather(packed, n_tm)
    n_tile = lax.axis_size("tile")
    other = lax.ppermute(mine, "tile", [(i, n_tile - 1 - i) for i in range(n_tile)])
    row_tables, col_table = image_tables(n_tm)
    row_table = lax.dynamic_index_in_dim(jnp.asarray(row_tables), lax.axis_index("tm"), 0, keepdims=False)
    return make_image(acc, mine, other, row_table, jnp.asarray(col_table), G // n_tm)


def solution(mesh):
    return jax.shard_map(
        body,
        mesh=mesh,
        in_specs=(
            P(("grp", "tile"), "tm", None, None),
            P(("grp", "tile"), "tm", None),
            P(("grp", "tile"), "tm", None, None, None),
            P(("grp", "tile"), "tm", None, None),
            P(("grp", "tile"), "tm"),
            P(("grp", "tile"), "tm"),
        ),
        out_specs=P(None, None, ("grp", "tile"), "tm", None),
        check_vma=False,
    )
```

```python
import math

import jax
import jax.numpy as jnp
import ml_dtypes
import numpy as np
from jax import lax
from jax.experimental import pallas as pl
from jax.experimental.pallas import tpu as pltpu
from jax.sharding import PartitionSpec as P

G = 256
P_SIZE = 128
K = 8
B = 256
POLS = 2
NT_C = 2
PATCHES = 4 * NT_C
GRIDS = 1 + 2 * POLS
X_ROW = 2 * K
OFF_ROW = X_ROW + GRIDS
ID_ROW = OFF_ROW + 2
ROWS = ID_ROW + 1
COUNT_LANE = 128
HIGH = lax.Precision.HIGHEST
VMEM = pl.BlockSpec(memory_space=pltpu.VMEM)
PARAMS = pltpu.CompilerParams(vmem_limit_bytes=20 * 1024 * 1024)


def pack_kernel(pieces, vis_hbm, weight_hbm, taps_hbm, offs_hbm, patch_hbm, count_ref, *refs):
    outs, scratch = refs[: len(pieces)], refs[len(pieces) :]
    vis_ref, weight_ref, taps_ref, offs_ref, patch_ref, sems = scratch
    pairs = (
        (offs_hbm, offs_ref),
        (taps_hbm, taps_ref),
        (weight_hbm, weight_ref),
        (vis_hbm, vis_ref),
        (patch_hbm, patch_ref),
    )
    copies = [pltpu.make_async_copy(a, b, sems.at[i]) for i, (a, b) in enumerate(pairs)]
    for copy in copies:
        copy.start()
    places = []
    base = 0
    for out_ref, size in zip(outs, pieces):
        places += [(out_ref, j, base + j) for j in range(size)]
        base += size
    copies[0].wait()
    copies[1].wait()
    for out_ref, j, at in places:
        for side in range(2):
            off = offs_ref[at, side : side + 1, :]
            taps = taps_ref[at, side]
            for bit in range(3):
                moved = pltpu.roll(taps, 1 << bit, 0)
                turn = jnp.broadcast_to((off >> bit) & 1, taps.shape) == 1
                taps = jnp.where(turn, moved, taps)
            out_ref[j, side * K : (side + 1) * K, :] = taps
        out_ref[j, OFF_ROW:ID_ROW, :] = offs_ref[at].astype(jnp.float32)
    copies[2].wait()
    copies[3].wait()
    for out_ref, j, at in places:
        weight = weight_ref[at : at + 1, :]
        out_ref[j, X_ROW : X_ROW + 1, :] = weight
        out_ref[j, X_ROW + 1 : OFF_ROW, :] = weight * vis_ref[at]
    copies[4].wait()
    lane = lax.broadcasted_iota(jnp.int32, (1, B), 1)
    for out_ref, j, at in places:
        live = jnp.clip(count_ref[0, 0] - (at - j), 0, out_ref.shape[0])
        row = jnp.where(lane < COUNT_LANE, patch_ref[0, at], live)
        out_ref[j, ID_ROW:ROWS, :] = row.astype(jnp.float32)


def pack(pieces, vis, weight, taps, offs, patches, count):
    arrays = (vis, weight, taps, offs, patches)
    spaces = [pltpu.VMEM] * 4 + [pltpu.SMEM]
    hbm, smem = pl.BlockSpec(memory_space=pltpu.HBM), pl.BlockSpec(memory_space=pltpu.SMEM)
    return pl.pallas_call(
        lambda *refs: pack_kernel(pieces, *refs),
        out_shape=[jax.ShapeDtypeStruct((size, ROWS, B), jnp.float32) for size in pieces],
        in_specs=[hbm] * 5 + [smem],
        out_specs=[VMEM] * len(pieces),
        scratch_shapes=[space(a.shape, a.dtype) for space, a in zip(spaces, arrays)] + [pltpu.SemaphoreType.DMA((5,))],
        compiler_params=PARAMS,
        name="pack",
    )(*[pltpu.with_memory_space_constraint(a, pltpu.HBM) for a in arrays], count)


def spread(off):
    row = lax.broadcasted_iota(jnp.int32, (16, B), 0)
    gap = off.astype(jnp.int32) - row
    step = (gap + 15) >> 4
    inside = (step << 4) - gap < K
    return jnp.where(inside, step, -1).astype(jnp.float32).astype(jnp.bfloat16)


def block_factors(block, live):
    rows_u = jnp.concatenate([block[0:K]] * 2, axis=0)
    rows_v = jnp.concatenate([block[K : 2 * K]] * 2, axis=0)
    step_u = spread(block[OFF_ROW : OFF_ROW + 1])
    step_v = spread(block[OFF_ROW + 1 : OFF_ROW + 2])
    if live is not None:
        rows_v = jnp.where(live, rows_v, 0.0)
    rows_v = rows_v.astype(jnp.bfloat16)
    zero = jnp.zeros((16, B), jnp.bfloat16)
    steps = P_SIZE // 16
    right = jnp.concatenate([jnp.where(step_v == s, rows_v, zero) for s in range(steps)], axis=0)
    hits = [step_u == s for s in range(steps)]
    left = []
    for e in range(GRIDS):
        product = (rows_u * block[X_ROW + e : X_ROW + e + 1]).astype(jnp.bfloat16)
        left += [jnp.where(hit, product, zero) for hit in hits]
    return jnp.concatenate(left, axis=0), right


def add_some(buf_ref, acc_ref, first, count, unroll):
    waiting = None
    for i in range(unroll):
        j = first if i == 0 else jnp.minimum(first + i, buf_ref.shape[0] - 1)
        block = buf_ref[j]
        left, right = block_factors(block, None if i == 0 else first + i < count)
        patch = lax.dot_general(
            right, left, (((1,), (1,)), ((), ())), preferred_element_type=jnp.float32
        )
        if waiting is not None:
            acc_ref[waiting[0]] += waiting[1]
        waiting = block[ID_ROW:ROWS, 0:1][0, 0].astype(jnp.int32), patch
    acc_ref[waiting[0]] += waiting[1]


def grid_kernel(n, first, last, *refs):
    bufs = refs[:n]
    acc_ref = refs[n] if first else refs[n + 1]
    if first:
        acc_ref[...] = jnp.zeros_like(acc_ref)
    for buf_ref in bufs:
        count = buf_ref[0, ID_ROW:ROWS, COUNT_LANE : COUNT_LANE + 1][0, 0].astype(jnp.int32)

        tall = (count + 3) // 8

        def eight(step, _, buf_ref=buf_ref, count=count):
            add_some(buf_ref, acc_ref, 8 * step, count, 8)
            return 0

        lax.fori_loop(0, tall, eight, 0)

        @pl.when(count > 8 * tall)
        def _(buf_ref=buf_ref, count=count, tall=tall):
            add_some(buf_ref, acc_ref, 8 * tall, count, 4)

    if last:
        sums_ref = refs[-1]
        dens = acc_ref[:, :, :P_SIZE]
        for i, value in enumerate((dens, dens * dens)):
            part = jnp.sum(value.reshape(-1, 8, P_SIZE), axis=0)
            part = jnp.sum(jnp.sum(part, axis=0, keepdims=True), axis=1, keepdims=True)
            sums_ref[8 * i : 8 * i + 8, :] = jnp.broadcast_to(part, (8, P_SIZE))


def add_blocks(acc, bufs, last=False):
    first = acc is None
    n = len(bufs)
    slots = sum(buf.shape[0] for buf in bufs)
    out_shape = [jax.ShapeDtypeStruct((PATCHES, P_SIZE, GRIDS * P_SIZE), jnp.float32)]
    if last:
        out_shape.append(jax.ShapeDtypeStruct((16, P_SIZE), jnp.float32))
    args = list(bufs) + ([] if first else [acc])
    flops = 4 * slots * GRIDS * P_SIZE * P_SIZE * B
    out = pl.pallas_call(
        lambda *refs: grid_kernel(n, first, last, *refs),
        out_shape=out_shape,
        in_specs=[VMEM] * len(args),
        out_specs=[VMEM] * len(out_shape),
        input_output_aliases={} if first else {n: 0},
        compiler_params=PARAMS,
        cost_estimate=pl.CostEstimate(flops=flops, bytes_accessed=slots * ROWS * B, transcendentals=0),
        name="grid",
    )(*args)
    return tuple(out) if last else out[0]


def two_parts(value):
    high = value.astype(jnp.bfloat16)
    return high, (value - high.astype(jnp.float32)).astype(jnp.bfloat16)


def image_kernel(acc_ref, mine_ref, other_ref, row_ref, col_ref, out_ref):
    s1 = mine_ref[0:1, :] + other_ref[0:1, :]
    s2 = mine_ref[8:9, :] + other_ref[8:9, :]
    factor = 2.5 * s1 / s2
    width = out_ref.shape[3]
    half = 2 * width
    done = []
    for t in range(NT_C):
        tiles = [[acc_ref.at[4 * t + 2 * pr + pc] for pr in range(2)] for pc in range(2)]
        weights = [[1.0 / (1.0 + factor * tile[:, :P_SIZE]) for tile in pair] for pair in tiles]
        for pol in range(POLS):
            cells = []
            for e in (1 + 2 * pol, 2 + 2 * pol):
                for pc in range(2):
                    strip = [
                        tiles[pc][pr][:, e * P_SIZE : (e + 1) * P_SIZE] * weights[pc][pr] for pr in range(2)
                    ]
                    cells.append(jnp.concatenate(strip, axis=1))
            high, low = two_parts(jnp.concatenate(cells, axis=0))
            both = jnp.dot(row_ref[...], high, preferred_element_type=jnp.float32)
            rest = jnp.dot(row_ref[:half], low, preferred_element_type=jnp.float32)
            done.append(both[:half] + both[half:] + rest)
    high, low = two_parts(jnp.concatenate(done, axis=0))
    both = jnp.dot(high, col_ref[...], preferred_element_type=jnp.float32)
    rest = jnp.dot(low, col_ref[:, : 2 * G], preferred_element_type=jnp.float32)
    done = both[:, : 2 * G] + both[:, 2 * G :] + rest
    for t in range(NT_C):
        for pol in range(POLS):
            at = (t * POLS + pol) * half
            real, imag = done[at : at + width], done[at + width : at + half]
            out_ref[pol, 0, t] = real[:, :G] + imag[:, G:]
            out_ref[pol, 1, t] = imag[:, :G] - real[:, G:]


def make_image(acc, mine, other, row_table, col_table, width):
    return pl.pallas_call(
        image_kernel,
        out_shape=jax.ShapeDtypeStruct((POLS, 2, NT_C, width, G), jnp.float32),
        in_specs=[VMEM] * 5,
        out_specs=VMEM,
        compiler_params=PARAMS,
        name="image",
    )(acc, mine, other, row_table, col_table)


def dft_tables():
    index = np.arange(G)
    phase = (index[:, None] * index[None, :] % G) * (2.0 * math.pi / G)
    return np.cos(phase).astype(np.float32), np.sin(phase).astype(np.float32)


def np_parts(table, axis):
    high = table.astype(ml_dtypes.bfloat16)
    low = (table - high.astype(np.float32)).astype(ml_dtypes.bfloat16)
    return np.concatenate([high, low], axis=axis)


def image_tables(n_tm):
    cosine, sine = dft_tables()
    rows = []
    for cos_part, sin_part in zip(np.split(cosine, n_tm, axis=1), np.split(sine, n_tm, axis=1)):
        rows.append(np_parts(np.block([[cos_part, -sin_part], [sin_part, cos_part]]).T, 0))
    return np.stack(rows), np_parts(np.concatenate([cosine, sine], axis=1) / G, 1)


def by_gather(packed, n_tm, n_tile):
    order = list(range(0, n_tm, 2)) + list(range(1, n_tm, 2))[::-1]
    ways = [[], []]
    for i in range(n_tm):
        for tile in range(n_tile):
            here, there = (n_tile * order[k] + tile for k in (i, (i + 1) % n_tm))
            ways[tile % 2].append((here, there))
            ways[1 - tile % 2].append((there, here))

    def both_ways(pair):
        return [lax.ppermute(a, ("tm", "tile"), way) for a, way in zip(pair, ways)]

    leading = both_ways(packed)
    trailing = both_ways(packed[::-1])
    acc = add_blocks(None, packed)
    for step in range(2, n_tm // 2 + 1):
        following = both_ways(leading)
        acc = add_blocks(acc, leading)
        acc, *trailing = lax.optimization_barrier((acc, *trailing))
        leading = following
        following = both_ways(trailing) if step < n_tm // 2 else None
        acc = add_blocks(acc, trailing)
        trailing = following
    acc = add_blocks(acc, leading[:1])
    return add_blocks(acc, leading[1:], last=True)


def rest_by_rows(acc, cosine, sine):
    grid = acc.reshape(NT_C, 2, 2, P_SIZE, GRIDS, P_SIZE)
    flat = jnp.transpose(grid, (4, 0, 1, 5, 2, 3)).reshape(GRIDS, NT_C * G, G)
    owned = lax.psum_scatter(flat, "tm", scatter_dimension=1, tiled=True)
    dens = owned[0]
    totals = lax.psum((jnp.sum(dens), jnp.sum(dens * dens)), ("tm", "tile"))
    factor = 2.5 * totals[0] / totals[1]
    weighted = owned[1:] / (1.0 + factor * dens[None])
    weighted = weighted.reshape(POLS, 2, dens.shape[0], G)
    real, imag = weighted[:, 0], weighted[:, 1]

    def rows(a, b):
        return jnp.einsum("prj,jn->prn", a, b, precision=HIGH)

    done = jnp.stack([rows(real, cosine) + rows(imag, sine), rows(imag, cosine) - rows(real, sine)], axis=1)
    width = G // lax.axis_size("tm")
    every_row = lax.all_gather(done, "tm", axis=2, tiled=True)
    columns = lax.dynamic_slice_in_dim(every_row, lax.axis_index("tm") * width, width, 3)
    columns = columns.reshape(POLS, 2, NT_C, G, width)
    real, imag = columns[:, 0], columns[:, 1]

    def cols(a, b):
        return jnp.einsum("mi,ptic->ptcm", a, b, precision=HIGH)

    out = jnp.stack([cols(cosine, real) + cols(sine, imag), cols(cosine, imag) - cols(sine, real)], axis=1)
    return out / G


def body(vis_data, vis_weight, kernel_taps, offsets, block_patch, block_count):
    slots = vis_weight.shape[1]
    n_tm = lax.axis_size("tm")
    pieces = (slots // 2, slots - slots // 2)
    packed = pack(pieces, vis_data[0], vis_weight[0], kernel_taps[0], offsets[0], block_patch, block_count)
    if n_tm > 8:
        cosine, sine = dft_tables()
        return rest_by_rows(add_blocks(None, packed), jnp.asarray(cosine), jnp.asarray(sine))
    n_tile = lax.axis_size("tile")
    acc, mine = by_gather(packed, n_tm, n_tile)
    other = lax.ppermute(mine, "tile", [(i, n_tile - 1 - i) for i in range(n_tile)])
    row_tables, col_table = image_tables(n_tm)
    row_table = lax.dynamic_index_in_dim(jnp.asarray(row_tables), lax.axis_index("tm"), 0, keepdims=False)
    return make_image(acc, mine, other, row_table, jnp.asarray(col_table), G // n_tm)


def solution(mesh):
    return jax.shard_map(
        body,
        mesh=mesh,
        in_specs=(
            P(("grp", "tile"), "tm", None, None),
            P(("grp", "tile"), "tm", None),
            P(("grp", "tile"), "tm", None, None, None),
            P(("grp", "tile"), "tm", None, None),
            P(("grp", "tile"), "tm"),
            P(("grp", "tile"), "tm"),
        ),
        out_specs=P(None, None, ("grp", "tile"), "tm", None),
        check_vma=False,
    )
```

```python
import math

import jax
import jax.numpy as jnp
import ml_dtypes
import numpy as np
from jax import lax
from jax.experimental import pallas as pl
from jax.experimental.pallas import tpu as pltpu
from jax.sharding import PartitionSpec as P

G = 256
P_SIZE = 128
K = 8
B = 256
POLS = 2
NT_C = 2
PATCHES = 4 * NT_C
GRIDS = 1 + 2 * POLS
LANES = 128
HALVES = B // LANES
AUX = GRIDS + 2
TAP_ROWS = 2 * HALVES * K
ID_START = TAP_ROWS + AUX * HALVES
PIECE_ROWS = ID_START + 1
COUNT_LANE = 64
HIGH = lax.Precision.HIGHEST
VMEM = pl.BlockSpec(memory_space=pltpu.VMEM)
PARAMS = pltpu.CompilerParams(vmem_limit_bytes=20 * 1024 * 1024)


def half_lanes(half):
    return slice(half * LANES, (half + 1) * LANES)


def pack_kernel(pieces, vis_hbm, weight_hbm, taps_hbm, offs_hbm, patch_hbm, count_ref, *refs):
    outs, scratch = refs[: len(pieces)], refs[len(pieces) :]
    vis_ref, weight_ref, taps_ref, offs_ref, patch_ref, sems = scratch
    pairs = (
        (offs_hbm, offs_ref),
        (taps_hbm, taps_ref),
        (weight_hbm, weight_ref),
        (vis_hbm, vis_ref),
        (patch_hbm, patch_ref),
    )
    copies = [pltpu.make_async_copy(a, b, sems.at[i]) for i, (a, b) in enumerate(pairs)]
    for copy in copies:
        copy.start()
    bases = [sum(pieces[:i]) for i in range(len(pieces))]
    copies[0].wait()
    copies[1].wait()
    for out_ref, n, base in zip(outs, pieces, bases):
        for j in range(n):
            for side in range(2):
                off = offs_ref[base + j, side : side + 1, :]
                taps = taps_ref[base + j, side]
                for bit in range(3):
                    moved = pltpu.roll(taps, 1 << bit, 0)
                    turn = jnp.broadcast_to((off >> bit) & 1, taps.shape) == 1
                    taps = jnp.where(turn, moved, taps)
                for half in range(HALVES):
                    at = j * TAP_ROWS + (side * HALVES + half) * K
                    out_ref[at : at + K, :] = taps[:, half_lanes(half)]
    copies[2].wait()
    copies[3].wait()
    copies[4].wait()
    for out_ref, n, base in zip(outs, pieces, bases):
        for half in range(HALVES):
            lanes = half_lanes(half)
            weight = weight_ref[base : base + n, lanes]
            kinds = [weight] + [weight * vis_ref[base : base + n, m, lanes] for m in range(2 * POLS)]
            kinds += [offs_ref[base : base + n, side, lanes].astype(jnp.float32) for side in range(2)]
            for kind, rows in enumerate(kinds):
                at = n * (TAP_ROWS + kind * HALVES + half)
                out_ref[at : at + n, :] = rows
        lane = lax.broadcasted_iota(jnp.int32, (1, LANES), 1)
        live = jnp.clip(count_ref[0, 0] - base, 0, n)
        for j in range(n):
            row = jnp.where(lane < COUNT_LANE, patch_ref[0, base + j], live)
            out_ref[n * ID_START + j : n * ID_START + j + 1, :] = row.astype(jnp.float32)


def pack(pieces, vis, weight, taps, offs, patches, count):
    arrays = (vis, weight, taps, offs, patches)
    spaces = [pltpu.VMEM] * 4 + [pltpu.SMEM]
    hbm, smem = pl.BlockSpec(memory_space=pltpu.HBM), pl.BlockSpec(memory_space=pltpu.SMEM)
    return pl.pallas_call(
        lambda *refs: pack_kernel(pieces, *refs),
        out_shape=[jax.ShapeDtypeStruct((n * PIECE_ROWS, LANES), jnp.float32) for n in pieces],
        in_specs=[hbm] * 5 + [smem],
        out_specs=[VMEM] * len(pieces),
        scratch_shapes=[space(a.shape, a.dtype) for space, a in zip(spaces, arrays)] + [pltpu.SemaphoreType.DMA((5,))],
        compiler_params=PARAMS,
        name="pack",
    )(*[pltpu.with_memory_space_constraint(a, pltpu.HBM) for a in arrays], count)


def spread(off):
    row = lax.broadcasted_iota(jnp.int32, (16, B), 0)
    gap = off.astype(jnp.int32) - row
    step = (gap + 15) >> 4
    inside = (step << 4) - gap < K
    return jnp.where(inside, step, -1).astype(jnp.float32).astype(jnp.bfloat16)


def slot_taps(buf_ref, j, side):
    halves = []
    for half in range(HALVES):
        at = pl.multiple_of(j * TAP_ROWS, K) + (side * HALVES + half) * K
        halves.append(buf_ref[pl.ds(at, K), :])
    return jnp.concatenate([jnp.concatenate(halves, axis=1)] * 2, axis=0)


def slot_row(buf_ref, n, j, kind):
    at = [n * (TAP_ROWS + kind * HALVES + half) + j for half in range(HALVES)]
    return jnp.concatenate([buf_ref[pl.ds(r, 1), :] for r in at], axis=1)


def block_factors(buf_ref, n, j, live):
    rows_u = slot_taps(buf_ref, j, 0)
    rows_v = slot_taps(buf_ref, j, 1)
    step_u = spread(slot_row(buf_ref, n, j, GRIDS))
    step_v = spread(slot_row(buf_ref, n, j, GRIDS + 1))
    if live is not None:
        rows_v = jnp.where(live, rows_v, 0.0)
    rows_v = rows_v.astype(jnp.bfloat16)
    zero = jnp.zeros((16, B), jnp.bfloat16)
    steps = P_SIZE // 16
    right = jnp.concatenate([jnp.where(step_v == s, rows_v, zero) for s in range(steps)], axis=0)
    hits = [step_u == s for s in range(steps)]
    left = []
    for e in range(GRIDS):
        product = (rows_u * slot_row(buf_ref, n, j, e)).astype(jnp.bfloat16)
        left += [jnp.where(hit, product, zero) for hit in hits]
    return jnp.concatenate(left, axis=0), right


def add_some(buf_ref, acc_ref, first, count, unroll):
    n = buf_ref.shape[0] // PIECE_ROWS
    waiting = None
    for i in range(unroll):
        j = first if i == 0 else jnp.minimum(first + i, n - 1)
        left, right = block_factors(buf_ref, n, j, None if i == 0 else first + i < count)
        patch = lax.dot_general(
            right, left, (((1,), (1,)), ((), ())), preferred_element_type=jnp.float32
        )
        if waiting is not None:
            acc_ref[waiting[0]] += waiting[1]
        waiting = buf_ref[pl.ds(n * ID_START + j, 1), 0:1][0, 0].astype(jnp.int32), patch
    acc_ref[waiting[0]] += waiting[1]


def grid_kernel(n, first, last, *refs):
    bufs = refs[:n]
    acc_ref = refs[n] if first else refs[n + 1]
    if first:
        acc_ref[...] = jnp.zeros_like(acc_ref)
    for buf_ref in bufs:
        at = buf_ref.shape[0] // PIECE_ROWS * ID_START
        count = buf_ref[at : at + 1, COUNT_LANE : COUNT_LANE + 1][0, 0].astype(jnp.int32)
        tall = (count + 3) // 8

        def eight(step, _, buf_ref=buf_ref, count=count):
            add_some(buf_ref, acc_ref, 8 * step, count, 8)
            return 0

        lax.fori_loop(0, tall, eight, 0)

        @pl.when(count > 8 * tall)
        def _(buf_ref=buf_ref, count=count, tall=tall):
            add_some(buf_ref, acc_ref, 8 * tall, count, 4)

    if last:
        sums_ref = refs[-1]
        dens = acc_ref[:, :, :P_SIZE]
        for i, value in enumerate((dens, dens * dens)):
            part = jnp.sum(value.reshape(-1, 8, P_SIZE), axis=0)
            part = jnp.sum(jnp.sum(part, axis=0, keepdims=True), axis=1, keepdims=True)
            sums_ref[8 * i : 8 * i + 8, :] = jnp.broadcast_to(part, (8, P_SIZE))


def add_blocks(acc, bufs, last=False):
    first = acc is None
    n = len(bufs)
    slots = sum(buf.shape[0] for buf in bufs) // PIECE_ROWS
    out_shape = [jax.ShapeDtypeStruct((PATCHES, P_SIZE, GRIDS * P_SIZE), jnp.float32)]
    if last:
        out_shape.append(jax.ShapeDtypeStruct((16, P_SIZE), jnp.float32))
    args = list(bufs) + ([] if first else [acc])
    flops = 4 * slots * GRIDS * P_SIZE * P_SIZE * B
    out = pl.pallas_call(
        lambda *refs: grid_kernel(n, first, last, *refs),
        out_shape=out_shape,
        in_specs=[VMEM] * len(args),
        out_specs=[VMEM] * len(out_shape),
        input_output_aliases={} if first else {n: 0},
        compiler_params=PARAMS,
        cost_estimate=pl.CostEstimate(flops=flops, bytes_accessed=slots * PIECE_ROWS * LANES, transcendentals=0),
        name="grid",
    )(*args)
    return tuple(out) if last else out[0]


def two_parts(value):
    high = value.astype(jnp.bfloat16)
    return high, (value - high.astype(jnp.float32)).astype(jnp.bfloat16)


def image_kernel(acc_ref, mine_ref, other_ref, row_ref, col_ref, out_ref):
    s1 = mine_ref[0:1, :] + other_ref[0:1, :]
    s2 = mine_ref[8:9, :] + other_ref[8:9, :]
    factor = 2.5 * s1 / s2
    width = out_ref.shape[3]
    half = 2 * width
    done = []
    for t in range(NT_C):
        tiles = [[acc_ref.at[4 * t + 2 * pr + pc] for pr in range(2)] for pc in range(2)]
        weights = [[1.0 / (1.0 + factor * tile[:, :P_SIZE]) for tile in pair] for pair in tiles]
        for pol in range(POLS):
            cells = []
            for e in (1 + 2 * pol, 2 + 2 * pol):
                for pc in range(2):
                    strip = [
                        tiles[pc][pr][:, e * P_SIZE : (e + 1) * P_SIZE] * weights[pc][pr] for pr in range(2)
                    ]
                    cells.append(jnp.concatenate(strip, axis=1))
            high, low = two_parts(jnp.concatenate(cells, axis=0))
            both = jnp.dot(row_ref[...], high, preferred_element_type=jnp.float32)
            rest = jnp.dot(row_ref[:half], low, preferred_element_type=jnp.float32)
            done.append(both[:half] + both[half:] + rest)
    high, low = two_parts(jnp.concatenate(done, axis=0))
    both = jnp.dot(high, col_ref[...], preferred_element_type=jnp.float32)
    rest = jnp.dot(low, col_ref[:, : 2 * G], preferred_element_type=jnp.float32)
    done = both[:, : 2 * G] + both[:, 2 * G :] + rest
    for t in range(NT_C):
        for pol in range(POLS):
            at = (t * POLS + pol) * half
            real, imag = done[at : at + width], done[at + width : at + half]
            out_ref[pol, 0, t] = real[:, :G] + imag[:, G:]
            out_ref[pol, 1, t] = imag[:, :G] - real[:, G:]


def make_image(acc, mine, other, row_table, col_table, width):
    return pl.pallas_call(
        image_kernel,
        out_shape=jax.ShapeDtypeStruct((POLS, 2, NT_C, width, G), jnp.float32),
        in_specs=[VMEM] * 5,
        out_specs=VMEM,
        compiler_params=PARAMS,
        name="image",
    )(acc, mine, other, row_table, col_table)


def dft_tables():
    index = np.arange(G)
    phase = (index[:, None] * index[None, :] % G) * (2.0 * math.pi / G)
    return np.cos(phase).astype(np.float32), np.sin(phase).astype(np.float32)


def np_parts(table, axis):
    high = table.astype(ml_dtypes.bfloat16)
    low = (table - high.astype(np.float32)).astype(ml_dtypes.bfloat16)
    return np.concatenate([high, low], axis=axis)


def image_tables(n_tm):
    cosine, sine = dft_tables()
    rows = []
    for cos_part, sin_part in zip(np.split(cosine, n_tm, axis=1), np.split(sine, n_tm, axis=1)):
        rows.append(np_parts(np.block([[cos_part, -sin_part], [sin_part, cos_part]]).T, 0))
    return np.stack(rows), np_parts(np.concatenate([cosine, sine], axis=1) / G, 1)


def by_gather(packed, n_tm, n_tile):
    order = list(range(0, n_tm, 2)) + list(range(1, n_tm, 2))[::-1]
    ways = [[], []]
    for i in range(n_tm):
        for tile in range(n_tile):
            here, there = (n_tile * order[k] + tile for k in (i, (i + 1) % n_tm))
            ways[tile % 2].append((here, there))
            ways[1 - tile % 2].append((there, here))

    def both_ways(pair):
        return [lax.ppermute(a, ("tm", "tile"), way) for a, way in zip(pair, ways)]

    leading = both_ways(packed)
    trailing = both_ways(packed[::-1])
    acc = add_blocks(None, packed)
    for step in range(2, n_tm // 2 + 1):
        following = both_ways(leading)
        acc = add_blocks(acc, leading)
        acc, *trailing = lax.optimization_barrier((acc, *trailing))
        leading = following
        following = both_ways(trailing) if step < n_tm // 2 else None
        acc = add_blocks(acc, trailing)
        trailing = following
    acc = add_blocks(acc, leading[:1])
    return add_blocks(acc, leading[1:], last=True)


def rest_by_rows(acc, cosine, sine):
    grid = acc.reshape(NT_C, 2, 2, P_SIZE, GRIDS, P_SIZE)
    flat = jnp.transpose(grid, (4, 0, 1, 5, 2, 3)).reshape(GRIDS, NT_C * G, G)
    owned = lax.psum_scatter(flat, "tm", scatter_dimension=1, tiled=True)
    dens = owned[0]
    totals = lax.psum((jnp.sum(dens), jnp.sum(dens * dens)), ("tm", "tile"))
    factor = 2.5 * totals[0] / totals[1]
    weighted = owned[1:] / (1.0 + factor * dens[None])
    weighted = weighted.reshape(POLS, 2, dens.shape[0], G)
    real, imag = weighted[:, 0], weighted[:, 1]

    def rows(a, b):
        return jnp.einsum("prj,jn->prn", a, b, precision=HIGH)

    done = jnp.stack([rows(real, cosine) + rows(imag, sine), rows(imag, cosine) - rows(real, sine)], axis=1)
    width = G // lax.axis_size("tm")
    every_row = lax.all_gather(done, "tm", axis=2, tiled=True)
    columns = lax.dynamic_slice_in_dim(every_row, lax.axis_index("tm") * width, width, 3)
    columns = columns.reshape(POLS, 2, NT_C, G, width)
    real, imag = columns[:, 0], columns[:, 1]

    def cols(a, b):
        return jnp.einsum("mi,ptic->ptcm", a, b, precision=HIGH)

    out = jnp.stack([cols(cosine, real) + cols(sine, imag), cols(cosine, imag) - cols(sine, real)], axis=1)
    return out / G


def body(vis_data, vis_weight, kernel_taps, offsets, block_patch, block_count):
    slots = vis_weight.shape[1]
    n_tm = lax.axis_size("tm")
    pieces = (slots // 2, slots - slots // 2)
    packed = pack(pieces, vis_data[0], vis_weight[0], kernel_taps[0], offsets[0], block_patch, block_count)
    if n_tm > 8:
        cosine, sine = dft_tables()
        return rest_by_rows(add_blocks(None, packed), jnp.asarray(cosine), jnp.asarray(sine))
    n_tile = lax.axis_size("tile")
    acc, mine = by_gather(packed, n_tm, n_tile)
    other = lax.ppermute(mine, "tile", [(i, n_tile - 1 - i) for i in range(n_tile)])
    row_tables, col_table = image_tables(n_tm)
    row_table = lax.dynamic_index_in_dim(jnp.asarray(row_tables), lax.axis_index("tm"), 0, keepdims=False)
    return make_image(acc, mine, other, row_table, jnp.asarray(col_table), G // n_tm)


def solution(mesh):
    return jax.shard_map(
        body,
        mesh=mesh,
        in_specs=(
            P(("grp", "tile"), "tm", None, None),
            P(("grp", "tile"), "tm", None),
            P(("grp", "tile"), "tm", None, None, None),
            P(("grp", "tile"), "tm", None, None),
            P(("grp", "tile"), "tm"),
            P(("grp", "tile"), "tm"),
        ),
        out_specs=P(None, None, ("grp", "tile"), "tm", None),
        check_vma=False,
    )
```

```python
import math

import jax
import jax.numpy as jnp
import ml_dtypes
import numpy as np
from jax import lax
from jax.experimental import pallas as pl
from jax.experimental.pallas import tpu as pltpu
from jax.sharding import PartitionSpec as P

G = 256
P_SIZE = 128
K = 8
B = 256
POLS = 2
NT_C = 2
PATCHES = 4 * NT_C
GRIDS = 1 + 2 * POLS
LANES = 128
HALVES = B // LANES
AUX = GRIDS + 2
TAP_ROWS = 2 * HALVES * K
ID_START = TAP_ROWS + AUX * HALVES
PIECE_ROWS = ID_START + 1
COUNT_LANE = 64
HIGH = lax.Precision.HIGHEST
VMEM = pl.BlockSpec(memory_space=pltpu.VMEM)
PARAMS = pltpu.CompilerParams(vmem_limit_bytes=20 * 1024 * 1024)


def half_lanes(half):
    return slice(half * LANES, (half + 1) * LANES)


def pack_kernel(pieces, vis_hbm, weight_hbm, taps_hbm, offs_hbm, patch_hbm, count_ref, *refs):
    outs, scratch = refs[: len(pieces)], refs[len(pieces) :]
    vis_ref, weight_ref, taps_ref, offs_ref, patch_ref, sems = scratch
    pairs = (
        (offs_hbm, offs_ref),
        (taps_hbm, taps_ref),
        (weight_hbm, weight_ref),
        (vis_hbm, vis_ref),
        (patch_hbm, patch_ref),
    )
    copies = [pltpu.make_async_copy(a, b, sems.at[i]) for i, (a, b) in enumerate(pairs)]
    for copy in copies:
        copy.start()
    bases = [sum(pieces[:i]) for i in range(len(pieces))]
    copies[0].wait()
    copies[1].wait()
    for out_ref, n, base in zip(outs, pieces, bases):
        for j in range(n):
            for side in range(2):
                off = offs_ref[base + j, side : side + 1, :]
                taps = taps_ref[base + j, side]
                for bit in range(3):
                    moved = pltpu.roll(taps, 1 << bit, 0)
                    turn = jnp.broadcast_to((off >> bit) & 1, taps.shape) == 1
                    taps = jnp.where(turn, moved, taps)
                for half in range(HALVES):
                    at = j * TAP_ROWS + (side * HALVES + half) * K
                    out_ref[at : at + K, :] = taps[:, half_lanes(half)]
    copies[2].wait()
    copies[3].wait()
    copies[4].wait()
    for out_ref, n, base in zip(outs, pieces, bases):
        for half in range(HALVES):
            lanes = half_lanes(half)
            weight = weight_ref[base : base + n, lanes]
            kinds = [weight] + [weight * vis_ref[base : base + n, m, lanes] for m in range(2 * POLS)]
            kinds += [offs_ref[base : base + n, side, lanes].astype(jnp.float32) for side in range(2)]
            for kind, rows in enumerate(kinds):
                at = n * (TAP_ROWS + kind * HALVES + half)
                out_ref[at : at + n, :] = rows
        lane = lax.broadcasted_iota(jnp.int32, (1, LANES), 1)
        live = jnp.clip(count_ref[0, 0] - base, 0, n)
        for j in range(n):
            row = jnp.where(lane < COUNT_LANE, patch_ref[0, base + j], live)
            out_ref[n * ID_START + j : n * ID_START + j + 1, :] = row.astype(jnp.float32)


def pack(pieces, vis, weight, taps, offs, patches, count):
    arrays = (vis, weight, taps, offs, patches)
    spaces = [pltpu.VMEM] * 4 + [pltpu.SMEM]
    hbm, smem = pl.BlockSpec(memory_space=pltpu.HBM), pl.BlockSpec(memory_space=pltpu.SMEM)
    return pl.pallas_call(
        lambda *refs: pack_kernel(pieces, *refs),
        out_shape=[jax.ShapeDtypeStruct((n * PIECE_ROWS, LANES), jnp.float32) for n in pieces],
        in_specs=[hbm] * 5 + [smem],
        out_specs=[VMEM] * len(pieces),
        scratch_shapes=[space(a.shape, a.dtype) for space, a in zip(spaces, arrays)] + [pltpu.SemaphoreType.DMA((5,))],
        compiler_params=PARAMS,
        name="pack",
    )(*[pltpu.with_memory_space_constraint(a, pltpu.HBM) for a in arrays], count)


def spread(off):
    row = lax.broadcasted_iota(jnp.int32, (16, B), 0)
    gap = off.astype(jnp.int32) - row
    step = (gap + 15) >> 4
    inside = (step << 4) - gap < K
    return jnp.where(inside, step, -1).astype(jnp.float32).astype(jnp.bfloat16)


def slot_taps(buf_ref, j, side):
    halves = []
    for half in range(HALVES):
        at = pl.multiple_of(j * TAP_ROWS, K) + (side * HALVES + half) * K
        halves.append(buf_ref[pl.ds(at, K), :])
    return jnp.concatenate([jnp.concatenate(halves, axis=1)] * 2, axis=0)


def slot_row(buf_ref, n, j, kind):
    at = [n * (TAP_ROWS + kind * HALVES + half) + j for half in range(HALVES)]
    return jnp.concatenate([buf_ref[pl.ds(r, 1), :] for r in at], axis=1)


def block_factors(buf_ref, n, j, live):
    rows_u = slot_taps(buf_ref, j, 0)
    rows_v = slot_taps(buf_ref, j, 1)
    step_u = spread(slot_row(buf_ref, n, j, GRIDS))
    step_v = spread(slot_row(buf_ref, n, j, GRIDS + 1))
    if live is not None:
        rows_v = jnp.where(live, rows_v, 0.0)
    rows_v = rows_v.astype(jnp.bfloat16)
    zero = jnp.zeros((16, B), jnp.bfloat16)
    steps = P_SIZE // 16
    right = jnp.concatenate([jnp.where(step_v == s, rows_v, zero) for s in range(steps)], axis=0)
    hits = [step_u == s for s in range(steps)]
    left = []
    for e in range(GRIDS):
        product = (rows_u * slot_row(buf_ref, n, j, e)).astype(jnp.bfloat16)
        left += [jnp.where(hit, product, zero) for hit in hits]
    return jnp.concatenate(left, axis=0), right


def add_some(buf_ref, acc_ref, first, count, unroll):
    n = buf_ref.shape[0] // PIECE_ROWS
    waiting = None
    for i in range(unroll):
        j = first if i == 0 else jnp.minimum(first + i, n - 1)
        left, right = block_factors(buf_ref, n, j, None if i == 0 else first + i < count)
        patch = lax.dot_general(
            right, left, (((1,), (1,)), ((), ())), preferred_element_type=jnp.float32
        )
        if waiting is not None:
            acc_ref[waiting[0]] += waiting[1]
        waiting = buf_ref[pl.ds(n * ID_START + j, 1), 0:1][0, 0].astype(jnp.int32), patch
    acc_ref[waiting[0]] += waiting[1]


def grid_kernel(n, first, last, *refs):
    bufs = refs[:n]
    acc_ref = refs[n] if first else refs[n + 1]
    if first:
        acc_ref[...] = jnp.zeros_like(acc_ref)
    for buf_ref in bufs:
        at = buf_ref.shape[0] // PIECE_ROWS * ID_START
        count = buf_ref[at : at + 1, COUNT_LANE : COUNT_LANE + 1][0, 0].astype(jnp.int32)
        tall = (count + 3) // 8

        def eight(step, _, buf_ref=buf_ref, count=count):
            add_some(buf_ref, acc_ref, 8 * step, count, 8)
            return 0

        lax.fori_loop(0, tall, eight, 0)

        @pl.when(count > 8 * tall)
        def _(buf_ref=buf_ref, count=count, tall=tall):
            add_some(buf_ref, acc_ref, 8 * tall, count, 4)

    if last:
        sums_ref = refs[-1]
        dens = acc_ref[:, :, :P_SIZE]
        for i, value in enumerate((dens, dens * dens)):
            part = jnp.sum(value.reshape(-1, 8, P_SIZE), axis=0)
            part = jnp.sum(jnp.sum(part, axis=0, keepdims=True), axis=1, keepdims=True)
            sums_ref[8 * i : 8 * i + 8, :] = jnp.broadcast_to(part, (8, P_SIZE))


def add_blocks(acc, bufs, last=False):
    first = acc is None
    n = len(bufs)
    slots = sum(buf.shape[0] for buf in bufs) // PIECE_ROWS
    out_shape = [jax.ShapeDtypeStruct((PATCHES, P_SIZE, GRIDS * P_SIZE), jnp.float32)]
    if last:
        out_shape.append(jax.ShapeDtypeStruct((16, P_SIZE), jnp.float32))
    args = list(bufs) + ([] if first else [acc])
    flops = 4 * slots * GRIDS * P_SIZE * P_SIZE * B
    out = pl.pallas_call(
        lambda *refs: grid_kernel(n, first, last, *refs),
        out_shape=out_shape,
        in_specs=[VMEM] * len(args),
        out_specs=[VMEM] * len(out_shape),
        input_output_aliases={} if first else {n: 0},
        compiler_params=PARAMS,
        cost_estimate=pl.CostEstimate(flops=flops, bytes_accessed=slots * PIECE_ROWS * LANES, transcendentals=0),
        name="grid",
    )(*args)
    return tuple(out) if last else out[0]


def two_parts(value):
    high = value.astype(jnp.bfloat16)
    return high, (value - high.astype(jnp.float32)).astype(jnp.bfloat16)


def image_kernel(acc_ref, mine_ref, other_ref, row_ref, col_ref, out_ref):
    s1 = mine_ref[0:1, :] + other_ref[0:1, :]
    s2 = mine_ref[8:9, :] + other_ref[8:9, :]
    factor = 2.5 * s1 / s2
    width = out_ref.shape[3]
    half = 2 * width
    done = []
    for t in range(NT_C):
        tiles = [[acc_ref.at[4 * t + 2 * pr + pc] for pr in range(2)] for pc in range(2)]
        weights = [[1.0 / (1.0 + factor * tile[:, :P_SIZE]) for tile in pair] for pair in tiles]
        for pol in range(POLS):
            cells = []
            for e in (1 + 2 * pol, 2 + 2 * pol):
                for pc in range(2):
                    strip = [
                        tiles[pc][pr][:, e * P_SIZE : (e + 1) * P_SIZE] * weights[pc][pr] for pr in range(2)
                    ]
                    cells.append(jnp.concatenate(strip, axis=1))
            high, low = two_parts(jnp.concatenate(cells, axis=0))
            both = jnp.dot(row_ref[...], high, preferred_element_type=jnp.float32)
            rest = jnp.dot(row_ref[:half], low, preferred_element_type=jnp.float32)
            done.append(both[:half] + both[half:] + rest)
    high, low = two_parts(jnp.concatenate(done, axis=0))
    both = jnp.dot(high, col_ref[...], preferred_element_type=jnp.float32)
    rest = jnp.dot(low, col_ref[:, : 2 * G], preferred_element_type=jnp.float32)
    done = both[:, : 2 * G] + both[:, 2 * G :] + rest
    for t in range(NT_C):
        for pol in range(POLS):
            at = (t * POLS + pol) * half
            real, imag = done[at : at + width], done[at + width : at + half]
            out_ref[pol, 0, t] = real[:, :G] + imag[:, G:]
            out_ref[pol, 1, t] = imag[:, :G] - real[:, G:]


def make_image(acc, mine, other, row_table, col_table, width):
    return pl.pallas_call(
        image_kernel,
        out_shape=jax.ShapeDtypeStruct((POLS, 2, NT_C, width, G), jnp.float32),
        in_specs=[VMEM] * 5,
        out_specs=VMEM,
        compiler_params=PARAMS,
        name="image",
    )(acc, mine, other, row_table, col_table)


def dft_tables():
    index = np.arange(G)
    phase = (index[:, None] * index[None, :] % G) * (2.0 * math.pi / G)
    return np.cos(phase).astype(np.float32), np.sin(phase).astype(np.float32)


def np_parts(table, axis):
    high = table.astype(ml_dtypes.bfloat16)
    low = (table - high.astype(np.float32)).astype(ml_dtypes.bfloat16)
    return np.concatenate([high, low], axis=axis)


def image_tables(n_tm):
    cosine, sine = dft_tables()
    rows = []
    for cos_part, sin_part in zip(np.split(cosine, n_tm, axis=1), np.split(sine, n_tm, axis=1)):
        rows.append(np_parts(np.block([[cos_part, -sin_part], [sin_part, cos_part]]).T, 0))
    return np.stack(rows), np_parts(np.concatenate([cosine, sine], axis=1) / G, 1)


def by_gather(packed, n_tm, n_tile):
    order = list(range(0, n_tm, 2)) + list(range(1, n_tm, 2))[::-1]
    ways = [[], []]
    for i in range(n_tm):
        for tile in range(n_tile):
            here, there = (n_tile * order[k] + tile for k in (i, (i + 1) % n_tm))
            ways[tile % 2].append((here, there))
            ways[1 - tile % 2].append((there, here))

    def both_ways(pair):
        return [lax.ppermute(a, ("tm", "tile"), way) for a, way in zip(pair, ways)]

    leading = both_ways(packed)
    trailing = both_ways(packed[::-1])
    acc, *leading = lax.optimization_barrier((add_blocks(None, packed), *leading))
    following = both_ways(leading)
    acc = add_blocks(acc, leading)
    for _ in range(2, n_tm // 2):
        acc, *trailing = lax.optimization_barrier((acc, *trailing))
        behind = both_ways(trailing)
        acc, *arrived = lax.optimization_barrier((acc, *trailing, *following))
        following = both_ways(arrived[2:])
        acc = add_blocks(acc, arrived)
        trailing = behind
    acc = add_blocks(acc, trailing)
    acc = add_blocks(acc, following[:1])
    return add_blocks(acc, following[1:], last=True)


def rest_by_rows(acc, cosine, sine):
    grid = acc.reshape(NT_C, 2, 2, P_SIZE, GRIDS, P_SIZE)
    flat = jnp.transpose(grid, (4, 0, 1, 5, 2, 3)).reshape(GRIDS, NT_C * G, G)
    owned = lax.psum_scatter(flat, "tm", scatter_dimension=1, tiled=True)
    dens = owned[0]
    totals = lax.psum((jnp.sum(dens), jnp.sum(dens * dens)), ("tm", "tile"))
    factor = 2.5 * totals[0] / totals[1]
    weighted = owned[1:] / (1.0 + factor * dens[None])
    weighted = weighted.reshape(POLS, 2, dens.shape[0], G)
    real, imag = weighted[:, 0], weighted[:, 1]

    def rows(a, b):
        return jnp.einsum("prj,jn->prn", a, b, precision=HIGH)

    done = jnp.stack([rows(real, cosine) + rows(imag, sine), rows(imag, cosine) - rows(real, sine)], axis=1)
    width = G // lax.axis_size("tm")
    every_row = lax.all_gather(done, "tm", axis=2, tiled=True)
    columns = lax.dynamic_slice_in_dim(every_row, lax.axis_index("tm") * width, width, 3)
    columns = columns.reshape(POLS, 2, NT_C, G, width)
    real, imag = columns[:, 0], columns[:, 1]

    def cols(a, b):
        return jnp.einsum("mi,ptic->ptcm", a, b, precision=HIGH)

    out = jnp.stack([cols(cosine, real) + cols(sine, imag), cols(cosine, imag) - cols(sine, real)], axis=1)
    return out / G


def body(vis_data, vis_weight, kernel_taps, offsets, block_patch, block_count):
    slots = vis_weight.shape[1]
    n_tm = lax.axis_size("tm")
    pieces = (slots // 2, slots - slots // 2)
    packed = pack(pieces, vis_data[0], vis_weight[0], kernel_taps[0], offsets[0], block_patch, block_count)
    if n_tm > 8:
        cosine, sine = dft_tables()
        return rest_by_rows(add_blocks(None, packed), jnp.asarray(cosine), jnp.asarray(sine))
    n_tile = lax.axis_size("tile")
    acc, mine = by_gather(packed, n_tm, n_tile)
    other = lax.ppermute(mine, "tile", [(i, n_tile - 1 - i) for i in range(n_tile)])
    row_tables, col_table = image_tables(n_tm)
    row_table = lax.dynamic_index_in_dim(jnp.asarray(row_tables), lax.axis_index("tm"), 0, keepdims=False)
    return make_image(acc, mine, other, row_table, jnp.asarray(col_table), G // n_tm)


def solution(mesh):
    return jax.shard_map(
        body,
        mesh=mesh,
        in_specs=(
            P(("grp", "tile"), "tm", None, None),
            P(("grp", "tile"), "tm", None),
            P(("grp", "tile"), "tm", None, None, None),
            P(("grp", "tile"), "tm", None, None),
            P(("grp", "tile"), "tm"),
            P(("grp", "tile"), "tm"),
        ),
        out_specs=P(None, None, ("grp", "tile"), "tm", None),
        check_vma=False,
    )
```

```python
import math

import jax
import jax.numpy as jnp
import ml_dtypes
import numpy as np
from jax import lax
from jax.experimental import pallas as pl
from jax.experimental.pallas import tpu as pltpu
from jax.sharding import PartitionSpec as P

G = 256
P_SIZE = 128
K = 8
B = 256
POLS = 2
NT_C = 2
PATCHES = 4 * NT_C
GRIDS = 1 + 2 * POLS
LANES = 128
HALVES = B // LANES
AUX = GRIDS + 2
TAP_ROWS = 2 * HALVES * K
ID_START = TAP_ROWS + AUX * HALVES
PIECE_ROWS = ID_START + 1
HIGH = lax.Precision.HIGHEST
VMEM = pl.BlockSpec(memory_space=pltpu.VMEM)
PARAMS = pltpu.CompilerParams(vmem_limit_bytes=20 * 1024 * 1024)


def half_lanes(half):
    return slice(half * LANES, (half + 1) * LANES)


def pack_kernel(pieces, vis_hbm, weight_hbm, taps_hbm, offs_hbm, patch_hbm, count_ref, *refs):
    outs, scratch = refs[: len(pieces)], refs[len(pieces) :]
    vis_ref, weight_ref, taps_ref, offs_ref, patch_ref, sems = scratch
    pairs = (
        (offs_hbm, offs_ref),
        (taps_hbm, taps_ref),
        (weight_hbm, weight_ref),
        (vis_hbm, vis_ref),
        (patch_hbm, patch_ref),
    )
    copies = [pltpu.make_async_copy(a, b, sems.at[i]) for i, (a, b) in enumerate(pairs)]
    for copy in copies:
        copy.start()
    bases = [sum(pieces[:i]) for i in range(len(pieces))]
    copies[0].wait()
    copies[1].wait()
    for out_ref, n, base in zip(outs, pieces, bases):
        for j in range(n):
            for side in range(2):
                off = offs_ref[base + j, side : side + 1, :]
                taps = taps_ref[base + j, side]
                for bit in range(3):
                    moved = pltpu.roll(taps, 1 << bit, 0)
                    turn = jnp.broadcast_to((off >> bit) & 1, taps.shape) == 1
                    taps = jnp.where(turn, moved, taps)
                for half in range(HALVES):
                    at = j * TAP_ROWS + (side * HALVES + half) * K
                    out_ref[at : at + K, :] = taps[:, half_lanes(half)]
    copies[2].wait()
    copies[3].wait()
    copies[4].wait()
    for out_ref, n, base in zip(outs, pieces, bases):
        for half in range(HALVES):
            lanes = half_lanes(half)
            weight = weight_ref[base : base + n, lanes]
            kinds = [weight] + [weight * vis_ref[base : base + n, m, lanes] for m in range(2 * POLS)]
            kinds += [offs_ref[base : base + n, side, lanes].astype(jnp.float32) for side in range(2)]
            for kind, rows in enumerate(kinds):
                at = n * (TAP_ROWS + kind * HALVES + half)
                out_ref[at : at + n, :] = rows
        for j in range(n):
            patch = jnp.where(base + j < count_ref[0, 0], patch_ref[0, base + j], -1)
            row = jnp.full((1, LANES), patch, jnp.int32).astype(jnp.float32)
            out_ref[n * ID_START + j : n * ID_START + j + 1, :] = row


def pack(pieces, vis, weight, taps, offs, patches, count):
    arrays = (vis, weight, taps, offs, patches)
    spaces = [pltpu.VMEM] * 4 + [pltpu.SMEM]
    hbm, smem = pl.BlockSpec(memory_space=pltpu.HBM), pl.BlockSpec(memory_space=pltpu.SMEM)
    return pl.pallas_call(
        lambda *refs: pack_kernel(pieces, *refs),
        out_shape=[jax.ShapeDtypeStruct((n * PIECE_ROWS, LANES), jnp.float32) for n in pieces],
        in_specs=[hbm] * 5 + [smem],
        out_specs=[VMEM] * len(pieces),
        scratch_shapes=[space(a.shape, a.dtype) for space, a in zip(spaces, arrays)] + [pltpu.SemaphoreType.DMA((5,))],
        compiler_params=PARAMS,
        name="pack",
    )(*[pltpu.with_memory_space_constraint(a, pltpu.HBM) for a in arrays], count)


def spread(off):
    row = lax.broadcasted_iota(jnp.int32, (16, B), 0)
    gap = off.astype(jnp.int32) - row
    step = (gap + 15) >> 4
    inside = (step << 4) - gap < K
    return jnp.where(inside, step, -1).astype(jnp.float32).astype(jnp.bfloat16)


def slot_taps(buf_ref, j, side):
    starts = [j * TAP_ROWS + (side * HALVES + half) * K for half in range(HALVES)]
    rows = jnp.concatenate([buf_ref[at : at + K, :] for at in starts], axis=1)
    return jnp.concatenate([rows, rows], axis=0)


def slot_row(buf_ref, n, j, kind):
    starts = [n * (TAP_ROWS + kind * HALVES + half) + j for half in range(HALVES)]
    return jnp.concatenate([buf_ref[at : at + 1, :] for at in starts], axis=1)


def slot_patch(buf_ref, n, j):
    return buf_ref[n * ID_START + j : n * ID_START + j + 1, 0:1][0, 0].astype(jnp.int32)


def block_factors(buf_ref, n, j, live, grids):
    rows_u = slot_taps(buf_ref, j, 0)
    rows_v = slot_taps(buf_ref, j, 1)
    step_u = spread(slot_row(buf_ref, n, j, GRIDS))
    step_v = spread(slot_row(buf_ref, n, j, GRIDS + 1))
    if live is not None:
        rows_v = jnp.where(live, rows_v, 0.0)
    rows_v = rows_v.astype(jnp.bfloat16)
    zero = jnp.zeros((16, B), jnp.bfloat16)
    steps = P_SIZE // 16
    right = jnp.concatenate([jnp.where(step_v == s, rows_v, zero) for s in range(steps)], axis=0)
    hits = [step_u == s for s in range(steps)]
    left = []
    for e in grids:
        product = (rows_u * slot_row(buf_ref, n, j, e)).astype(jnp.bfloat16)
        left += [jnp.where(hit, product, zero) for hit in hits]
    return jnp.concatenate(left, axis=0), right


def add_some(buf_ref, acc_ref, n, slots, grids):
    lanes = slice(grids[0] * P_SIZE, (grids[-1] + 1) * P_SIZE)
    waiting = None
    for i, j in enumerate(slots):
        where_at = slot_patch(buf_ref, n, j)
        left, right = block_factors(buf_ref, n, j, where_at >= 0 if i else None, grids)
        patch = lax.dot_general(
            right, left, (((1,), (1,)), ((), ())), preferred_element_type=jnp.float32
        )
        if waiting is not None:
            acc_ref[waiting[0], :, lanes] += waiting[1]
        waiting = jnp.maximum(where_at, 0), patch
    acc_ref[waiting[0], :, lanes] += waiting[1]


def grid_kernel(n_bufs, first, last, grids, *refs):
    acc_ref = refs[n_bufs] if first else refs[n_bufs + 1]
    if first:
        acc_ref[...] = jnp.zeros_like(acc_ref)
    for buf_ref in refs[:n_bufs]:
        n = buf_ref.shape[0] // PIECE_ROWS
        for low in range(0, n, 8):
            few, many = range(low, min(low + 4, n)), range(low, min(low + 8, n))
            some = slot_patch(buf_ref, n, low) >= 0
            more = slot_patch(buf_ref, n, low + 4) >= 0 if len(many) > 4 else jnp.bool_(False)

            @pl.when(more)
            def _(buf_ref=buf_ref, n=n, many=many):
                add_some(buf_ref, acc_ref, n, many, grids)

            @pl.when(jnp.logical_and(some, jnp.logical_not(more)))
            def _(buf_ref=buf_ref, n=n, few=few):
                add_some(buf_ref, acc_ref, n, few, grids)

    if last:
        sums_ref = refs[-1]
        dens = acc_ref[:, :, :P_SIZE]
        for i, value in enumerate((dens, dens * dens)):
            part = jnp.sum(value.reshape(-1, 8, P_SIZE), axis=0)
            part = jnp.sum(jnp.sum(part, axis=0, keepdims=True), axis=1, keepdims=True)
            sums_ref[8 * i : 8 * i + 8, :] = jnp.broadcast_to(part, (8, P_SIZE))


def add_blocks(acc, bufs, last=False, grids=range(GRIDS)):
    first = acc is None
    n = len(bufs)
    slots = sum(buf.shape[0] for buf in bufs) // PIECE_ROWS
    out_shape = [jax.ShapeDtypeStruct((PATCHES, P_SIZE, GRIDS * P_SIZE), jnp.float32)]
    if last:
        out_shape.append(jax.ShapeDtypeStruct((16, P_SIZE), jnp.float32))
    args = list(bufs) + ([] if first else [acc])
    flops = 4 * slots * len(grids) * P_SIZE * P_SIZE * B
    out = pl.pallas_call(
        lambda *refs: grid_kernel(n, first, last, grids, *refs),
        out_shape=out_shape,
        in_specs=[VMEM] * len(args),
        out_specs=[VMEM] * len(out_shape),
        input_output_aliases={} if first else {n: 0},
        compiler_params=PARAMS,
        cost_estimate=pl.CostEstimate(flops=flops, bytes_accessed=slots * PIECE_ROWS * LANES, transcendentals=0),
        name="grid",
    )(*args)
    return tuple(out) if last else out[0]


def two_parts(value):
    high = value.astype(jnp.bfloat16)
    return high, (value - high.astype(jnp.float32)).astype(jnp.bfloat16)


def image_kernel(acc_ref, mine_ref, other_ref, row_ref, col_ref, out_ref):
    s1 = mine_ref[0:1, :] + other_ref[0:1, :]
    s2 = mine_ref[8:9, :] + other_ref[8:9, :]
    factor = 2.5 * s1 / s2
    width = out_ref.shape[3]
    half = 2 * width
    done = []
    for t in range(NT_C):
        tiles = [[acc_ref.at[4 * t + 2 * pr + pc] for pr in range(2)] for pc in range(2)]
        weights = [[1.0 / (1.0 + factor * tile[:, :P_SIZE]) for tile in pair] for pair in tiles]
        for pol in range(POLS):
            cells = []
            for e in (1 + 2 * pol, 2 + 2 * pol):
                for pc in range(2):
                    strip = [
                        tiles[pc][pr][:, e * P_SIZE : (e + 1) * P_SIZE] * weights[pc][pr] for pr in range(2)
                    ]
                    cells.append(jnp.concatenate(strip, axis=1))
            high, low = two_parts(jnp.concatenate(cells, axis=0))
            both = jnp.dot(row_ref[...], high, preferred_element_type=jnp.float32)
            rest = jnp.dot(row_ref[:half], low, preferred_element_type=jnp.float32)
            done.append(both[:half] + both[half:] + rest)
    high, low = two_parts(jnp.concatenate(done, axis=0))
    both = jnp.dot(high, col_ref[...], preferred_element_type=jnp.float32)
    rest = jnp.dot(low, col_ref[:, : 2 * G], preferred_element_type=jnp.float32)
    done = both[:, : 2 * G] + both[:, 2 * G :] + rest
    for t in range(NT_C):
        for pol in range(POLS):
            at = (t * POLS + pol) * half
            real, imag = done[at : at + width], done[at + width : at + half]
            out_ref[pol, 0, t] = real[:, :G] + imag[:, G:]
            out_ref[pol, 1, t] = imag[:, :G] - real[:, G:]


def make_image(acc, mine, other, row_table, col_table, width):
    return pl.pallas_call(
        image_kernel,
        out_shape=jax.ShapeDtypeStruct((POLS, 2, NT_C, width, G), jnp.float32),
        in_specs=[VMEM] * 5,
        out_specs=VMEM,
        compiler_params=PARAMS,
        name="image",
    )(acc, mine, other, row_table, col_table)


def dft_tables():
    index = np.arange(G)
    phase = (index[:, None] * index[None, :] % G) * (2.0 * math.pi / G)
    return np.cos(phase).astype(np.float32), np.sin(phase).astype(np.float32)


def np_parts(table, axis):
    high = table.astype(ml_dtypes.bfloat16)
    low = (table - high.astype(np.float32)).astype(ml_dtypes.bfloat16)
    return np.concatenate([high, low], axis=axis)


def image_tables(n_tm):
    cosine, sine = dft_tables()
    rows = []
    for cos_part, sin_part in zip(np.split(cosine, n_tm, axis=1), np.split(sine, n_tm, axis=1)):
        rows.append(np_parts(np.block([[cos_part, -sin_part], [sin_part, cos_part]]).T, 0))
    return np.stack(rows), np_parts(np.concatenate([cosine, sine], axis=1) / G, 1)


def by_gather(packed, n_tm, n_tile):
    order = list(range(0, n_tm, 2)) + list(range(1, n_tm, 2))[::-1]
    ways = [[], []]
    for i in range(n_tm):
        for tile in range(n_tile):
            here, there = (n_tile * order[k] + tile for k in (i, (i + 1) % n_tm))
            ways[tile % 2].append((here, there))
            ways[1 - tile % 2].append((there, here))

    def both_ways(pair):
        return [lax.ppermute(a, ("tm", "tile"), way) for a, way in zip(pair, ways)]

    leading = both_ways(packed)
    trailing = both_ways(packed[::-1])
    acc = add_blocks(None, packed)
    for step in range(2, n_tm // 2 + 1):
        following = both_ways(leading)
        acc = add_blocks(acc, leading)
        acc, *trailing = lax.optimization_barrier((acc, *trailing))
        leading = following
        following = both_ways(trailing) if step < n_tm // 2 else None
        acc = add_blocks(acc, trailing)
        trailing = following
    acc = add_blocks(acc, leading[:1], grids=range(1))
    acc, sums = add_blocks(acc, leading[1:], last=True, grids=range(1))
    return add_blocks(acc, leading, grids=range(1, GRIDS)), sums


def rest_by_rows(acc, cosine, sine):
    grid = acc.reshape(NT_C, 2, 2, P_SIZE, GRIDS, P_SIZE)
    flat = jnp.transpose(grid, (4, 0, 1, 5, 2, 3)).reshape(GRIDS, NT_C * G, G)
    owned = lax.psum_scatter(flat, "tm", scatter_dimension=1, tiled=True)
    dens = owned[0]
    totals = lax.psum((jnp.sum(dens), jnp.sum(dens * dens)), ("tm", "tile"))
    factor = 2.5 * totals[0] / totals[1]
    weighted = owned[1:] / (1.0 + factor * dens[None])
    weighted = weighted.reshape(POLS, 2, dens.shape[0], G)
    real, imag = weighted[:, 0], weighted[:, 1]

    def rows(a, b):
        return jnp.einsum("prj,jn->prn", a, b, precision=HIGH)

    done = jnp.stack([rows(real, cosine) + rows(imag, sine), rows(imag, cosine) - rows(real, sine)], axis=1)
    width = G // lax.axis_size("tm")
    every_row = lax.all_gather(done, "tm", axis=2, tiled=True)
    columns = lax.dynamic_slice_in_dim(every_row, lax.axis_index("tm") * width, width, 3)
    columns = columns.reshape(POLS, 2, NT_C, G, width)
    real, imag = columns[:, 0], columns[:, 1]

    def cols(a, b):
        return jnp.einsum("mi,ptic->ptcm", a, b, precision=HIGH)

    out = jnp.stack([cols(cosine, real) + cols(sine, imag), cols(cosine, imag) - cols(sine, real)], axis=1)
    return out / G


def body(vis_data, vis_weight, kernel_taps, offsets, block_patch, block_count):
    slots = vis_weight.shape[1]
    n_tm = lax.axis_size("tm")
    pieces = (slots // 2, slots - slots // 2)
    packed = pack(pieces, vis_data[0], vis_weight[0], kernel_taps[0], offsets[0], block_patch, block_count)
    if n_tm > 8:
        cosine, sine = dft_tables()
        return rest_by_rows(add_blocks(None, packed), jnp.asarray(cosine), jnp.asarray(sine))
    n_tile = lax.axis_size("tile")
    acc, mine = by_gather(packed, n_tm, n_tile)
    other = lax.ppermute(mine, "tile", [(i, n_tile - 1 - i) for i in range(n_tile)])
    row_tables, col_table = image_tables(n_tm)
    row_table = lax.dynamic_index_in_dim(jnp.asarray(row_tables), lax.axis_index("tm"), 0, keepdims=False)
    return make_image(acc, mine, other, row_table, jnp.asarray(col_table), G // n_tm)


def solution(mesh):
    return jax.shard_map(
        body,
        mesh=mesh,
        in_specs=(
            P(("grp", "tile"), "tm", None, None),
            P(("grp", "tile"), "tm", None),
            P(("grp", "tile"), "tm", None, None, None),
            P(("grp", "tile"), "tm", None, None),
            P(("grp", "tile"), "tm"),
            P(("grp", "tile"), "tm"),
        ),
        out_specs=P(None, None, ("grp", "tile"), "tm", None),
        check_vma=False,
    )
```

```python
import math

import jax
import jax.numpy as jnp
import ml_dtypes
import numpy as np
from jax import lax
from jax.experimental import pallas as pl
from jax.experimental.pallas import tpu as pltpu
from jax.sharding import PartitionSpec as P

G = 256
P_SIZE = 128
K = 8
B = 256
POLS = 2
NT_C = 2
PATCHES = 4 * NT_C
GRIDS = 1 + 2 * POLS
LANES = 128
HALVES = B // LANES
AUX = GRIDS + 2
TAP_ROWS = 2 * HALVES * K
ID_START = TAP_ROWS + AUX * HALVES
PIECE_ROWS = ID_START + 1
HIGH = lax.Precision.HIGHEST
VMEM = pl.BlockSpec(memory_space=pltpu.VMEM)
PARAMS = pltpu.CompilerParams(vmem_limit_bytes=20 * 1024 * 1024)


def half_lanes(half):
    return slice(half * LANES, (half + 1) * LANES)


def pack_kernel(pieces, vis_hbm, weight_hbm, taps_hbm, offs_hbm, patch_hbm, count_ref, *refs):
    outs, scratch = refs[: len(pieces)], refs[len(pieces) :]
    vis_ref, weight_ref, taps_ref, offs_ref, patch_ref, sems = scratch
    pairs = (
        (offs_hbm, offs_ref),
        (taps_hbm, taps_ref),
        (weight_hbm, weight_ref),
        (vis_hbm, vis_ref),
        (patch_hbm, patch_ref),
    )
    copies = [pltpu.make_async_copy(a, b, sems.at[i]) for i, (a, b) in enumerate(pairs)]
    for copy in copies:
        copy.start()
    bases = [sum(pieces[:i]) for i in range(len(pieces))]
    copies[0].wait()
    copies[1].wait()
    for out_ref, n, base in zip(outs, pieces, bases):
        for j in range(n):
            for side in range(2):
                off = offs_ref[base + j, side : side + 1, :]
                taps = taps_ref[base + j, side]
                for bit in range(3):
                    moved = pltpu.roll(taps, 1 << bit, 0)
                    turn = jnp.broadcast_to((off >> bit) & 1, taps.shape) == 1
                    taps = jnp.where(turn, moved, taps)
                for half in range(HALVES):
                    at = j * TAP_ROWS + (side * HALVES + half) * K
                    out_ref[at : at + K, :] = taps[:, half_lanes(half)]
    copies[2].wait()
    copies[3].wait()
    copies[4].wait()
    for out_ref, n, base in zip(outs, pieces, bases):
        for half in range(HALVES):
            lanes = half_lanes(half)
            weight = weight_ref[base : base + n, lanes]
            kinds = [weight] + [weight * vis_ref[base : base + n, m, lanes] for m in range(2 * POLS)]
            kinds += [offs_ref[base : base + n, side, lanes].astype(jnp.float32) for side in range(2)]
            for kind, rows in enumerate(kinds):
                at = n * (TAP_ROWS + kind * HALVES + half)
                out_ref[at : at + n, :] = rows
        for j in range(n):
            patch = jnp.where(base + j < count_ref[0, 0], patch_ref[0, base + j], -1)
            row = jnp.full((1, LANES), patch, jnp.int32).astype(jnp.float32)
            out_ref[n * ID_START + j : n * ID_START + j + 1, :] = row


def pack(pieces, vis, weight, taps, offs, patches, count):
    arrays = (vis, weight, taps, offs, patches)
    spaces = [pltpu.VMEM] * 4 + [pltpu.SMEM]
    hbm, smem = pl.BlockSpec(memory_space=pltpu.HBM), pl.BlockSpec(memory_space=pltpu.SMEM)
    return pl.pallas_call(
        lambda *refs: pack_kernel(pieces, *refs),
        out_shape=[jax.ShapeDtypeStruct((n * PIECE_ROWS, LANES), jnp.float32) for n in pieces],
        in_specs=[hbm] * 5 + [smem],
        out_specs=[VMEM] * len(pieces),
        scratch_shapes=[space(a.shape, a.dtype) for space, a in zip(spaces, arrays)] + [pltpu.SemaphoreType.DMA((5,))],
        compiler_params=PARAMS,
        name="pack",
    )(*[pltpu.with_memory_space_constraint(a, pltpu.HBM) for a in arrays], count)


def spread(off):
    row = lax.broadcasted_iota(jnp.int32, (16, B), 0)
    gap = off.astype(jnp.int32) - row
    step = (gap + 15) >> 4
    inside = (step << 4) - gap < K
    return jnp.where(inside, step, -1).astype(jnp.float32).astype(jnp.bfloat16)


def slot_taps(buf_ref, j, side):
    starts = [j * TAP_ROWS + (side * HALVES + half) * K for half in range(HALVES)]
    rows = jnp.concatenate([buf_ref[at : at + K, :] for at in starts], axis=1)
    return jnp.concatenate([rows, rows], axis=0)


def slot_row(buf_ref, n, j, kind):
    starts = [n * (TAP_ROWS + kind * HALVES + half) + j for half in range(HALVES)]
    return jnp.concatenate([buf_ref[at : at + 1, :] for at in starts], axis=1)


def slot_patch(buf_ref, n, j):
    return buf_ref[n * ID_START + j : n * ID_START + j + 1, 0:1][0, 0].astype(jnp.int32)


def block_factors(buf_ref, n, j, live, grids):
    rows_u = slot_taps(buf_ref, j, 0)
    rows_v = slot_taps(buf_ref, j, 1)
    step_u = spread(slot_row(buf_ref, n, j, GRIDS))
    step_v = spread(slot_row(buf_ref, n, j, GRIDS + 1))
    if live is not None:
        rows_v = jnp.where(live, rows_v, 0.0)
    rows_v = rows_v.astype(jnp.bfloat16)
    zero = jnp.zeros((16, B), jnp.bfloat16)
    steps = P_SIZE // 16
    right = jnp.concatenate([jnp.where(step_v == s, rows_v, zero) for s in range(steps)], axis=0)
    hits = [step_u == s for s in range(steps)]
    left = []
    for e in grids:
        product = (rows_u * slot_row(buf_ref, n, j, e)).astype(jnp.bfloat16)
        left += [jnp.where(hit, product, zero) for hit in hits]
    return jnp.concatenate(left, axis=0), right


def add_some(buf_ref, acc_ref, n, slots, grids):
    lanes = slice(grids[0] * P_SIZE, (grids[-1] + 1) * P_SIZE)
    waiting = None
    for i, j in enumerate(slots):
        where_at = slot_patch(buf_ref, n, j)
        left, right = block_factors(buf_ref, n, j, where_at >= 0 if i else None, grids)
        patch = lax.dot_general(
            right, left, (((1,), (1,)), ((), ())), preferred_element_type=jnp.float32
        )
        if waiting is not None:
            acc_ref[waiting[0], :, lanes] += waiting[1]
        waiting = jnp.maximum(where_at, 0), patch
    acc_ref[waiting[0], :, lanes] += waiting[1]


def grid_kernel(n_bufs, first, last, grids, *refs):
    acc_ref = refs[n_bufs] if first else refs[n_bufs + 1]
    if first:
        acc_ref[...] = jnp.zeros_like(acc_ref)
    for buf_ref in refs[:n_bufs]:
        n = buf_ref.shape[0] // PIECE_ROWS
        for low in range(0, n, 8):
            few, many = range(low, min(low + 4, n)), range(low, min(low + 8, n))
            some = slot_patch(buf_ref, n, low) >= 0
            more = slot_patch(buf_ref, n, low + 4) >= 0 if len(many) > 4 else jnp.bool_(False)

            @pl.when(more)
            def _(buf_ref=buf_ref, n=n, many=many):
                add_some(buf_ref, acc_ref, n, many, grids)

            @pl.when(jnp.logical_and(some, jnp.logical_not(more)))
            def _(buf_ref=buf_ref, n=n, few=few):
                add_some(buf_ref, acc_ref, n, few, grids)

    if last:
        sums_ref = refs[-1]
        dens = acc_ref[:, :, :P_SIZE]
        for i, value in enumerate((dens, dens * dens)):
            part = jnp.sum(value.reshape(-1, 8, P_SIZE), axis=0)
            part = jnp.sum(jnp.sum(part, axis=0, keepdims=True), axis=1, keepdims=True)
            sums_ref[8 * i : 8 * i + 8, :] = jnp.broadcast_to(part, (8, P_SIZE))


def add_blocks(acc, bufs, last=False, grids=range(GRIDS)):
    first = acc is None
    n = len(bufs)
    slots = sum(buf.shape[0] for buf in bufs) // PIECE_ROWS
    out_shape = [jax.ShapeDtypeStruct((PATCHES, P_SIZE, GRIDS * P_SIZE), jnp.float32)]
    if last:
        out_shape.append(jax.ShapeDtypeStruct((16, P_SIZE), jnp.float32))
    args = list(bufs) + ([] if first else [acc])
    flops = (2 if first else 4) * slots * len(grids) * P_SIZE * P_SIZE * B
    out = pl.pallas_call(
        lambda *refs: grid_kernel(n, first, last, grids, *refs),
        out_shape=out_shape,
        in_specs=[VMEM] * len(args),
        out_specs=[VMEM] * len(out_shape),
        input_output_aliases={} if first else {n: 0},
        compiler_params=PARAMS,
        cost_estimate=pl.CostEstimate(flops=flops, bytes_accessed=slots * PIECE_ROWS * LANES, transcendentals=0),
        name="grid",
    )(*args)
    return tuple(out) if last else out[0]


def two_parts(value):
    high = value.astype(jnp.bfloat16)
    return high, (value - high.astype(jnp.float32)).astype(jnp.bfloat16)


def image_kernel(acc_ref, mine_ref, other_ref, row_ref, col_ref, out_ref):
    s1 = mine_ref[0:1, :] + other_ref[0:1, :]
    s2 = mine_ref[8:9, :] + other_ref[8:9, :]
    factor = 2.5 * s1 / s2
    width = out_ref.shape[3]
    half = 2 * width
    done = []
    for t in range(NT_C):
        tiles = [[acc_ref.at[4 * t + 2 * pr + pc] for pr in range(2)] for pc in range(2)]
        weights = [[1.0 / (1.0 + factor * tile[:, :P_SIZE]) for tile in pair] for pair in tiles]
        for pol in range(POLS):
            cells = []
            for e in (1 + 2 * pol, 2 + 2 * pol):
                for pc in range(2):
                    strip = [
                        tiles[pc][pr][:, e * P_SIZE : (e + 1) * P_SIZE] * weights[pc][pr] for pr in range(2)
                    ]
                    cells.append(jnp.concatenate(strip, axis=1))
            high, low = two_parts(jnp.concatenate(cells, axis=0))
            both = jnp.dot(row_ref[...], high, preferred_element_type=jnp.float32)
            rest = jnp.dot(row_ref[:half], low, preferred_element_type=jnp.float32)
            done.append(both[:half] + both[half:] + rest)
    high, low = two_parts(jnp.concatenate(done, axis=0))
    both = jnp.dot(high, col_ref[...], preferred_element_type=jnp.float32)
    rest = jnp.dot(low, col_ref[:, : 2 * G], preferred_element_type=jnp.float32)
    done = both[:, : 2 * G] + both[:, 2 * G :] + rest
    for t in range(NT_C):
        for pol in range(POLS):
            at = (t * POLS + pol) * half
            real, imag = done[at : at + width], done[at + width : at + half]
            out_ref[pol, 0, t] = real[:, :G] + imag[:, G:]
            out_ref[pol, 1, t] = imag[:, :G] - real[:, G:]


def make_image(acc, mine, other, row_table, col_table, width):
    return pl.pallas_call(
        image_kernel,
        out_shape=jax.ShapeDtypeStruct((POLS, 2, NT_C, width, G), jnp.float32),
        in_specs=[VMEM] * 5,
        out_specs=VMEM,
        compiler_params=PARAMS,
        name="image",
    )(acc, mine, other, row_table, col_table)


def dft_tables():
    index = np.arange(G)
    phase = (index[:, None] * index[None, :] % G) * (2.0 * math.pi / G)
    return np.cos(phase).astype(np.float32), np.sin(phase).astype(np.float32)


def np_parts(table, axis):
    high = table.astype(ml_dtypes.bfloat16)
    low = (table - high.astype(np.float32)).astype(ml_dtypes.bfloat16)
    return np.concatenate([high, low], axis=axis)


def image_tables(n_tm):
    cosine, sine = dft_tables()
    rows = []
    for cos_part, sin_part in zip(np.split(cosine, n_tm, axis=1), np.split(sine, n_tm, axis=1)):
        rows.append(np_parts(np.block([[cos_part, -sin_part], [sin_part, cos_part]]).T, 0))
    return np.stack(rows), np_parts(np.concatenate([cosine, sine], axis=1) / G, 1)


def by_gather(packed, n_tm, n_tile):
    order = list(range(0, n_tm, 2)) + list(range(1, n_tm, 2))[::-1]
    ways = [[], []]
    for i in range(n_tm):
        for tile in range(n_tile):
            here, there = (n_tile * order[k] + tile for k in (i, (i + 1) % n_tm))
            ways[tile % 2].append((here, there))
            ways[1 - tile % 2].append((there, here))

    def both_ways(pair):
        return [lax.ppermute(a, ("tm", "tile"), way) for a, way in zip(pair, ways)]

    leading = both_ways(packed)
    trailing = both_ways(packed[::-1])
    acc = add_blocks(None, packed)
    for step in range(2, n_tm // 2 + 1):
        following = both_ways(leading)
        acc = add_blocks(acc, leading)
        acc, *trailing = lax.optimization_barrier((acc, *trailing))
        leading = following
        following = both_ways(trailing) if step < n_tm // 2 else None
        acc = add_blocks(acc, trailing)
        trailing = following
    acc = add_blocks(acc, leading[:1], grids=range(1))
    acc, sums = add_blocks(acc, leading[1:], last=True, grids=range(1))
    return add_blocks(acc, leading, grids=range(1, GRIDS)), sums


def rest_by_rows(acc, cosine, sine):
    grid = acc.reshape(NT_C, 2, 2, P_SIZE, GRIDS, P_SIZE)
    flat = jnp.transpose(grid, (4, 0, 1, 5, 2, 3)).reshape(GRIDS, NT_C * G, G)
    owned = lax.psum_scatter(flat, "tm", scatter_dimension=1, tiled=True)
    dens = owned[0]
    totals = lax.psum((jnp.sum(dens), jnp.sum(dens * dens)), ("tm", "tile"))
    factor = 2.5 * totals[0] / totals[1]
    weighted = owned[1:] / (1.0 + factor * dens[None])
    weighted = weighted.reshape(POLS, 2, dens.shape[0], G)
    real, imag = weighted[:, 0], weighted[:, 1]

    def rows(a, b):
        return jnp.einsum("prj,jn->prn", a, b, precision=HIGH)

    done = jnp.stack([rows(real, cosine) + rows(imag, sine), rows(imag, cosine) - rows(real, sine)], axis=1)
    width = G // lax.axis_size("tm")
    every_row = lax.all_gather(done, "tm", axis=2, tiled=True)
    columns = lax.dynamic_slice_in_dim(every_row, lax.axis_index("tm") * width, width, 3)
    columns = columns.reshape(POLS, 2, NT_C, G, width)
    real, imag = columns[:, 0], columns[:, 1]

    def cols(a, b):
        return jnp.einsum("mi,ptic->ptcm", a, b, precision=HIGH)

    out = jnp.stack([cols(cosine, real) + cols(sine, imag), cols(cosine, imag) - cols(sine, real)], axis=1)
    return out / G


def body(vis_data, vis_weight, kernel_taps, offsets, block_patch, block_count):
    slots = vis_weight.shape[1]
    n_tm = lax.axis_size("tm")
    pieces = (slots // 2, slots - slots // 2)
    packed = pack(pieces, vis_data[0], vis_weight[0], kernel_taps[0], offsets[0], block_patch, block_count)
    if n_tm > 8:
        cosine, sine = dft_tables()
        return rest_by_rows(add_blocks(None, packed), jnp.asarray(cosine), jnp.asarray(sine))
    n_tile = lax.axis_size("tile")
    acc, mine = by_gather(packed, n_tm, n_tile)
    other = lax.ppermute(mine, "tile", [(i, n_tile - 1 - i) for i in range(n_tile)])
    row_tables, col_table = image_tables(n_tm)
    row_table = lax.dynamic_index_in_dim(jnp.asarray(row_tables), lax.axis_index("tm"), 0, keepdims=False)
    return make_image(acc, mine, other, row_table, jnp.asarray(col_table), G // n_tm)


def solution(mesh):
    return jax.shard_map(
        body,
        mesh=mesh,
        in_specs=(
            P(("grp", "tile"), "tm", None, None),
            P(("grp", "tile"), "tm", None),
            P(("grp", "tile"), "tm", None, None, None),
            P(("grp", "tile"), "tm", None, None),
            P(("grp", "tile"), "tm"),
            P(("grp", "tile"), "tm"),
        ),
        out_specs=P(None, None, ("grp", "tile"), "tm", None),
        check_vma=False,
    )
```

```python
import math

import jax
import jax.numpy as jnp
import ml_dtypes
import numpy as np
from jax import lax
from jax.experimental import pallas as pl
from jax.experimental.pallas import tpu as pltpu
from jax.sharding import PartitionSpec as P

G = 256
P_SIZE = 128
K = 8
B = 256
POLS = 2
NT_C = 2
PATCHES = 4 * NT_C
GRIDS = 1 + 2 * POLS
LANES = 128
HALVES = B // LANES
AUX = GRIDS + 2
TAP_ROWS = 2 * HALVES * K
ID_START = TAP_ROWS + AUX * HALVES
PIECE_ROWS = ID_START + 1
HIGH = lax.Precision.HIGHEST
VMEM = pl.BlockSpec(memory_space=pltpu.VMEM)
PARAMS = pltpu.CompilerParams(vmem_limit_bytes=20 * 1024 * 1024)


def half_lanes(half):
    return slice(half * LANES, (half + 1) * LANES)


def pack_kernel(pieces, vis_hbm, weight_hbm, taps_hbm, offs_hbm, patch_hbm, count_ref, *refs):
    outs, scratch = refs[: len(pieces)], refs[len(pieces) :]
    vis_ref, weight_ref, taps_ref, offs_ref, patch_ref, sems = scratch
    pairs = (
        (offs_hbm, offs_ref),
        (taps_hbm, taps_ref),
        (weight_hbm, weight_ref),
        (vis_hbm, vis_ref),
        (patch_hbm, patch_ref),
    )
    copies = [pltpu.make_async_copy(a, b, sems.at[i]) for i, (a, b) in enumerate(pairs)]
    for copy in copies:
        copy.start()
    bases = [sum(pieces[:i]) for i in range(len(pieces))]
    copies[0].wait()
    copies[1].wait()
    for out_ref, n, base in zip(outs, pieces, bases):
        for j in range(n):
            for side in range(2):
                off = offs_ref[base + j, side : side + 1, :]
                taps = taps_ref[base + j, side]
                for bit in range(3):
                    moved = pltpu.roll(taps, 1 << bit, 0)
                    turn = jnp.broadcast_to((off >> bit) & 1, taps.shape) == 1
                    taps = jnp.where(turn, moved, taps)
                for half in range(HALVES):
                    at = j * TAP_ROWS + (side * HALVES + half) * K
                    out_ref[at : at + K, :] = taps[:, half_lanes(half)]
    copies[2].wait()
    copies[3].wait()
    copies[4].wait()
    for out_ref, n, base in zip(outs, pieces, bases):
        for half in range(HALVES):
            lanes = half_lanes(half)
            weight = weight_ref[base : base + n, lanes]
            kinds = [weight] + [weight * vis_ref[base : base + n, m, lanes] for m in range(2 * POLS)]
            kinds += [offs_ref[base : base + n, side, lanes].astype(jnp.float32) for side in range(2)]
            for kind, rows in enumerate(kinds):
                at = n * (TAP_ROWS + kind * HALVES + half)
                out_ref[at : at + n, :] = rows
        for j in range(n):
            patch = jnp.where(base + j < count_ref[0, 0], patch_ref[0, base + j], -1)
            row = jnp.full((1, LANES), patch, jnp.int32).astype(jnp.float32)
            out_ref[n * ID_START + j : n * ID_START + j + 1, :] = row


def pack(pieces, vis, weight, taps, offs, patches, count):
    arrays = (vis, weight, taps, offs, patches)
    spaces = [pltpu.VMEM] * 4 + [pltpu.SMEM]
    hbm, smem = pl.BlockSpec(memory_space=pltpu.HBM), pl.BlockSpec(memory_space=pltpu.SMEM)
    return pl.pallas_call(
        lambda *refs: pack_kernel(pieces, *refs),
        out_shape=[jax.ShapeDtypeStruct((n * PIECE_ROWS, LANES), jnp.float32) for n in pieces],
        in_specs=[hbm] * 5 + [smem],
        out_specs=[VMEM] * len(pieces),
        scratch_shapes=[space(a.shape, a.dtype) for space, a in zip(spaces, arrays)] + [pltpu.SemaphoreType.DMA((5,))],
        compiler_params=PARAMS,
        name="pack",
    )(*[pltpu.with_memory_space_constraint(a, pltpu.HBM) for a in arrays], count)


def spread(off):
    row = lax.broadcasted_iota(jnp.int32, (16, B), 0)
    gap = off.astype(jnp.int32) - row
    step = (gap + 15) >> 4
    inside = (step << 4) - gap < K
    return jnp.where(inside, step, -1).astype(jnp.float32).astype(jnp.bfloat16)


def slot_taps(buf_ref, j, side):
    starts = [j * TAP_ROWS + (side * HALVES + half) * K for half in range(HALVES)]
    rows = jnp.concatenate([buf_ref[at : at + K, :] for at in starts], axis=1)
    return jnp.concatenate([rows, rows], axis=0)


def slot_row(buf_ref, n, j, kind):
    starts = [n * (TAP_ROWS + kind * HALVES + half) + j for half in range(HALVES)]
    return jnp.concatenate([buf_ref[at : at + 1, :] for at in starts], axis=1)


def slot_patch(buf_ref, n, j):
    return buf_ref[n * ID_START + j : n * ID_START + j + 1, 0:1][0, 0].astype(jnp.int32)


def block_factors(buf_ref, n, j, live, grids):
    rows_u = slot_taps(buf_ref, j, 0)
    rows_v = slot_taps(buf_ref, j, 1)
    step_u = spread(slot_row(buf_ref, n, j, GRIDS))
    step_v = spread(slot_row(buf_ref, n, j, GRIDS + 1))
    if live is not None:
        rows_v = jnp.where(live, rows_v, 0.0)
    rows_v = rows_v.astype(jnp.bfloat16)
    zero = jnp.zeros((16, B), jnp.bfloat16)
    steps = P_SIZE // 16
    right = jnp.concatenate([jnp.where(step_v == s, rows_v, zero) for s in range(steps)], axis=0)
    hits = [step_u == s for s in range(steps)]
    left = []
    for e in grids:
        product = (rows_u * slot_row(buf_ref, n, j, e)).astype(jnp.bfloat16)
        left += [jnp.where(hit, product, zero) for hit in hits]
    return jnp.concatenate(left, axis=0), right


def add_some(buf_ref, acc_ref, n, slots, grids):
    lanes = slice(grids[0] * P_SIZE, (grids[-1] + 1) * P_SIZE)
    waiting = None
    for i, j in enumerate(slots):
        where_at = slot_patch(buf_ref, n, j)
        left, right = block_factors(buf_ref, n, j, where_at >= 0 if i else None, grids)
        patch = lax.dot_general(
            right, left, (((1,), (1,)), ((), ())), preferred_element_type=jnp.float32
        )
        if waiting is not None:
            acc_ref[waiting[0], :, lanes] += waiting[1]
        waiting = jnp.maximum(where_at, 0), patch
    acc_ref[waiting[0], :, lanes] += waiting[1]


def grid_kernel(n_bufs, first, last, grids, *refs):
    acc_ref = refs[n_bufs] if first else refs[n_bufs + 1]
    if first:
        acc_ref[...] = jnp.zeros_like(acc_ref)
    for buf_ref in refs[:n_bufs]:
        n = buf_ref.shape[0] // PIECE_ROWS
        for low in range(0, n, 8):
            few, many = range(low, min(low + 4, n)), range(low, min(low + 8, n))
            some = slot_patch(buf_ref, n, low) >= 0
            more = slot_patch(buf_ref, n, low + 4) >= 0 if len(many) > 4 else jnp.bool_(False)

            @pl.when(more)
            def _(buf_ref=buf_ref, n=n, many=many):
                add_some(buf_ref, acc_ref, n, many, grids)

            @pl.when(jnp.logical_and(some, jnp.logical_not(more)))
            def _(buf_ref=buf_ref, n=n, few=few):
                add_some(buf_ref, acc_ref, n, few, grids)

    if last:
        sums_ref = refs[-1]
        dens = acc_ref[:, :, :P_SIZE]
        for i, value in enumerate((dens, dens * dens)):
            part = jnp.sum(value.reshape(-1, 8, P_SIZE), axis=0)
            part = jnp.sum(jnp.sum(part, axis=0, keepdims=True), axis=1, keepdims=True)
            sums_ref[8 * i : 8 * i + 8, :] = jnp.broadcast_to(part, (8, P_SIZE))


def add_blocks(acc, bufs, last=False, grids=range(GRIDS)):
    first = acc is None
    n = len(bufs)
    slots = sum(buf.shape[0] for buf in bufs) // PIECE_ROWS
    out_shape = [jax.ShapeDtypeStruct((PATCHES, P_SIZE, GRIDS * P_SIZE), jnp.float32)]
    if last:
        out_shape.append(jax.ShapeDtypeStruct((16, P_SIZE), jnp.float32))
    args = list(bufs) + ([] if first else [acc])
    flops = (2 if first else 4) * slots * len(grids) * P_SIZE * P_SIZE * B
    out = pl.pallas_call(
        lambda *refs: grid_kernel(n, first, last, grids, *refs),
        out_shape=out_shape,
        in_specs=[VMEM] * len(args),
        out_specs=[VMEM] * len(out_shape),
        input_output_aliases={} if first else {n: 0},
        compiler_params=PARAMS,
        cost_estimate=pl.CostEstimate(flops=flops, bytes_accessed=slots * PIECE_ROWS * LANES, transcendentals=0),
        name="grid",
    )(*args)
    return tuple(out) if last else out[0]


def two_parts(value):
    high = value.astype(jnp.bfloat16)
    return high, (value - high.astype(jnp.float32)).astype(jnp.bfloat16)


def image_kernel(acc_ref, mine_ref, other_ref, row_ref, col_ref, out_ref):
    s1 = mine_ref[0:1, :] + other_ref[0:1, :]
    s2 = mine_ref[8:9, :] + other_ref[8:9, :]
    factor = 2.5 * s1 / s2
    width = out_ref.shape[3]
    half = 2 * width
    done = []
    for t in range(NT_C):
        tiles = [[acc_ref.at[4 * t + 2 * pr + pc] for pr in range(2)] for pc in range(2)]
        weights = [[1.0 / (1.0 + factor * tile[:, :P_SIZE]) for tile in pair] for pair in tiles]
        for pol in range(POLS):
            cells = []
            for e in (1 + 2 * pol, 2 + 2 * pol):
                for pc in range(2):
                    strip = [
                        tiles[pc][pr][:, e * P_SIZE : (e + 1) * P_SIZE] * weights[pc][pr] for pr in range(2)
                    ]
                    cells.append(jnp.concatenate(strip, axis=1))
            cells = jnp.concatenate(cells, axis=0).astype(jnp.bfloat16)
            both = jnp.dot(row_ref[...], cells, preferred_element_type=jnp.float32)
            done.append(both[:half] + both[half:])
    high, low = two_parts(jnp.concatenate(done, axis=0))
    both = jnp.dot(high, col_ref[...], preferred_element_type=jnp.float32)
    rest = jnp.dot(low, col_ref[:, : 2 * G], preferred_element_type=jnp.float32)
    done = both[:, : 2 * G] + both[:, 2 * G :] + rest
    for t in range(NT_C):
        for pol in range(POLS):
            at = (t * POLS + pol) * half
            real, imag = done[at : at + width], done[at + width : at + half]
            out_ref[pol, 0, t] = real[:, :G] + imag[:, G:]
            out_ref[pol, 1, t] = imag[:, :G] - real[:, G:]


def make_image(acc, mine, other, row_table, col_table, width):
    return pl.pallas_call(
        image_kernel,
        out_shape=jax.ShapeDtypeStruct((POLS, 2, NT_C, width, G), jnp.float32),
        in_specs=[VMEM] * 5,
        out_specs=VMEM,
        compiler_params=PARAMS,
        name="image",
    )(acc, mine, other, row_table, col_table)


def dft_tables():
    index = np.arange(G)
    phase = (index[:, None] * index[None, :] % G) * (2.0 * math.pi / G)
    return np.cos(phase).astype(np.float32), np.sin(phase).astype(np.float32)


def np_parts(table, axis):
    high = table.astype(ml_dtypes.bfloat16)
    low = (table - high.astype(np.float32)).astype(ml_dtypes.bfloat16)
    return np.concatenate([high, low], axis=axis)


def image_tables(n_tm):
    cosine, sine = dft_tables()
    rows = []
    for cos_part, sin_part in zip(np.split(cosine, n_tm, axis=1), np.split(sine, n_tm, axis=1)):
        rows.append(np_parts(np.block([[cos_part, -sin_part], [sin_part, cos_part]]).T, 0))
    return np.stack(rows), np_parts(np.concatenate([cosine, sine], axis=1) / G, 1)


def by_gather(packed, n_tm, n_tile):
    order = list(range(0, n_tm, 2)) + list(range(1, n_tm, 2))[::-1]
    ways = [[], []]
    for i in range(n_tm):
        for tile in range(n_tile):
            here, there = (n_tile * order[k] + tile for k in (i, (i + 1) % n_tm))
            ways[tile % 2].append((here, there))
            ways[1 - tile % 2].append((there, here))

    def both_ways(pair):
        return [lax.ppermute(a, ("tm", "tile"), way) for a, way in zip(pair, ways)]

    leading = both_ways(packed)
    trailing = both_ways(packed[::-1])
    acc = add_blocks(None, packed)
    for step in range(2, n_tm // 2 + 1):
        following = both_ways(leading)
        acc = add_blocks(acc, leading)
        acc, *trailing = lax.optimization_barrier((acc, *trailing))
        leading = following
        following = both_ways(trailing) if step < n_tm // 2 else None
        acc = add_blocks(acc, trailing)
        trailing = following
    acc, sums = add_blocks(acc, leading, last=True, grids=range(1))
    return add_blocks(acc, leading, grids=range(1, GRIDS)), sums


def rest_by_rows(acc, cosine, sine):
    grid = acc.reshape(NT_C, 2, 2, P_SIZE, GRIDS, P_SIZE)
    flat = jnp.transpose(grid, (4, 0, 1, 5, 2, 3)).reshape(GRIDS, NT_C * G, G)
    owned = lax.psum_scatter(flat, "tm", scatter_dimension=1, tiled=True)
    dens = owned[0]
    totals = lax.psum((jnp.sum(dens), jnp.sum(dens * dens)), ("tm", "tile"))
    factor = 2.5 * totals[0] / totals[1]
    weighted = owned[1:] / (1.0 + factor * dens[None])
    weighted = weighted.reshape(POLS, 2, dens.shape[0], G)
    real, imag = weighted[:, 0], weighted[:, 1]

    def rows(a, b):
        return jnp.einsum("prj,jn->prn", a, b, precision=HIGH)

    done = jnp.stack([rows(real, cosine) + rows(imag, sine), rows(imag, cosine) - rows(real, sine)], axis=1)
    width = G // lax.axis_size("tm")
    every_row = lax.all_gather(done, "tm", axis=2, tiled=True)
    columns = lax.dynamic_slice_in_dim(every_row, lax.axis_index("tm") * width, width, 3)
    columns = columns.reshape(POLS, 2, NT_C, G, width)
    real, imag = columns[:, 0], columns[:, 1]

    def cols(a, b):
        return jnp.einsum("mi,ptic->ptcm", a, b, precision=HIGH)

    out = jnp.stack([cols(cosine, real) + cols(sine, imag), cols(cosine, imag) - cols(sine, real)], axis=1)
    return out / G


def body(vis_data, vis_weight, kernel_taps, offsets, block_patch, block_count):
    slots = vis_weight.shape[1]
    n_tm = lax.axis_size("tm")
    pieces = (slots // 2, slots - slots // 2)
    packed = pack(pieces, vis_data[0], vis_weight[0], kernel_taps[0], offsets[0], block_patch, block_count)
    if n_tm > 8:
        cosine, sine = dft_tables()
        return rest_by_rows(add_blocks(None, packed), jnp.asarray(cosine), jnp.asarray(sine))
    n_tile = lax.axis_size("tile")
    acc, mine = by_gather(packed, n_tm, n_tile)
    other = lax.ppermute(mine, "tile", [(i, n_tile - 1 - i) for i in range(n_tile)])
    row_tables, col_table = image_tables(n_tm)
    row_table = lax.dynamic_index_in_dim(jnp.asarray(row_tables), lax.axis_index("tm"), 0, keepdims=False)
    return make_image(acc, mine, other, row_table, jnp.asarray(col_table), G // n_tm)


def solution(mesh):
    return jax.shard_map(
        body,
        mesh=mesh,
        in_specs=(
            P(("grp", "tile"), "tm", None, None),
            P(("grp", "tile"), "tm", None),
            P(("grp", "tile"), "tm", None, None, None),
            P(("grp", "tile"), "tm", None, None),
            P(("grp", "tile"), "tm"),
            P(("grp", "tile"), "tm"),
        ),
        out_specs=P(None, None, ("grp", "tile"), "tm", None),
        check_vma=False,
    )
```

```python
import math

import jax
import jax.numpy as jnp
import ml_dtypes
import numpy as np
from jax import lax
from jax.experimental import pallas as pl
from jax.experimental.pallas import tpu as pltpu
from jax.sharding import PartitionSpec as P

G = 256
P_SIZE = 128
K = 8
B = 256
POLS = 2
NT_C = 2
PATCHES = 4 * NT_C
GRIDS = 1 + 2 * POLS
LANES = 128
HALVES = B // LANES
AUX = GRIDS + 2
TAP_ROWS = 2 * HALVES * K
ID_START = TAP_ROWS + AUX * HALVES
PIECE_ROWS = ID_START + 1
HIGH = lax.Precision.HIGHEST
VMEM = pl.BlockSpec(memory_space=pltpu.VMEM)
PARAMS = pltpu.CompilerParams(vmem_limit_bytes=20 * 1024 * 1024)


def half_lanes(half):
    return slice(half * LANES, (half + 1) * LANES)


def pack_kernel(pieces, vis_hbm, weight_hbm, taps_hbm, offs_hbm, patch_hbm, count_ref, *refs):
    outs, scratch = refs[: len(pieces)], refs[len(pieces) :]
    vis_ref, weight_ref, taps_ref, offs_ref, patch_ref, sems = scratch
    pairs = (
        (offs_hbm, offs_ref),
        (taps_hbm, taps_ref),
        (weight_hbm, weight_ref),
        (vis_hbm, vis_ref),
        (patch_hbm, patch_ref),
    )
    copies = [pltpu.make_async_copy(a, b, sems.at[i]) for i, (a, b) in enumerate(pairs)]
    for copy in copies:
        copy.start()
    bases = [sum(pieces[:i]) for i in range(len(pieces))]
    copies[0].wait()
    copies[1].wait()
    for out_ref, n, base in zip(outs, pieces, bases):
        for j in range(n):
            for side in range(2):
                off = offs_ref[base + j, side : side + 1, :]
                taps = taps_ref[base + j, side]
                for bit in range(3):
                    moved = pltpu.roll(taps, 1 << bit, 0)
                    turn = jnp.broadcast_to((off >> bit) & 1, taps.shape) == 1
                    taps = jnp.where(turn, moved, taps)
                for half in range(HALVES):
                    at = j * TAP_ROWS + (side * HALVES + half) * K
                    out_ref[at : at + K, :] = taps[:, half_lanes(half)]
    copies[2].wait()
    copies[3].wait()
    copies[4].wait()
    for out_ref, n, base in zip(outs, pieces, bases):
        for half in range(HALVES):
            lanes = half_lanes(half)
            weight = weight_ref[base : base + n, lanes]
            kinds = [weight] + [weight * vis_ref[base : base + n, m, lanes] for m in range(2 * POLS)]
            kinds += [offs_ref[base : base + n, side, lanes].astype(jnp.float32) for side in range(2)]
            for kind, rows in enumerate(kinds):
                at = n * (TAP_ROWS + kind * HALVES + half)
                out_ref[at : at + n, :] = rows
        for j in range(n):
            patch = jnp.where(base + j < count_ref[0, 0], patch_ref[0, base + j], -1)
            row = jnp.full((1, LANES), patch, jnp.int32).astype(jnp.float32)
            out_ref[n * ID_START + j : n * ID_START + j + 1, :] = row


def pack(pieces, vis, weight, taps, offs, patches, count):
    arrays = (vis, weight, taps, offs, patches)
    spaces = [pltpu.VMEM] * 4 + [pltpu.SMEM]
    hbm, smem = pl.BlockSpec(memory_space=pltpu.HBM), pl.BlockSpec(memory_space=pltpu.SMEM)
    return pl.pallas_call(
        lambda *refs: pack_kernel(pieces, *refs),
        out_shape=[jax.ShapeDtypeStruct((n * PIECE_ROWS, LANES), jnp.float32) for n in pieces],
        in_specs=[hbm] * 5 + [smem],
        out_specs=[VMEM] * len(pieces),
        scratch_shapes=[space(a.shape, a.dtype) for space, a in zip(spaces, arrays)] + [pltpu.SemaphoreType.DMA((5,))],
        compiler_params=PARAMS,
        name="pack",
    )(*[pltpu.with_memory_space_constraint(a, pltpu.HBM) for a in arrays], count)


def spread(off):
    row = lax.broadcasted_iota(jnp.int32, (16, B), 0)
    gap = off.astype(jnp.int32) - row
    step = (gap + 15) >> 4
    inside = (step << 4) - gap < K
    return jnp.where(inside, step, -1).astype(jnp.float32).astype(jnp.bfloat16)


def slot_taps(buf_ref, j, side):
    starts = [j * TAP_ROWS + (side * HALVES + half) * K for half in range(HALVES)]
    rows = jnp.concatenate([buf_ref[at : at + K, :] for at in starts], axis=1)
    return jnp.concatenate([rows, rows], axis=0)


def slot_row(buf_ref, n, j, kind):
    starts = [n * (TAP_ROWS + kind * HALVES + half) + j for half in range(HALVES)]
    return jnp.concatenate([buf_ref[at : at + 1, :] for at in starts], axis=1)


def slot_patch(buf_ref, n, j):
    return buf_ref[n * ID_START + j : n * ID_START + j + 1, 0:1][0, 0].astype(jnp.int32)


def block_factors(buf_ref, n, j, live, grids):
    rows_u = slot_taps(buf_ref, j, 0)
    rows_v = slot_taps(buf_ref, j, 1)
    step_u = spread(slot_row(buf_ref, n, j, GRIDS))
    step_v = spread(slot_row(buf_ref, n, j, GRIDS + 1))
    if live is not None:
        rows_v = jnp.where(live, rows_v, 0.0)
    rows_v = rows_v.astype(jnp.bfloat16)
    zero = jnp.zeros((16, B), jnp.bfloat16)
    steps = P_SIZE // 16
    right = jnp.concatenate([jnp.where(step_v == s, rows_v, zero) for s in range(steps)], axis=0)
    hits = [step_u == s for s in range(steps)]
    left = []
    for e in grids:
        product = (rows_u * slot_row(buf_ref, n, j, e)).astype(jnp.bfloat16)
        left += [jnp.where(hit, product, zero) for hit in hits]
    return jnp.concatenate(left, axis=0), right


def add_some(buf_ref, acc_ref, n, slots, grids):
    lanes = slice(grids[0] * P_SIZE, (grids[-1] + 1) * P_SIZE)
    waiting = None
    for i, j in enumerate(slots):
        where_at = slot_patch(buf_ref, n, j)
        left, right = block_factors(buf_ref, n, j, where_at >= 0 if i else None, grids)
        patch = lax.dot_general(
            right, left, (((1,), (1,)), ((), ())), preferred_element_type=jnp.float32
        )
        if waiting is not None:
            acc_ref[waiting[0], :, lanes] += waiting[1]
        waiting = jnp.maximum(where_at, 0), patch
    acc_ref[waiting[0], :, lanes] += waiting[1]


def grid_kernel(n_bufs, first, last, grids, *refs):
    acc_ref = refs[n_bufs] if first else refs[n_bufs + 1]
    if first:
        acc_ref[...] = jnp.zeros_like(acc_ref)
    for buf_ref in refs[:n_bufs]:
        n = buf_ref.shape[0] // PIECE_ROWS
        for low in range(0, n, 8):
            few, many = range(low, min(low + 4, n)), range(low, min(low + 8, n))
            some = slot_patch(buf_ref, n, low) >= 0
            more = slot_patch(buf_ref, n, low + 4) >= 0 if len(many) > 4 else jnp.bool_(False)

            @pl.when(more)
            def _(buf_ref=buf_ref, n=n, many=many):
                add_some(buf_ref, acc_ref, n, many, grids)

            @pl.when(jnp.logical_and(some, jnp.logical_not(more)))
            def _(buf_ref=buf_ref, n=n, few=few):
                add_some(buf_ref, acc_ref, n, few, grids)

    if last:
        sums_ref = refs[-1]
        dens = acc_ref[:, :, :P_SIZE]
        for i, value in enumerate((dens, dens * dens)):
            part = jnp.sum(value.reshape(-1, 8, P_SIZE), axis=0)
            part = jnp.sum(jnp.sum(part, axis=0, keepdims=True), axis=1, keepdims=True)
            sums_ref[8 * i : 8 * i + 8, :] = jnp.broadcast_to(part, (8, P_SIZE))


def add_blocks(acc, bufs, last=False, grids=range(GRIDS)):
    first = acc is None
    n = len(bufs)
    slots = sum(buf.shape[0] for buf in bufs) // PIECE_ROWS
    out_shape = [jax.ShapeDtypeStruct((PATCHES, P_SIZE, GRIDS * P_SIZE), jnp.float32)]
    if last:
        out_shape.append(jax.ShapeDtypeStruct((16, P_SIZE), jnp.float32))
    args = list(bufs) + ([] if first else [acc])
    flops = (2 if first else 4) * slots * len(grids) * P_SIZE * P_SIZE * B
    out = pl.pallas_call(
        lambda *refs: grid_kernel(n, first, last, grids, *refs),
        out_shape=out_shape,
        in_specs=[VMEM] * len(args),
        out_specs=[VMEM] * len(out_shape),
        input_output_aliases={} if first else {n: 0},
        compiler_params=PARAMS,
        cost_estimate=pl.CostEstimate(flops=flops, bytes_accessed=slots * PIECE_ROWS * LANES, transcendentals=0),
        name="grid",
    )(*args)
    return tuple(out) if last else out[0]


def two_parts(value):
    high = value.astype(jnp.bfloat16)
    return high, (value - high.astype(jnp.float32)).astype(jnp.bfloat16)


def image_kernel(acc_ref, mine_ref, other_ref, row_ref, col_ref, out_ref):
    s1 = mine_ref[0:1, :] + other_ref[0:1, :]
    s2 = mine_ref[8:9, :] + other_ref[8:9, :]
    factor = 2.5 * s1 / s2
    width = out_ref.shape[3]
    half = 2 * width
    done = []
    for t in range(NT_C):
        tiles = [[acc_ref.at[4 * t + 2 * pr + pc] for pr in range(2)] for pc in range(2)]
        weights = [[1.0 / (1.0 + factor * tile[:, :P_SIZE]) for tile in pair] for pair in tiles]
        for pol in range(POLS):
            cells = []
            for e in (1 + 2 * pol, 2 + 2 * pol):
                for pc in range(2):
                    strip = [
                        tiles[pc][pr][:, e * P_SIZE : (e + 1) * P_SIZE] * weights[pc][pr] for pr in range(2)
                    ]
                    cells.append(jnp.concatenate(strip, axis=1))
            high, low = two_parts(jnp.concatenate(cells, axis=0))
            both = jnp.dot(row_ref[...], high, preferred_element_type=jnp.float32)
            rest = jnp.dot(row_ref[:half], low, preferred_element_type=jnp.float32)
            done.append(both[:half] + both[half:] + rest)
    high, low = two_parts(jnp.concatenate(done, axis=0))
    both = jnp.dot(high, col_ref[...], preferred_element_type=jnp.float32)
    rest = jnp.dot(low, col_ref[:, : 2 * G], preferred_element_type=jnp.float32)
    done = both[:, : 2 * G] + both[:, 2 * G :] + rest
    for t in range(NT_C):
        for pol in range(POLS):
            at = (t * POLS + pol) * half
            real, imag = done[at : at + width], done[at + width : at + half]
            out_ref[pol, 0, t] = real[:, :G] + imag[:, G:]
            out_ref[pol, 1, t] = imag[:, :G] - real[:, G:]


def make_image(acc, mine, other, row_table, col_table, width):
    return pl.pallas_call(
        image_kernel,
        out_shape=jax.ShapeDtypeStruct((POLS, 2, NT_C, width, G), jnp.float32),
        in_specs=[VMEM] * 5,
        out_specs=VMEM,
        compiler_params=PARAMS,
        name="image",
    )(acc, mine, other, row_table, col_table)


def dft_tables():
    index = np.arange(G)
    phase = (index[:, None] * index[None, :] % G) * (2.0 * math.pi / G)
    return np.cos(phase).astype(np.float32), np.sin(phase).astype(np.float32)


def np_parts(table, axis):
    high = table.astype(ml_dtypes.bfloat16)
    low = (table - high.astype(np.float32)).astype(ml_dtypes.bfloat16)
    return np.concatenate([high, low], axis=axis)


def image_tables(n_tm):
    cosine, sine = dft_tables()
    rows = []
    for cos_part, sin_part in zip(np.split(cosine, n_tm, axis=1), np.split(sine, n_tm, axis=1)):
        rows.append(np_parts(np.block([[cos_part, -sin_part], [sin_part, cos_part]]).T, 0))
    return np.stack(rows), np_parts(np.concatenate([cosine, sine], axis=1) / G, 1)


def by_gather(packed, n_tm, n_tile):
    order = list(range(0, n_tm, 2)) + list(range(1, n_tm, 2))[::-1]
    ways = [[], []]
    for i in range(n_tm):
        for tile in range(n_tile):
            here, there = (n_tile * order[k] + tile for k in (i, (i + 1) % n_tm))
            ways[tile % 2].append((here, there))
            ways[1 - tile % 2].append((there, here))

    def both_ways(pair):
        return [lax.ppermute(a, ("tm", "tile"), way) for a, way in zip(pair, ways)]

    leading = both_ways(packed)
    trailing = both_ways(packed[::-1])
    acc = add_blocks(None, packed)
    for step in range(2, n_tm // 2 + 1):
        following = both_ways(leading)
        acc = add_blocks(acc, leading)
        acc, *trailing = lax.optimization_barrier((acc, *trailing))
        leading = following
        following = both_ways(trailing) if step < n_tm // 2 else None
        acc = add_blocks(acc, trailing)
        trailing = following
    acc, sums = add_blocks(acc, leading, last=True, grids=range(1))
    return add_blocks(acc, leading, grids=range(1, GRIDS)), sums


def rest_by_rows(acc, cosine, sine):
    grid = acc.reshape(NT_C, 2, 2, P_SIZE, GRIDS, P_SIZE)
    flat = jnp.transpose(grid, (4, 0, 1, 5, 2, 3)).reshape(GRIDS, NT_C * G, G)
    owned = lax.psum_scatter(flat, "tm", scatter_dimension=1, tiled=True)
    dens = owned[0]
    totals = lax.psum((jnp.sum(dens), jnp.sum(dens * dens)), ("tm", "tile"))
    factor = 2.5 * totals[0] / totals[1]
    weighted = owned[1:] / (1.0 + factor * dens[None])
    weighted = weighted.reshape(POLS, 2, dens.shape[0], G)
    real, imag = weighted[:, 0], weighted[:, 1]

    def rows(a, b):
        return jnp.einsum("prj,jn->prn", a, b, precision=HIGH)

    done = jnp.stack([rows(real, cosine) + rows(imag, sine), rows(imag, cosine) - rows(real, sine)], axis=1)
    width = G // lax.axis_size("tm")
    every_row = lax.all_gather(done, "tm", axis=2, tiled=True)
    columns = lax.dynamic_slice_in_dim(every_row, lax.axis_index("tm") * width, width, 3)
    columns = columns.reshape(POLS, 2, NT_C, G, width)
    real, imag = columns[:, 0], columns[:, 1]

    def cols(a, b):
        return jnp.einsum("mi,ptic->ptcm", a, b, precision=HIGH)

    out = jnp.stack([cols(cosine, real) + cols(sine, imag), cols(cosine, imag) - cols(sine, real)], axis=1)
    return out / G


def body(vis_data, vis_weight, kernel_taps, offsets, block_patch, block_count):
    slots = vis_weight.shape[1]
    n_tm = lax.axis_size("tm")
    pieces = (slots // 2, slots - slots // 2)
    packed = pack(pieces, vis_data[0], vis_weight[0], kernel_taps[0], offsets[0], block_patch, block_count)
    if n_tm > 8:
        cosine, sine = dft_tables()
        return rest_by_rows(add_blocks(None, packed), jnp.asarray(cosine), jnp.asarray(sine))
    n_tile = lax.axis_size("tile")
    acc, mine = by_gather(packed, n_tm, n_tile)
    other = lax.ppermute(mine, "tile", [(i, n_tile - 1 - i) for i in range(n_tile)])
    row_tables, col_table = image_tables(n_tm)
    row_table = lax.dynamic_index_in_dim(jnp.asarray(row_tables), lax.axis_index("tm"), 0, keepdims=False)
    return make_image(acc, mine, other, row_table, jnp.asarray(col_table), G // n_tm)


def solution(mesh):
    return jax.shard_map(
        body,
        mesh=mesh,
        in_specs=(
            P(("grp", "tile"), "tm", None, None),
            P(("grp", "tile"), "tm", None),
            P(("grp", "tile"), "tm", None, None, None),
            P(("grp", "tile"), "tm", None, None),
            P(("grp", "tile"), "tm"),
            P(("grp", "tile"), "tm"),
        ),
        out_specs=P(None, None, ("grp", "tile"), "tm", None),
        check_vma=False,
    )
```

```python
import math

import jax
import jax.numpy as jnp
import ml_dtypes
import numpy as np
from jax import lax
from jax.experimental import pallas as pl
from jax.experimental.pallas import tpu as pltpu
from jax.sharding import PartitionSpec as P

G = 256
P_SIZE = 128
K = 8
B = 256
POLS = 2
NT_C = 2
PATCHES = 4 * NT_C
GRIDS = 1 + 2 * POLS
LANES = 128
HALVES = B // LANES
AUX = GRIDS + 2
TAP_ROWS = 2 * HALVES * K
ID_START = TAP_ROWS + AUX * HALVES
PIECE_ROWS = ID_START + 1
HIGH = lax.Precision.HIGHEST
VMEM = pl.BlockSpec(memory_space=pltpu.VMEM)
PARAMS = pltpu.CompilerParams(vmem_limit_bytes=20 * 1024 * 1024)


def half_lanes(half):
    return slice(half * LANES, (half + 1) * LANES)


def pack_kernel(pieces, vis_hbm, weight_hbm, taps_hbm, offs_hbm, patch_hbm, count_ref, *refs):
    outs, scratch = refs[: len(pieces)], refs[len(pieces) :]
    vis_ref, weight_ref, taps_ref, offs_ref, patch_ref, sems = scratch
    pairs = (
        (offs_hbm, offs_ref),
        (taps_hbm, taps_ref),
        (weight_hbm, weight_ref),
        (vis_hbm, vis_ref),
        (patch_hbm, patch_ref),
    )
    copies = [pltpu.make_async_copy(a, b, sems.at[i]) for i, (a, b) in enumerate(pairs)]
    for copy in copies:
        copy.start()
    bases = [sum(pieces[:i]) for i in range(len(pieces))]
    copies[0].wait()
    copies[1].wait()
    for out_ref, n, base in zip(outs, pieces, bases):
        for j in range(n):
            for side in range(2):
                off = offs_ref[base + j, side : side + 1, :]
                taps = taps_ref[base + j, side]
                for bit in range(3):
                    moved = pltpu.roll(taps, 1 << bit, 0)
                    turn = jnp.broadcast_to((off >> bit) & 1, taps.shape) == 1
                    taps = jnp.where(turn, moved, taps)
                for half in range(HALVES):
                    at = j * TAP_ROWS + (side * HALVES + half) * K
                    out_ref[at : at + K, :] = taps[:, half_lanes(half)]
    copies[2].wait()
    copies[3].wait()
    copies[4].wait()
    for out_ref, n, base in zip(outs, pieces, bases):
        for half in range(HALVES):
            lanes = half_lanes(half)
            weight = weight_ref[base : base + n, lanes]
            kinds = [weight] + [weight * vis_ref[base : base + n, m, lanes] for m in range(2 * POLS)]
            kinds += [offs_ref[base : base + n, side, lanes].astype(jnp.float32) for side in range(2)]
            for kind, rows in enumerate(kinds):
                at = n * (TAP_ROWS + kind * HALVES + half)
                out_ref[at : at + n, :] = rows
        for j in range(n):
            patch = jnp.where(base + j < count_ref[0, 0], patch_ref[0, base + j], -1)
            row = jnp.full((1, LANES), patch, jnp.int32).astype(jnp.float32)
            out_ref[n * ID_START + j : n * ID_START + j + 1, :] = row


def pack(pieces, vis, weight, taps, offs, patches, count):
    arrays = (vis, weight, taps, offs, patches)
    spaces = [pltpu.VMEM] * 4 + [pltpu.SMEM]
    hbm, smem = pl.BlockSpec(memory_space=pltpu.HBM), pl.BlockSpec(memory_space=pltpu.SMEM)
    return pl.pallas_call(
        lambda *refs: pack_kernel(pieces, *refs),
        out_shape=[jax.ShapeDtypeStruct((n * PIECE_ROWS, LANES), jnp.float32) for n in pieces],
        in_specs=[hbm] * 5 + [smem],
        out_specs=[VMEM] * len(pieces),
        scratch_shapes=[space(a.shape, a.dtype) for space, a in zip(spaces, arrays)] + [pltpu.SemaphoreType.DMA((5,))],
        compiler_params=PARAMS,
        name="pack",
    )(*[pltpu.with_memory_space_constraint(a, pltpu.HBM) for a in arrays], count)


def spread(off):
    row = lax.broadcasted_iota(jnp.int32, (16, B), 0)
    gap = off.astype(jnp.int32) - row
    step = (gap + 15) >> 4
    inside = (step << 4) - gap < K
    return jnp.where(inside, step, -1).astype(jnp.float32).astype(jnp.bfloat16)


def slot_taps(buf_ref, j, side):
    starts = [j * TAP_ROWS + (side * HALVES + half) * K for half in range(HALVES)]
    rows = jnp.concatenate([buf_ref[at : at + K, :] for at in starts], axis=1)
    return jnp.concatenate([rows, rows], axis=0)


def slot_row(buf_ref, n, j, kind):
    starts = [n * (TAP_ROWS + kind * HALVES + half) + j for half in range(HALVES)]
    return jnp.concatenate([buf_ref[at : at + 1, :] for at in starts], axis=1)


def slot_patch(buf_ref, n, j):
    return buf_ref[n * ID_START + j : n * ID_START + j + 1, 0:1][0, 0].astype(jnp.int32)


def block_factors(buf_ref, n, j, live, grids):
    rows_u = slot_taps(buf_ref, j, 0)
    rows_v = slot_taps(buf_ref, j, 1)
    step_u = spread(slot_row(buf_ref, n, j, GRIDS))
    step_v = spread(slot_row(buf_ref, n, j, GRIDS + 1))
    if live is not None:
        rows_v = jnp.where(live, rows_v, 0.0)
    rows_v = rows_v.astype(jnp.bfloat16)
    zero = jnp.zeros((16, B), jnp.bfloat16)
    steps = P_SIZE // 16
    right = jnp.concatenate([jnp.where(step_v == s, rows_v, zero) for s in range(steps)], axis=0)
    hits = [step_u == s for s in range(steps)]
    left = []
    for e in grids:
        product = (rows_u * slot_row(buf_ref, n, j, e)).astype(jnp.bfloat16)
        left += [jnp.where(hit, product, zero) for hit in hits]
    return jnp.concatenate(left, axis=0), right


def add_some(buf_ref, acc_ref, n, slots, grids):
    lanes = slice(grids[0] * P_SIZE, (grids[-1] + 1) * P_SIZE)
    waiting = None
    for i, j in enumerate(slots):
        where_at = slot_patch(buf_ref, n, j)
        left, right = block_factors(buf_ref, n, j, where_at >= 0 if i else None, grids)
        patch = lax.dot_general(
            right, left, (((1,), (1,)), ((), ())), preferred_element_type=jnp.float32
        )
        if waiting is not None:
            acc_ref[waiting[0], :, lanes] += waiting[1]
        waiting = jnp.maximum(where_at, 0), patch
    acc_ref[waiting[0], :, lanes] += waiting[1]


def grid_kernel(n_bufs, first, last, grids, *refs):
    acc_ref = refs[n_bufs] if first else refs[n_bufs + 1]
    if first:
        acc_ref[...] = jnp.zeros_like(acc_ref)
    for buf_ref in refs[:n_bufs]:
        n = buf_ref.shape[0] // PIECE_ROWS
        for low in range(0, n, 8):
            few, many = range(low, min(low + 4, n)), range(low, min(low + 8, n))
            some = slot_patch(buf_ref, n, low) >= 0
            more = slot_patch(buf_ref, n, low + 4) >= 0 if len(many) > 4 else jnp.bool_(False)

            @pl.when(more)
            def _(buf_ref=buf_ref, n=n, many=many):
                add_some(buf_ref, acc_ref, n, many, grids)

            @pl.when(jnp.logical_and(some, jnp.logical_not(more)))
            def _(buf_ref=buf_ref, n=n, few=few):
                add_some(buf_ref, acc_ref, n, few, grids)

    if last:
        sums_ref = refs[-1]
        dens = acc_ref[:, :, :P_SIZE]
        for i, value in enumerate((dens, dens * dens)):
            part = jnp.sum(value.reshape(-1, 8, P_SIZE), axis=0)
            part = jnp.sum(jnp.sum(part, axis=0, keepdims=True), axis=1, keepdims=True)
            sums_ref[8 * i : 8 * i + 8, :] = jnp.broadcast_to(part, (8, P_SIZE))


def add_blocks(acc, bufs, last=False, grids=range(GRIDS)):
    first = acc is None
    n = len(bufs)
    slots = sum(buf.shape[0] for buf in bufs) // PIECE_ROWS
    out_shape = [jax.ShapeDtypeStruct((PATCHES, P_SIZE, GRIDS * P_SIZE), jnp.float32)]
    if last:
        out_shape.append(jax.ShapeDtypeStruct((16, P_SIZE), jnp.float32))
    args = list(bufs) + ([] if first else [acc])
    flops = (2 if first else 4) * slots * len(grids) * P_SIZE * P_SIZE * B
    out = pl.pallas_call(
        lambda *refs: grid_kernel(n, first, last, grids, *refs),
        out_shape=out_shape,
        in_specs=[VMEM] * len(args),
        out_specs=[VMEM] * len(out_shape),
        input_output_aliases={} if first else {n: 0},
        compiler_params=PARAMS,
        cost_estimate=pl.CostEstimate(flops=flops, bytes_accessed=slots * PIECE_ROWS * LANES, transcendentals=0),
        name="grid",
    )(*args)
    return tuple(out) if last else out[0]


def two_parts(value):
    high = value.astype(jnp.bfloat16)
    return high, (value - high.astype(jnp.float32)).astype(jnp.bfloat16)


def image_kernel(acc_ref, mine_ref, other_ref, row_ref, col_ref, out_ref):
    s1 = mine_ref[0:1, :] + other_ref[0:1, :]
    s2 = mine_ref[8:9, :] + other_ref[8:9, :]
    factor = 2.5 * s1 / s2
    width = out_ref.shape[3]
    half = 2 * width
    done = []
    for t in range(NT_C):
        tiles = [[acc_ref.at[4 * t + 2 * pr + pc] for pr in range(2)] for pc in range(2)]
        weights = [[1.0 / (1.0 + factor * tile[:, :P_SIZE]) for tile in pair] for pair in tiles]
        for pol in range(POLS):
            cells = []
            for e in (1 + 2 * pol, 2 + 2 * pol):
                for pc in range(2):
                    strip = [
                        tiles[pc][pr][:, e * P_SIZE : (e + 1) * P_SIZE] * weights[pc][pr] for pr in range(2)
                    ]
                    cells.append(jnp.concatenate(strip, axis=1))
            high, low = two_parts(jnp.concatenate(cells, axis=0))
            both = jnp.dot(row_ref[...], high, preferred_element_type=jnp.float32)
            rest = jnp.dot(row_ref[:half], low, preferred_element_type=jnp.float32)
            done.append(both[:half] + both[half:] + rest)
    high, low = two_parts(jnp.concatenate(done, axis=0))
    both = jnp.dot(high, col_ref[...], preferred_element_type=jnp.float32)
    rest = jnp.dot(low, col_ref[:, : 2 * G], preferred_element_type=jnp.float32)
    done = both[:, : 2 * G] + both[:, 2 * G :] + rest
    for t in range(NT_C):
        for pol in range(POLS):
            at = (t * POLS + pol) * half
            real, imag = done[at : at + width], done[at + width : at + half]
            out_ref[pol, 0, t] = real[:, :G] + imag[:, G:]
            out_ref[pol, 1, t] = imag[:, :G] - real[:, G:]


def make_image(acc, mine, other, row_table, col_table, width):
    return pl.pallas_call(
        image_kernel,
        out_shape=jax.ShapeDtypeStruct((POLS, 2, NT_C, width, G), jnp.float32),
        in_specs=[VMEM] * 5,
        out_specs=VMEM,
        compiler_params=PARAMS,
        name="image",
    )(acc, mine, other, row_table, col_table)


def dft_tables():
    index = np.arange(G)
    phase = (index[:, None] * index[None, :] % G) * (2.0 * math.pi / G)
    return np.cos(phase).astype(np.float32), np.sin(phase).astype(np.float32)


def np_parts(table, axis):
    high = table.astype(ml_dtypes.bfloat16)
    low = (table - high.astype(np.float32)).astype(ml_dtypes.bfloat16)
    return np.concatenate([high, low], axis=axis)


def image_tables(n_tm):
    cosine, sine = dft_tables()
    rows = []
    for cos_part, sin_part in zip(np.split(cosine, n_tm, axis=1), np.split(sine, n_tm, axis=1)):
        rows.append(np_parts(np.block([[cos_part, -sin_part], [sin_part, cos_part]]).T, 0))
    return np.stack(rows), np_parts(np.concatenate([cosine, sine], axis=1) / G, 1)


def by_gather(packed, n_tm, n_tile):
    order = list(range(0, n_tm, 2)) + list(range(1, n_tm, 2))[::-1]
    ways = [[], []]
    for i in range(n_tm):
        for tile in range(n_tile):
            here, there = (n_tile * order[k] + tile for k in (i, (i + 1) % n_tm))
            ways[tile % 2].append((here, there))
            ways[1 - tile % 2].append((there, here))

    def both_ways(pair):
        return [lax.ppermute(a, ("tm", "tile"), way) for a, way in zip(pair, ways)]

    leading = both_ways(packed)
    trailing = both_ways(packed[::-1])
    acc = add_blocks(None, packed[:1])
    for step in range(2, n_tm // 2 + 1):
        following = both_ways(leading)
        acc = add_blocks(acc, leading + (list(packed[1:]) if step == 2 else []))
        acc, *trailing = lax.optimization_barrier((acc, *trailing))
        leading = following
        following = both_ways(trailing) if step < n_tm // 2 else None
        acc = add_blocks(acc, trailing)
        trailing = following
    acc, sums = add_blocks(acc, leading, last=True, grids=range(1))
    return add_blocks(acc, leading, grids=range(1, GRIDS)), sums


def rest_by_rows(acc, cosine, sine):
    grid = acc.reshape(NT_C, 2, 2, P_SIZE, GRIDS, P_SIZE)
    flat = jnp.transpose(grid, (4, 0, 1, 5, 2, 3)).reshape(GRIDS, NT_C * G, G)
    owned = lax.psum_scatter(flat, "tm", scatter_dimension=1, tiled=True)
    dens = owned[0]
    totals = lax.psum((jnp.sum(dens), jnp.sum(dens * dens)), ("tm", "tile"))
    factor = 2.5 * totals[0] / totals[1]
    weighted = owned[1:] / (1.0 + factor * dens[None])
    weighted = weighted.reshape(POLS, 2, dens.shape[0], G)
    real, imag = weighted[:, 0], weighted[:, 1]

    def rows(a, b):
        return jnp.einsum("prj,jn->prn", a, b, precision=HIGH)

    done = jnp.stack([rows(real, cosine) + rows(imag, sine), rows(imag, cosine) - rows(real, sine)], axis=1)
    width = G // lax.axis_size("tm")
    every_row = lax.all_gather(done, "tm", axis=2, tiled=True)
    columns = lax.dynamic_slice_in_dim(every_row, lax.axis_index("tm") * width, width, 3)
    columns = columns.reshape(POLS, 2, NT_C, G, width)
    real, imag = columns[:, 0], columns[:, 1]

    def cols(a, b):
        return jnp.einsum("mi,ptic->ptcm", a, b, precision=HIGH)

    out = jnp.stack([cols(cosine, real) + cols(sine, imag), cols(cosine, imag) - cols(sine, real)], axis=1)
    return out / G


def body(vis_data, vis_weight, kernel_taps, offsets, block_patch, block_count):
    slots = vis_weight.shape[1]
    n_tm = lax.axis_size("tm")
    pieces = (slots // 2, slots - slots // 2)
    packed = pack(pieces, vis_data[0], vis_weight[0], kernel_taps[0], offsets[0], block_patch, block_count)
    if n_tm > 8:
        cosine, sine = dft_tables()
        return rest_by_rows(add_blocks(None, packed), jnp.asarray(cosine), jnp.asarray(sine))
    n_tile = lax.axis_size("tile")
    acc, mine = by_gather(packed, n_tm, n_tile)
    other = lax.ppermute(mine, "tile", [(i, n_tile - 1 - i) for i in range(n_tile)])
    row_tables, col_table = image_tables(n_tm)
    row_table = lax.dynamic_index_in_dim(jnp.asarray(row_tables), lax.axis_index("tm"), 0, keepdims=False)
    return make_image(acc, mine, other, row_table, jnp.asarray(col_table), G // n_tm)


def solution(mesh):
    return jax.shard_map(
        body,
        mesh=mesh,
        in_specs=(
            P(("grp", "tile"), "tm", None, None),
            P(("grp", "tile"), "tm", None),
            P(("grp", "tile"), "tm", None, None, None),
            P(("grp", "tile"), "tm", None, None),
            P(("grp", "tile"), "tm"),
            P(("grp", "tile"), "tm"),
        ),
        out_specs=P(None, None, ("grp", "tile"), "tm", None),
        check_vma=False,
    )
```

```python
import math

import jax
import jax.numpy as jnp
import ml_dtypes
import numpy as np
from jax import lax
from jax.experimental import pallas as pl
from jax.experimental.pallas import tpu as pltpu
from jax.sharding import PartitionSpec as P

G = 256
P_SIZE = 128
K = 8
B = 256
POLS = 2
NT_C = 2
PATCHES = 4 * NT_C
GRIDS = 1 + 2 * POLS
LANES = 128
HALVES = B // LANES
AUX = GRIDS + 2
TAP_ROWS = 2 * HALVES * K
ID_START = TAP_ROWS + AUX * HALVES
PIECE_ROWS = ID_START + 1
HIGH = lax.Precision.HIGHEST
VMEM = pl.BlockSpec(memory_space=pltpu.VMEM)
PARAMS = pltpu.CompilerParams(vmem_limit_bytes=20 * 1024 * 1024)


def half_lanes(half):
    return slice(half * LANES, (half + 1) * LANES)


def pack_kernel(pieces, vis_hbm, weight_hbm, taps_hbm, offs_hbm, patch_hbm, count_ref, *refs):
    outs, scratch = refs[: len(pieces)], refs[len(pieces) :]
    vis_ref, weight_ref, taps_ref, offs_ref, patch_ref, sems = scratch
    pairs = (
        (offs_hbm, offs_ref),
        (taps_hbm, taps_ref),
        (weight_hbm, weight_ref),
        (vis_hbm, vis_ref),
        (patch_hbm, patch_ref),
    )
    copies = [pltpu.make_async_copy(a, b, sems.at[i]) for i, (a, b) in enumerate(pairs)]
    for copy in copies:
        copy.start()
    bases = [sum(pieces[:i]) for i in range(len(pieces))]
    copies[0].wait()
    copies[1].wait()
    for out_ref, n, base in zip(outs, pieces, bases):
        for j in range(n):
            for side in range(2):
                off = offs_ref[base + j, side : side + 1, :]
                taps = taps_ref[base + j, side]
                for bit in range(3):
                    moved = pltpu.roll(taps, 1 << bit, 0)
                    turn = jnp.broadcast_to((off >> bit) & 1, taps.shape) == 1
                    taps = jnp.where(turn, moved, taps)
                for half in range(HALVES):
                    at = j * TAP_ROWS + (side * HALVES + half) * K
                    out_ref[at : at + K, :] = taps[:, half_lanes(half)]
    copies[2].wait()
    copies[3].wait()
    copies[4].wait()
    for out_ref, n, base in zip(outs, pieces, bases):
        for half in range(HALVES):
            lanes = half_lanes(half)
            weight = weight_ref[base : base + n, lanes]
            kinds = [weight] + [weight * vis_ref[base : base + n, m, lanes] for m in range(2 * POLS)]
            kinds += [offs_ref[base : base + n, side, lanes].astype(jnp.float32) for side in range(2)]
            for kind, rows in enumerate(kinds):
                at = n * (TAP_ROWS + kind * HALVES + half)
                out_ref[at : at + n, :] = rows
        for j in range(n):
            patch = jnp.where(base + j < count_ref[0, 0], patch_ref[0, base + j], -1)
            row = jnp.full((1, LANES), patch, jnp.int32).astype(jnp.float32)
            out_ref[n * ID_START + j : n * ID_START + j + 1, :] = row


def pack(pieces, vis, weight, taps, offs, patches, count):
    arrays = (vis, weight, taps, offs, patches)
    spaces = [pltpu.VMEM] * 4 + [pltpu.SMEM]
    hbm, smem = pl.BlockSpec(memory_space=pltpu.HBM), pl.BlockSpec(memory_space=pltpu.SMEM)
    return pl.pallas_call(
        lambda *refs: pack_kernel(pieces, *refs),
        out_shape=[jax.ShapeDtypeStruct((n * PIECE_ROWS, LANES), jnp.float32) for n in pieces],
        in_specs=[hbm] * 5 + [smem],
        out_specs=[VMEM] * len(pieces),
        scratch_shapes=[space(a.shape, a.dtype) for space, a in zip(spaces, arrays)] + [pltpu.SemaphoreType.DMA((5,))],
        compiler_params=PARAMS,
        name="pack",
    )(*[pltpu.with_memory_space_constraint(a, pltpu.HBM) for a in arrays], count)


def spread(off):
    row = lax.broadcasted_iota(jnp.int32, (16, B), 0)
    gap = off.astype(jnp.int32) - row
    step = (gap + 15) >> 4
    inside = (step << 4) - gap < K
    return jnp.where(inside, step, -1).astype(jnp.float32).astype(jnp.bfloat16)


def slot_taps(buf_ref, j, side):
    starts = [j * TAP_ROWS + (side * HALVES + half) * K for half in range(HALVES)]
    rows = jnp.concatenate([buf_ref[at : at + K, :] for at in starts], axis=1)
    return jnp.concatenate([rows, rows], axis=0)


def slot_row(buf_ref, n, j, kind):
    starts = [n * (TAP_ROWS + kind * HALVES + half) + j for half in range(HALVES)]
    return jnp.concatenate([buf_ref[at : at + 1, :] for at in starts], axis=1)


def slot_patch(buf_ref, n, j):
    return buf_ref[n * ID_START + j : n * ID_START + j + 1, 0:1][0, 0].astype(jnp.int32)


def block_factors(buf_ref, n, j, live, grids):
    rows_u = slot_taps(buf_ref, j, 0)
    rows_v = slot_taps(buf_ref, j, 1)
    step_u = spread(slot_row(buf_ref, n, j, GRIDS))
    step_v = spread(slot_row(buf_ref, n, j, GRIDS + 1))
    if live is not None:
        rows_v = jnp.where(live, rows_v, 0.0)
    rows_v = rows_v.astype(jnp.bfloat16)
    zero = jnp.zeros((16, B), jnp.bfloat16)
    steps = P_SIZE // 16
    right = jnp.concatenate([jnp.where(step_v == s, rows_v, zero) for s in range(steps)], axis=0)
    hits = [step_u == s for s in range(steps)]
    left = []
    for e in grids:
        product = (rows_u * slot_row(buf_ref, n, j, e)).astype(jnp.bfloat16)
        left += [jnp.where(hit, product, zero) for hit in hits]
    return jnp.concatenate(left, axis=0), right


def add_some(buf_ref, acc_ref, n, slots, grids):
    lanes = slice(grids[0] * P_SIZE, (grids[-1] + 1) * P_SIZE)
    waiting = None
    for i, j in enumerate(slots):
        where_at = slot_patch(buf_ref, n, j)
        left, right = block_factors(buf_ref, n, j, where_at >= 0 if i else None, grids)
        patch = lax.dot_general(
            right, left, (((1,), (1,)), ((), ())), preferred_element_type=jnp.float32
        )
        if waiting is not None:
            acc_ref[waiting[0], :, lanes] += waiting[1]
        waiting = jnp.maximum(where_at, 0), patch
    acc_ref[waiting[0], :, lanes] += waiting[1]


def grid_kernel(n_bufs, first, last, grids, *refs):
    acc_ref = refs[n_bufs] if first else refs[n_bufs + 1]
    if first:
        acc_ref[...] = jnp.zeros_like(acc_ref)
    for buf_ref in refs[:n_bufs]:
        n = buf_ref.shape[0] // PIECE_ROWS
        for low in range(0, n, 8):
            ends = range(min(low + 2, n), min(low + 8, n) + 1, 2)
            alive = [slot_patch(buf_ref, n, end - 2) >= 0 for end in ends] + [jnp.bool_(False)]
            for i, end in enumerate(ends):

                @pl.when(jnp.logical_and(alive[i], jnp.logical_not(alive[i + 1])))
                def _(buf_ref=buf_ref, n=n, slots=range(low, end)):
                    add_some(buf_ref, acc_ref, n, slots, grids)

    if last:
        sums_ref = refs[-1]
        dens = acc_ref[:, :, :P_SIZE]
        for i, value in enumerate((dens, dens * dens)):
            part = jnp.sum(value.reshape(-1, 8, P_SIZE), axis=0)
            part = jnp.sum(jnp.sum(part, axis=0, keepdims=True), axis=1, keepdims=True)
            sums_ref[8 * i : 8 * i + 8, :] = jnp.broadcast_to(part, (8, P_SIZE))


def add_blocks(acc, bufs, last=False, grids=range(GRIDS)):
    first = acc is None
    n = len(bufs)
    slots = sum(buf.shape[0] for buf in bufs) // PIECE_ROWS
    out_shape = [jax.ShapeDtypeStruct((PATCHES, P_SIZE, GRIDS * P_SIZE), jnp.float32)]
    if last:
        out_shape.append(jax.ShapeDtypeStruct((16, P_SIZE), jnp.float32))
    args = list(bufs) + ([] if first else [acc])
    flops = (2 if first else 4) * slots * len(grids) * P_SIZE * P_SIZE * B
    out = pl.pallas_call(
        lambda *refs: grid_kernel(n, first, last, grids, *refs),
        out_shape=out_shape,
        in_specs=[VMEM] * len(args),
        out_specs=[VMEM] * len(out_shape),
        input_output_aliases={} if first else {n: 0},
        compiler_params=PARAMS,
        cost_estimate=pl.CostEstimate(flops=flops, bytes_accessed=slots * PIECE_ROWS * LANES, transcendentals=0),
        name="grid",
    )(*args)
    return tuple(out) if last else out[0]


def two_parts(value):
    high = value.astype(jnp.bfloat16)
    return high, (value - high.astype(jnp.float32)).astype(jnp.bfloat16)


def image_kernel(acc_ref, mine_ref, other_ref, row_ref, col_ref, out_ref):
    s1 = mine_ref[0:1, :] + other_ref[0:1, :]
    s2 = mine_ref[8:9, :] + other_ref[8:9, :]
    factor = 2.5 * s1 / s2
    width = out_ref.shape[3]
    half = 2 * width
    done = []
    for t in range(NT_C):
        tiles = [[acc_ref.at[4 * t + 2 * pr + pc] for pr in range(2)] for pc in range(2)]
        weights = [[1.0 / (1.0 + factor * tile[:, :P_SIZE]) for tile in pair] for pair in tiles]
        for pol in range(POLS):
            cells = []
            for e in (1 + 2 * pol, 2 + 2 * pol):
                for pc in range(2):
                    strip = [
                        tiles[pc][pr][:, e * P_SIZE : (e + 1) * P_SIZE] * weights[pc][pr] for pr in range(2)
                    ]
                    cells.append(jnp.concatenate(strip, axis=1))
            high, low = two_parts(jnp.concatenate(cells, axis=0))
            both = jnp.dot(row_ref[...], high, preferred_element_type=jnp.float32)
            rest = jnp.dot(row_ref[:half], low, preferred_element_type=jnp.float32)
            done.append(both[:half] + both[half:] + rest)
    high, low = two_parts(jnp.concatenate(done, axis=0))
    both = jnp.dot(high, col_ref[...], preferred_element_type=jnp.float32)
    rest = jnp.dot(low, col_ref[:, : 2 * G], preferred_element_type=jnp.float32)
    done = both[:, : 2 * G] + both[:, 2 * G :] + rest
    for t in range(NT_C):
        for pol in range(POLS):
            at = (t * POLS + pol) * half
            real, imag = done[at : at + width], done[at + width : at + half]
            out_ref[pol, 0, t] = real[:, :G] + imag[:, G:]
            out_ref[pol, 1, t] = imag[:, :G] - real[:, G:]


def make_image(acc, mine, other, row_table, col_table, width):
    return pl.pallas_call(
        image_kernel,
        out_shape=jax.ShapeDtypeStruct((POLS, 2, NT_C, width, G), jnp.float32),
        in_specs=[VMEM] * 5,
        out_specs=VMEM,
        compiler_params=PARAMS,
        name="image",
    )(acc, mine, other, row_table, col_table)


def dft_tables():
    index = np.arange(G)
    phase = (index[:, None] * index[None, :] % G) * (2.0 * math.pi / G)
    return np.cos(phase).astype(np.float32), np.sin(phase).astype(np.float32)


def np_parts(table, axis):
    high = table.astype(ml_dtypes.bfloat16)
    low = (table - high.astype(np.float32)).astype(ml_dtypes.bfloat16)
    return np.concatenate([high, low], axis=axis)


def image_tables(n_tm):
    cosine, sine = dft_tables()
    rows = []
    for cos_part, sin_part in zip(np.split(cosine, n_tm, axis=1), np.split(sine, n_tm, axis=1)):
        rows.append(np_parts(np.block([[cos_part, -sin_part], [sin_part, cos_part]]).T, 0))
    return np.stack(rows), np_parts(np.concatenate([cosine, sine], axis=1) / G, 1)


def by_gather(packed, n_tm, n_tile):
    order = list(range(0, n_tm, 2)) + list(range(1, n_tm, 2))[::-1]
    ways = [[], []]
    for i in range(n_tm):
        for tile in range(n_tile):
            here, there = (n_tile * order[k] + tile for k in (i, (i + 1) % n_tm))
            ways[tile % 2].append((here, there))
            ways[1 - tile % 2].append((there, here))

    def both_ways(pair):
        return [lax.ppermute(a, ("tm", "tile"), way) for a, way in zip(pair, ways)]

    leading = both_ways(packed)
    trailing = both_ways(packed[::-1])
    acc = add_blocks(None, packed[:1])
    for step in range(2, n_tm // 2 + 1):
        following = both_ways(leading)
        acc = add_blocks(acc, leading + (list(packed[1:]) if step == 2 else []))
        acc, *trailing = lax.optimization_barrier((acc, *trailing))
        leading = following
        following = both_ways(trailing) if step < n_tm // 2 else None
        acc = add_blocks(acc, trailing)
        trailing = following
    acc, sums = add_blocks(acc, leading, last=True, grids=range(1))
    return add_blocks(acc, leading, grids=range(1, GRIDS)), sums


def rest_by_rows(acc, cosine, sine):
    grid = acc.reshape(NT_C, 2, 2, P_SIZE, GRIDS, P_SIZE)
    flat = jnp.transpose(grid, (4, 0, 1, 5, 2, 3)).reshape(GRIDS, NT_C * G, G)
    owned = lax.psum_scatter(flat, "tm", scatter_dimension=1, tiled=True)
    dens = owned[0]
    totals = lax.psum((jnp.sum(dens), jnp.sum(dens * dens)), ("tm", "tile"))
    factor = 2.5 * totals[0] / totals[1]
    weighted = owned[1:] / (1.0 + factor * dens[None])
    weighted = weighted.reshape(POLS, 2, dens.shape[0], G)
    real, imag = weighted[:, 0], weighted[:, 1]

    def rows(a, b):
        return jnp.einsum("prj,jn->prn", a, b, precision=HIGH)

    done = jnp.stack([rows(real, cosine) + rows(imag, sine), rows(imag, cosine) - rows(real, sine)], axis=1)
    width = G // lax.axis_size("tm")
    every_row = lax.all_gather(done, "tm", axis=2, tiled=True)
    columns = lax.dynamic_slice_in_dim(every_row, lax.axis_index("tm") * width, width, 3)
    columns = columns.reshape(POLS, 2, NT_C, G, width)
    real, imag = columns[:, 0], columns[:, 1]

    def cols(a, b):
        return jnp.einsum("mi,ptic->ptcm", a, b, precision=HIGH)

    out = jnp.stack([cols(cosine, real) + cols(sine, imag), cols(cosine, imag) - cols(sine, real)], axis=1)
    return out / G


def body(vis_data, vis_weight, kernel_taps, offsets, block_patch, block_count):
    slots = vis_weight.shape[1]
    n_tm = lax.axis_size("tm")
    pieces = (slots // 2, slots - slots // 2)
    packed = pack(pieces, vis_data[0], vis_weight[0], kernel_taps[0], offsets[0], block_patch, block_count)
    if n_tm > 8:
        cosine, sine = dft_tables()
        return rest_by_rows(add_blocks(None, packed), jnp.asarray(cosine), jnp.asarray(sine))
    n_tile = lax.axis_size("tile")
    acc, mine = by_gather(packed, n_tm, n_tile)
    other = lax.ppermute(mine, "tile", [(i, n_tile - 1 - i) for i in range(n_tile)])
    row_tables, col_table = image_tables(n_tm)
    row_table = lax.dynamic_index_in_dim(jnp.asarray(row_tables), lax.axis_index("tm"), 0, keepdims=False)
    return make_image(acc, mine, other, row_table, jnp.asarray(col_table), G // n_tm)


def solution(mesh):
    return jax.shard_map(
        body,
        mesh=mesh,
        in_specs=(
            P(("grp", "tile"), "tm", None, None),
            P(("grp", "tile"), "tm", None),
            P(("grp", "tile"), "tm", None, None, None),
            P(("grp", "tile"), "tm", None, None),
            P(("grp", "tile"), "tm"),
            P(("grp", "tile"), "tm"),
        ),
        out_specs=P(None, None, ("grp", "tile"), "tm", None),
        check_vma=False,
    )
```

```python
import math

import jax
import jax.numpy as jnp
import ml_dtypes
import numpy as np
from jax import lax
from jax.experimental import pallas as pl
from jax.experimental.pallas import tpu as pltpu
from jax.sharding import PartitionSpec as P

G = 256
P_SIZE = 128
K = 8
B = 256
POLS = 2
NT_C = 2
PATCHES = 4 * NT_C
GRIDS = 1 + 2 * POLS
LANES = 128
HALVES = B // LANES
AUX = GRIDS + 2
TAP_ROWS = 2 * HALVES * K
ID_START = TAP_ROWS + AUX * HALVES
PIECE_ROWS = ID_START + 1
HIGH = lax.Precision.HIGHEST
VMEM = pl.BlockSpec(memory_space=pltpu.VMEM)
PARAMS = pltpu.CompilerParams(vmem_limit_bytes=20 * 1024 * 1024)


def half_lanes(half):
    return slice(half * LANES, (half + 1) * LANES)


def pack_kernel(pieces, vis_hbm, weight_hbm, taps_hbm, offs_hbm, patch_hbm, count_ref, *refs):
    outs, scratch = refs[: len(pieces)], refs[len(pieces) :]
    vis_ref, weight_ref, taps_ref, offs_ref, patch_ref, sems = scratch
    pairs = (
        (offs_hbm, offs_ref),
        (taps_hbm, taps_ref),
        (weight_hbm, weight_ref),
        (vis_hbm, vis_ref),
        (patch_hbm, patch_ref),
    )
    copies = [pltpu.make_async_copy(a, b, sems.at[i]) for i, (a, b) in enumerate(pairs)]
    for copy in copies:
        copy.start()
    bases = [sum(pieces[:i]) for i in range(len(pieces))]
    copies[0].wait()
    copies[1].wait()
    for out_ref, n, base in zip(outs, pieces, bases):
        for j in range(n):
            for side in range(2):
                off = offs_ref[base + j, side : side + 1, :]
                taps = taps_ref[base + j, side]
                for bit in range(3):
                    moved = pltpu.roll(taps, 1 << bit, 0)
                    turn = jnp.broadcast_to((off >> bit) & 1, taps.shape) == 1
                    taps = jnp.where(turn, moved, taps)
                for half in range(HALVES):
                    at = j * TAP_ROWS + (side * HALVES + half) * K
                    out_ref[at : at + K, :] = taps[:, half_lanes(half)]
    copies[2].wait()
    copies[3].wait()
    copies[4].wait()
    for out_ref, n, base in zip(outs, pieces, bases):
        for half in range(HALVES):
            lanes = half_lanes(half)
            weight = weight_ref[base : base + n, lanes]
            kinds = [weight] + [weight * vis_ref[base : base + n, m, lanes] for m in range(2 * POLS)]
            kinds += [offs_ref[base : base + n, side, lanes].astype(jnp.float32) for side in range(2)]
            for kind, rows in enumerate(kinds):
                at = n * (TAP_ROWS + kind * HALVES + half)
                out_ref[at : at + n, :] = rows
        for j in range(n):
            patch = jnp.where(base + j < count_ref[0, 0], patch_ref[0, base + j], -1)
            row = jnp.full((1, LANES), patch, jnp.int32).astype(jnp.float32)
            out_ref[n * ID_START + j : n * ID_START + j + 1, :] = row


def pack(pieces, vis, weight, taps, offs, patches, count):
    arrays = (vis, weight, taps, offs, patches)
    spaces = [pltpu.VMEM] * 4 + [pltpu.SMEM]
    hbm, smem = pl.BlockSpec(memory_space=pltpu.HBM), pl.BlockSpec(memory_space=pltpu.SMEM)
    return pl.pallas_call(
        lambda *refs: pack_kernel(pieces, *refs),
        out_shape=[jax.ShapeDtypeStruct((n * PIECE_ROWS, LANES), jnp.float32) for n in pieces],
        in_specs=[hbm] * 5 + [smem],
        out_specs=[VMEM] * len(pieces),
        scratch_shapes=[space(a.shape, a.dtype) for space, a in zip(spaces, arrays)] + [pltpu.SemaphoreType.DMA((5,))],
        compiler_params=PARAMS,
        name="pack",
    )(*[pltpu.with_memory_space_constraint(a, pltpu.HBM) for a in arrays], count)


def spread(off):
    row = lax.broadcasted_iota(jnp.int32, (16, B), 0)
    gap = off.astype(jnp.int32) - row
    step = (gap + 15) >> 4
    inside = (step << 4) - gap < K
    return jnp.where(inside, step, -1).astype(jnp.float32).astype(jnp.bfloat16)


def slot_taps(buf_ref, j, side):
    starts = [j * TAP_ROWS + (side * HALVES + half) * K for half in range(HALVES)]
    rows = jnp.concatenate([buf_ref[at : at + K, :] for at in starts], axis=1)
    return jnp.concatenate([rows, rows], axis=0)


def slot_row(buf_ref, n, j, kind):
    starts = [n * (TAP_ROWS + kind * HALVES + half) + j for half in range(HALVES)]
    return jnp.concatenate([buf_ref[at : at + 1, :] for at in starts], axis=1)


def slot_patch(buf_ref, n, j):
    return buf_ref[n * ID_START + j : n * ID_START + j + 1, 0:1][0, 0].astype(jnp.int32)


def block_factors(buf_ref, n, j, live, grids):
    rows_u = slot_taps(buf_ref, j, 0)
    rows_v = slot_taps(buf_ref, j, 1)
    step_u = spread(slot_row(buf_ref, n, j, GRIDS))
    step_v = spread(slot_row(buf_ref, n, j, GRIDS + 1))
    if live is not None:
        rows_v = jnp.where(live, rows_v, 0.0)
    rows_v = rows_v.astype(jnp.bfloat16)
    zero = jnp.zeros((16, B), jnp.bfloat16)
    steps = P_SIZE // 16
    right = jnp.concatenate([jnp.where(step_v == s, rows_v, zero) for s in range(steps)], axis=0)
    hits = [step_u == s for s in range(steps)]
    left = []
    for e in grids:
        product = (rows_u * slot_row(buf_ref, n, j, e)).astype(jnp.bfloat16)
        left += [jnp.where(hit, product, zero) for hit in hits]
    return jnp.concatenate(left, axis=0), right


def add_some(buf_ref, acc_ref, n, slots, grids):
    lanes = slice(grids[0] * P_SIZE, (grids[-1] + 1) * P_SIZE)
    waiting = None
    for i, j in enumerate(slots):
        where_at = slot_patch(buf_ref, n, j)
        left, right = block_factors(buf_ref, n, j, where_at >= 0 if i else None, grids)
        patch = lax.dot_general(
            right, left, (((1,), (1,)), ((), ())), preferred_element_type=jnp.float32
        )
        if waiting is not None:
            acc_ref[waiting[0], :, lanes] += waiting[1]
        waiting = jnp.maximum(where_at, 0), patch
    acc_ref[waiting[0], :, lanes] += waiting[1]


def grid_kernel(n_bufs, first, last, grids, *refs):
    acc_ref = refs[n_bufs] if first else refs[n_bufs + 1]
    if first:
        acc_ref[...] = jnp.zeros_like(acc_ref)
    for buf_ref in refs[:n_bufs]:
        n = buf_ref.shape[0] // PIECE_ROWS
        for low in range(0, n, 4):

            @pl.when(slot_patch(buf_ref, n, low) >= 0)
            def _(buf_ref=buf_ref, n=n, slots=range(low, min(low + 4, n))):
                add_some(buf_ref, acc_ref, n, slots, grids)

    if last:
        sums_ref = refs[-1]
        dens = acc_ref[:, :, :P_SIZE]
        for i, value in enumerate((dens, dens * dens)):
            part = jnp.sum(value.reshape(-1, 8, P_SIZE), axis=0)
            part = jnp.sum(jnp.sum(part, axis=0, keepdims=True), axis=1, keepdims=True)
            sums_ref[8 * i : 8 * i + 8, :] = jnp.broadcast_to(part, (8, P_SIZE))


def add_blocks(acc, bufs, last=False, grids=range(GRIDS)):
    first = acc is None
    n = len(bufs)
    slots = sum(buf.shape[0] for buf in bufs) // PIECE_ROWS
    out_shape = [jax.ShapeDtypeStruct((PATCHES, P_SIZE, GRIDS * P_SIZE), jnp.float32)]
    if last:
        out_shape.append(jax.ShapeDtypeStruct((16, P_SIZE), jnp.float32))
    args = list(bufs) + ([] if first else [acc])
    flops = (2 if first else 4) * slots * len(grids) * P_SIZE * P_SIZE * B
    out = pl.pallas_call(
        lambda *refs: grid_kernel(n, first, last, grids, *refs),
        out_shape=out_shape,
        in_specs=[VMEM] * len(args),
        out_specs=[VMEM] * len(out_shape),
        input_output_aliases={} if first else {n: 0},
        compiler_params=PARAMS,
        cost_estimate=pl.CostEstimate(flops=flops, bytes_accessed=slots * PIECE_ROWS * LANES, transcendentals=0),
        name="grid",
    )(*args)
    return tuple(out) if last else out[0]


def two_parts(value):
    high = value.astype(jnp.bfloat16)
    return high, (value - high.astype(jnp.float32)).astype(jnp.bfloat16)


def image_kernel(acc_ref, mine_ref, other_ref, row_ref, col_ref, out_ref):
    s1 = mine_ref[0:1, :] + other_ref[0:1, :]
    s2 = mine_ref[8:9, :] + other_ref[8:9, :]
    factor = 2.5 * s1 / s2
    width = out_ref.shape[3]
    half = 2 * width
    done = []
    for t in range(NT_C):
        tiles = [[acc_ref.at[4 * t + 2 * pr + pc] for pr in range(2)] for pc in range(2)]
        weights = [[1.0 / (1.0 + factor * tile[:, :P_SIZE]) for tile in pair] for pair in tiles]
        for pol in range(POLS):
            cells = []
            for e in (1 + 2 * pol, 2 + 2 * pol):
                for pc in range(2):
                    strip = [
                        tiles[pc][pr][:, e * P_SIZE : (e + 1) * P_SIZE] * weights[pc][pr] for pr in range(2)
                    ]
                    cells.append(jnp.concatenate(strip, axis=1))
            high, low = two_parts(jnp.concatenate(cells, axis=0))
            both = jnp.dot(row_ref[...], high, preferred_element_type=jnp.float32)
            rest = jnp.dot(row_ref[:half], low, preferred_element_type=jnp.float32)
            done.append(both[:half] + both[half:] + rest)
    high, low = two_parts(jnp.concatenate(done, axis=0))
    both = jnp.dot(high, col_ref[...], preferred_element_type=jnp.float32)
    rest = jnp.dot(low, col_ref[:, : 2 * G], preferred_element_type=jnp.float32)
    done = both[:, : 2 * G] + both[:, 2 * G :] + rest
    for t in range(NT_C):
        for pol in range(POLS):
            at = (t * POLS + pol) * half
            real, imag = done[at : at + width], done[at + width : at + half]
            out_ref[pol, 0, t] = real[:, :G] + imag[:, G:]
            out_ref[pol, 1, t] = imag[:, :G] - real[:, G:]


def make_image(acc, mine, other, row_table, col_table, width):
    return pl.pallas_call(
        image_kernel,
        out_shape=jax.ShapeDtypeStruct((POLS, 2, NT_C, width, G), jnp.float32),
        in_specs=[VMEM] * 5,
        out_specs=VMEM,
        compiler_params=PARAMS,
        name="image",
    )(acc, mine, other, row_table, col_table)


def dft_tables():
    index = np.arange(G)
    phase = (index[:, None] * index[None, :] % G) * (2.0 * math.pi / G)
    return np.cos(phase).astype(np.float32), np.sin(phase).astype(np.float32)


def np_parts(table, axis):
    high = table.astype(ml_dtypes.bfloat16)
    low = (table - high.astype(np.float32)).astype(ml_dtypes.bfloat16)
    return np.concatenate([high, low], axis=axis)


def image_tables(n_tm):
    cosine, sine = dft_tables()
    rows = []
    for cos_part, sin_part in zip(np.split(cosine, n_tm, axis=1), np.split(sine, n_tm, axis=1)):
        rows.append(np_parts(np.block([[cos_part, -sin_part], [sin_part, cos_part]]).T, 0))
    return np.stack(rows), np_parts(np.concatenate([cosine, sine], axis=1) / G, 1)


def by_gather(packed, n_tm, n_tile):
    order = list(range(0, n_tm, 2)) + list(range(1, n_tm, 2))[::-1]
    ways = [[], []]
    for i in range(n_tm):
        for tile in range(n_tile):
            here, there = (n_tile * order[k] + tile for k in (i, (i + 1) % n_tm))
            ways[tile % 2].append((here, there))
            ways[1 - tile % 2].append((there, here))

    def both_ways(pair):
        return [lax.ppermute(a, ("tm", "tile"), way) for a, way in zip(pair, ways)]

    leading = both_ways(packed)
    trailing = both_ways(packed[::-1])
    acc = add_blocks(None, packed[:1])
    for step in range(2, n_tm // 2 + 1):
        following = both_ways(leading)
        acc = add_blocks(acc, leading + (list(packed[1:]) if step == 2 else []))
        acc, *trailing = lax.optimization_barrier((acc, *trailing))
        leading = following
        following = both_ways(trailing) if step < n_tm // 2 else None
        acc = add_blocks(acc, trailing)
        trailing = following
    acc, sums = add_blocks(acc, leading, last=True, grids=range(1))
    return add_blocks(acc, leading, grids=range(1, GRIDS)), sums


def rest_by_rows(acc, cosine, sine):
    grid = acc.reshape(NT_C, 2, 2, P_SIZE, GRIDS, P_SIZE)
    flat = jnp.transpose(grid, (4, 0, 1, 5, 2, 3)).reshape(GRIDS, NT_C * G, G)
    owned = lax.psum_scatter(flat, "tm", scatter_dimension=1, tiled=True)
    dens = owned[0]
    totals = lax.psum((jnp.sum(dens), jnp.sum(dens * dens)), ("tm", "tile"))
    factor = 2.5 * totals[0] / totals[1]
    weighted = owned[1:] / (1.0 + factor * dens[None])
    weighted = weighted.reshape(POLS, 2, dens.shape[0], G)
    real, imag = weighted[:, 0], weighted[:, 1]

    def rows(a, b):
        return jnp.einsum("prj,jn->prn", a, b, precision=HIGH)

    done = jnp.stack([rows(real, cosine) + rows(imag, sine), rows(imag, cosine) - rows(real, sine)], axis=1)
    width = G // lax.axis_size("tm")
    every_row = lax.all_gather(done, "tm", axis=2, tiled=True)
    columns = lax.dynamic_slice_in_dim(every_row, lax.axis_index("tm") * width, width, 3)
    columns = columns.reshape(POLS, 2, NT_C, G, width)
    real, imag = columns[:, 0], columns[:, 1]

    def cols(a, b):
        return jnp.einsum("mi,ptic->ptcm", a, b, precision=HIGH)

    out = jnp.stack([cols(cosine, real) + cols(sine, imag), cols(cosine, imag) - cols(sine, real)], axis=1)
    return out / G


def body(vis_data, vis_weight, kernel_taps, offsets, block_patch, block_count):
    slots = vis_weight.shape[1]
    n_tm = lax.axis_size("tm")
    pieces = (slots // 2, slots - slots // 2)
    packed = pack(pieces, vis_data[0], vis_weight[0], kernel_taps[0], offsets[0], block_patch, block_count)
    if n_tm > 8:
        cosine, sine = dft_tables()
        return rest_by_rows(add_blocks(None, packed), jnp.asarray(cosine), jnp.asarray(sine))
    n_tile = lax.axis_size("tile")
    acc, mine = by_gather(packed, n_tm, n_tile)
    other = lax.ppermute(mine, "tile", [(i, n_tile - 1 - i) for i in range(n_tile)])
    row_tables, col_table = image_tables(n_tm)
    row_table = lax.dynamic_index_in_dim(jnp.asarray(row_tables), lax.axis_index("tm"), 0, keepdims=False)
    return make_image(acc, mine, other, row_table, jnp.asarray(col_table), G // n_tm)


def solution(mesh):
    return jax.shard_map(
        body,
        mesh=mesh,
        in_specs=(
            P(("grp", "tile"), "tm", None, None),
            P(("grp", "tile"), "tm", None),
            P(("grp", "tile"), "tm", None, None, None),
            P(("grp", "tile"), "tm", None, None),
            P(("grp", "tile"), "tm"),
            P(("grp", "tile"), "tm"),
        ),
        out_specs=P(None, None, ("grp", "tile"), "tm", None),
        check_vma=False,
    )
```
